512 devices in a mesh: gx: 32 (over y, x), gy: 16 (over z, core).
Axes of the slice: x: 4, y: 8, z: 8, core: 2. Of those that a mesh axis runs over, the one named last changes fastest.
Arguments:
- basis: float32 [22, 6, 20, 65536], P(None, None, None, ('gx', 'gy'))
- geometry: float32 [9, 65536], P(None, ('gx', 'gy')), may hold values from -0.3 to 0.3
- face_normals: float32 [3, 4, 65536], P(None, None, ('gx', 'gy')), may hold values from -3 to 3
- face_scale: float32 [4, 65536], P(None, ('gx', 'gy')), may hold values from 0.02 to 0.2
- material: float32 [3, 65536], P(None, ('gx', 'gy')), may hold values from 0.25 to 4
- send_list: int32 [96, 48, 64], P('gx', 'gy'), may hold values from 0 to 511, as said below
- neighbour_source: int32 [4, 65536], P(None, ('gx', 'gy')), may hold values from 0 to 1087, as said below
- node_rotation: int32 [4, 65536], P(None, ('gx', 'gy')), may hold values from 0 to 2
- boundary_flag: int32 [4, 65536], P(None, ('gx', 'gy')), may hold values from 0 to 1
Outputs:
- new_basis: float32 [2, 6, 20, 65536], P(None, None, None, ('gx', 'gy'))
- hessenberg: float32 [2, 24], replicated
The draws below stay inside these ranges and needn't reach their ends.
Inputs may be any that keep to these rules, and one draw needn't show every extreme that they name: `send_list`: block (a, b) of device (i, j) lists local face ids meant for device (i + a - 1, j + b - 1); only the slots that device reads carry meaning; block (1, 1) is never read. `basis`: the stored vectors need not be orthonormal or of unit norm under <u, w>; the steps hold as written for any stored vectors. `neighbour_source`: remote sources always name an existing device. Faces pair up across devices: a device reads from one neighbour slots 0 to c - 1 of its block, with c at most 64, and c reaches 64 for some pairs in every draw. Faces with boundary_flag 1 ignore their source.
All inputs are finite; a program needn't handle non-finite values.
Results may differ from the reference program's by a relative error of at most 0.0003.
Values sent between devices are 32-bit elements; how exact they have to be, the bound alone decides.
A program may use at most 64 MiB of HBM per device.

```python
import math
import jax
import jax.numpy as jnp
import numpy as np
from jax import lax

COMPONENTS = 6
NODES = 20
KPREV = 22
E_DEV = 128
SLOT = 64
ELEMENTS = 65536
N_GX = 32
N_GY = 16


def connection_tables(key):
    key = jax.random.fold_in(key, 41)
    rows = N_GX
    cols = N_GY
    devices = rows * cols
    faces = 4 * E_DEV
    width = SLOT
    keys = jax.random.split(key, 5)
    grid_a = jnp.arange(rows)[:, None]
    grid_b = jnp.arange(cols)[None, :]
    across = jax.random.randint(keys[0], (rows, cols), width // 2, width + 1)
    across = jnp.where(grid_a < rows - 1, across, 0).at[0, 0].set(width).astype(jnp.int32)
    sideways = jax.random.randint(keys[1], (rows, cols), width // 2, width + 1)
    sideways = jnp.where(grid_b < cols - 1, sideways, 0).astype(jnp.int32)
    rising = jax.random.randint(keys[2], (rows, cols), 1, width // 2 + 1)
    rising = jnp.where((grid_a < rows - 1) & (grid_b < cols - 1), rising, 0).at[0, 0].set(width).astype(jnp.int32)
    falling = jax.random.randint(keys[3], (rows, cols), 1, width // 2 + 1)
    falling = jnp.where((grid_a < rows - 1) & (grid_b > 0), falling, 0).astype(jnp.int32)
    across_pad = jnp.pad(across, 1)
    sideways_pad = jnp.pad(sideways, 1)
    rising_pad = jnp.pad(rising, 1)
    falling_pad = jnp.pad(falling, 1)
    counts = jnp.stack([rising_pad[0:rows, 0:cols], across_pad[0:rows, 1:cols + 1], falling_pad[0:rows, 2:cols + 2], sideways_pad[1:rows + 1, 0:cols], jnp.zeros((rows, cols), jnp.int32), sideways, falling, across, rising], axis=-1).reshape(devices, 9).astype(jnp.int32)

    def one_device(device_key, count_row):
        order_key, bit_key = jax.random.split(device_key)
        order = jax.random.permutation(order_key, faces).astype(jnp.int32)
        ends = jnp.cumsum(count_row).astype(jnp.int32)
        starts = ends - count_row
        total = ends[8]
        direction = jnp.arange(9, dtype=jnp.int32)[:, None]
        place = jnp.arange(width, dtype=jnp.int32)[None, :]
        used = place < count_row[:, None]
        spare = order[(direction * width + place) % faces]
        spare = jnp.where(direction == 4, place * (faces - 1) // (width - 1), spare)
        outgoing = jnp.where(used, order[jnp.clip(starts[:, None] + place, 0, faces - 1)], spare).astype(jnp.int32)
        position = jnp.arange(faces, dtype=jnp.int32)
        which = jnp.minimum(jnp.sum((ends[None, :] <= position[:, None]).astype(jnp.int32), axis=1), 8)
        remote_source = faces + which * width + position - starts[which]
        rest = position - total
        partner = jnp.bitwise_xor(rest, 1)
        paired = (partner < faces - total) & (rest >= 0)
        inner_source = order[jnp.clip(total + partner, 0, faces - 1)]
        bits = jax.random.randint(bit_key, (faces,), 0, 4)
        wall = (rest >= 0) & ((bits[jnp.clip(rest // 2, 0, faces - 1)] == 0) | ~paired)
        source = jnp.where(rest < 0, remote_source, jnp.where(wall, order, inner_source)).astype(jnp.int32)
        by_face = jnp.zeros((faces,), jnp.int32).at[order].set(source)
        wall_face = jnp.zeros((faces,), jnp.int32).at[order].set(wall.astype(jnp.int32))
        return (outgoing, by_face, wall_face)
    outgoing, sources, walls = jax.vmap(one_device)(jax.random.split(keys[4], devices), counts)
    send = outgoing.reshape(rows, cols, 3, 3, width).transpose(0, 2, 1, 3, 4).reshape(3 * rows, 3 * cols, width)
    source_table = sources.reshape(devices, 4, E_DEV).transpose(1, 0, 2).reshape(4, devices * E_DEV)
    wall_table = walls.reshape(devices, 4, E_DEV).transpose(1, 0, 2).reshape(4, devices * E_DEV)
    return (send, source_table, wall_table)


def draw_send_list(key, part):
    return connection_tables(key)[0]


def draw_neighbour_source(key, part):
    return connection_tables(key)[1]


def draw_boundary_flag(key, part):
    return connection_tables(key)[2]


def draw_basis(key, part):
    key = jax.random.fold_in(key, 11)
    common_key, noise_key, weight_key = jax.random.split(key, 3)
    shape = (KPREV, COMPONENTS, NODES, ELEMENTS)
    ramp = 1.0 + 2.0 * jnp.arange(ELEMENTS, dtype=jnp.float32) / float(ELEMENTS - 1)
    common = jax.random.normal(common_key, (COMPONENTS, NODES, ELEMENTS), jnp.float32)
    noise = jax.random.normal(noise_key, shape, jnp.float32)
    weight = jax.random.uniform(weight_key, (KPREV, 1, 1, 1), jnp.float32, 0.3, 1.0)
    mixed = (weight * common[None] + noise) * ramp / jnp.sqrt(1.0 + weight * weight)
    return mixed.astype(jnp.float32)


def plant(drawn, own_key, low, largest):
    index_at = [jax.random.randint(jax.random.fold_in(own_key, axis), (), 0, length) for axis, length in enumerate(drawn.shape)]
    widest = drawn.shape.index(max(drawn.shape))
    neighbour = index_at[:widest] + [(index_at[widest] + 1) % drawn.shape[widest]] + index_at[widest + 1:]
    return drawn.at[tuple(index_at)].set(low).at[tuple(neighbour)].set(largest)


def steps_of(own_key, extent, cuts, low, largest):
    def one(dim, shards_of):
        steps = jax.random.uniform(jax.random.fold_in(jax.random.fold_in(own_key, 6), dim), (shards_of,), jnp.float32, low / len(cuts), largest / len(cuts))
        return jnp.repeat(jnp.exp(steps), extent[dim] // shards_of).reshape((-1,) + (1,) * (len(extent) - dim - 1))

    level = one(*cuts[0])
    for cut in cuts[1:]:
        level = level * one(*cut)
    return level


def gaussian(own_key, shape, scale, limit, cuts=(), held_as=jnp.bfloat16):
    values = scale * jax.random.normal(own_key, shape, jnp.float32)
    if cuts:
        values = values * steps_of(own_key, shape, cuts, -0.22, 0.18)
    return jnp.clip(values, -limit, limit).astype(held_as)


def setup_inputs(seed: int = 0) -> dict:
    streams_of = jax.random.split(jax.random.key(seed), 10)
    return {
        "basis": draw_basis(jax.random.fold_in(streams_of[9], 71), 0),
        "geometry": gaussian(streams_of[1], (9, ELEMENTS), 0.05, 0.3, ((1, 512),), jnp.float32),
        "face_normals": gaussian(streams_of[2], (3, 4, ELEMENTS), 0.577, 3.0, ((2, 512),), jnp.float32),
        "face_scale": jnp.clip(jnp.exp(math.log(0.2) - 2.3025851 * jax.random.uniform(streams_of[3], (4, ELEMENTS), jnp.float32) ** steps_of(streams_of[3], (4, ELEMENTS), ((1, 512),), -0.2, 0.2)), 0.02, 0.2),
        "material": jnp.clip(jnp.exp(math.log(4.0) - 2.7725887 * jax.random.uniform(streams_of[4], (3, ELEMENTS), jnp.float32) ** steps_of(streams_of[4], (3, ELEMENTS), ((1, 512),), -0.2, 0.2)), 0.25, 4.0),
        "send_list": draw_send_list(jax.random.fold_in(streams_of[9], 71), 0),
        "neighbour_source": draw_neighbour_source(jax.random.fold_in(streams_of[9], 71), 0),
        "node_rotation": plant(jax.random.randint(streams_of[7], (4, ELEMENTS), 0, 3), jax.random.fold_in(streams_of[7], 1), 0, 2).astype(jnp.int32),
        "boundary_flag": draw_boundary_flag(jax.random.fold_in(streams_of[9], 71), 0),
    }


highest = lax.Precision.HIGHEST

def invert(matrix):
    dimension = len(matrix)
    augmented = []
    for row_index in range(dimension):
        augmented.append([float(matrix[row_index][column]) for column in range(dimension)] + [1.0 if column == row_index else 0.0 for column in range(dimension)])
    for column in range(dimension):
        pivot_row = column
        for row_index in range(column + 1, dimension):
            if abs(augmented[row_index][column]) > abs(augmented[pivot_row][column]):
                pivot_row = row_index
        augmented[column], augmented[pivot_row] = (augmented[pivot_row], augmented[column])
        leading = augmented[column][column]
        augmented[column] = [value / leading for value in augmented[column]]
        for row_index in range(dimension):
            if row_index != column:
                factor = augmented[row_index][column]
                augmented[row_index] = [left - factor * right for left, right in zip(augmented[row_index], augmented[column])]
    return np.array([entries[dimension:] for entries in augmented])

def locate(face, first, second):
    if face == 0:
        return (first, second, 0)
    if face == 1:
        return (first, 0, second)
    if face == 2:
        return (3 - first - second, first, second)
    return (0, first, second)

def element_tables():
    nodes = [(i, j, k) for k in range(4) for j in range(4) for i in range(4) if i + j + k <= 3]
    points = np.array(nodes) / 3.0
    vander = np.zeros((20, 20))
    slopes = np.zeros((3, 20, 20))
    for row in range(20):
        for column in range(20):
            powers = np.array(nodes[column])
            vander[row, column] = np.prod(points[row] ** powers)
            for axis in range(3):
                if powers[axis] > 0:
                    lowered = powers.copy()
                    lowered[axis] -= 1
                    slopes[axis, row, column] = powers[axis] * np.prod(points[row] ** lowered)
    inverse = invert(vander)
    derivs = np.stack([slopes[axis] @ inverse for axis in range(3)])
    moments = np.zeros((20, 20))
    for row in range(20):
        for column in range(20):
            left = nodes[row]
            right = nodes[column]
            sums = [left[0] + right[0], left[1] + right[1], left[2] + right[2]]
            moments[row, column] = math.factorial(sums[0]) * math.factorial(sums[1]) * math.factorial(sums[2]) / math.factorial(sum(sums) + 3)
    mass = inverse.T @ moments @ inverse
    lattice = [(first, second) for second in range(4) for first in range(4) if first + second <= 3]
    face_nodes = np.array([[nodes.index(locate(face, pair[0], pair[1])) for face in range(4)] for pair in lattice])
    plane = np.array([[(pair[0] / 3.0) ** expo[0] * (pair[1] / 3.0) ** expo[1] for expo in lattice] for pair in lattice])
    plane_inverse = invert(plane)
    plane_moments = np.zeros((10, 10))
    for row in range(10):
        for column in range(10):
            first = lattice[row][0] + lattice[column][0]
            second = lattice[row][1] + lattice[column][1]
            plane_moments[row, column] = math.factorial(first) * math.factorial(second) / math.factorial(first + second + 2)
    face_mass = plane_inverse.T @ plane_moments @ plane_inverse
    edges = np.zeros((20, 40))
    for face in range(4):
        for row in range(10):
            for column in range(10):
                edges[face_nodes[row, face], column * 4 + face] += face_mass[row, column]
    lift = invert(mass) @ edges
    turned = np.array([lattice.index((pair[1], 3 - pair[0] - pair[1])) for pair in lattice])
    rotations = np.stack([np.arange(10), turned, turned[turned]])
    return (derivs, lift, face_nodes, rotations)

def curl_pair(field, geometry, derivs):
    along = jnp.einsum('qnm,cme->qcne', derivs, field, precision=highest)
    grads = [along[0] * geometry[axis] + along[1] * geometry[3 + axis] + along[2] * geometry[6 + axis] for axis in range(3)]
    curl_e = jnp.stack([grads[1][2] - grads[2][1], grads[2][0] - grads[0][2], grads[0][1] - grads[1][0]])
    curl_h = jnp.stack([grads[1][5] - grads[2][4], grads[2][3] - grads[0][5], grads[0][4] - grads[1][3]])
    return (curl_e, curl_h)

def turn_nodes(other, turns, rotations):
    first = other[:, rotations[1], :]
    second = other[:, rotations[2], :]
    return jnp.where(turns == 0, other, jnp.where(turns == 1, first, second))

def flux_terms(inside, other, flags, normals, scale):
    wall = flags == 1
    other_e = jnp.where(wall, -inside[:3], other[:3])
    other_h = jnp.where(wall, inside[3:], other[3:])
    jump_e = other_e - inside[:3]
    jump_h = other_h - inside[3:]
    normal_x = normals[0]
    normal_y = normals[1]
    normal_z = normals[2]
    along_e = normal_x * jump_e[0] + normal_y * jump_e[1] + normal_z * jump_e[2]
    along_h = normal_x * jump_h[0] + normal_y * jump_h[1] + normal_z * jump_h[2]
    flux = jnp.stack([normal_y * jump_h[2] - normal_z * jump_h[1] + jump_e[0] - along_e * normal_x, normal_z * jump_h[0] - normal_x * jump_h[2] + jump_e[1] - along_e * normal_y, normal_x * jump_h[1] - normal_y * jump_h[0] + jump_e[2] - along_e * normal_z, -normal_y * jump_e[2] + normal_z * jump_e[1] + jump_h[0] - along_h * normal_x, -normal_z * jump_e[0] + normal_x * jump_e[2] + jump_h[1] - along_h * normal_y, -normal_x * jump_e[1] + normal_y * jump_e[0] + jump_h[2] - along_h * normal_z])
    return flux * (0.5 * scale)

def assemble(field, curl_e, curl_h, flux, lift, material):
    count = field.shape[2]
    lifted = jnp.einsum('nk,cke->cne', lift, flux.reshape(6, 40, count), precision=highest)
    electric = material[0] * (curl_h + lifted[:3]) - material[2] * field[:3]
    magnetic = material[1] * (lifted[3:] - curl_e)
    return jnp.concatenate([electric, magnetic], axis=0)

def reference(basis, geometry, face_normals, face_scale, material, send_list, neighbour_source, node_rotation, boundary_flag):
    derivs_np, lift_np, face_nodes, rotations = element_tables()
    derivs = jnp.asarray(derivs_np, dtype=jnp.float32)
    lift = jnp.asarray(lift_np, dtype=jnp.float32)
    faces_dev = 4 * E_DEV
    blocks = send_list.reshape(N_GX, 3, N_GY, 3, SLOT).transpose(0, 2, 1, 3, 4).reshape(N_GX * N_GY, 9, SLOT)
    element = jnp.broadcast_to(jnp.arange(ELEMENTS, dtype=jnp.int32)[None, :], (4, ELEMENTS))
    device = element // E_DEV
    remote = neighbour_source >= faces_dev
    offset = jnp.maximum(neighbour_source - faces_dev, 0)
    direction = offset // SLOT
    place = offset % SLOT
    peer_gx = jnp.clip(device // N_GY + direction // 3 - 1, 0, N_GX - 1)
    peer_gy = jnp.clip(device % N_GY + direction % 3 - 1, 0, N_GY - 1)
    peer = (peer_gx * N_GY + peer_gy).astype(jnp.int32)
    remote_face = blocks[peer, 8 - direction, place]
    face_id = jnp.where(remote, remote_face, neighbour_source).astype(jnp.int32)
    owner = jnp.where(remote, peer, device).astype(jnp.int32)
    global_source = (face_id // E_DEV * ELEMENTS + owner * E_DEV + face_id % E_DEV).reshape(-1).astype(jnp.int32)
    normals = face_normals.reshape(3, 4 * ELEMENTS)
    scale = face_scale.reshape(-1)
    flags = boundary_flag.reshape(-1)
    turns = node_rotation.reshape(-1)
    components = basis.shape[1]
    nodes = basis.shape[2]

    def operate(field):
        curl_e, curl_h = curl_pair(field, geometry, derivs)
        inside = field[:, face_nodes, :].reshape(6, 10, 4 * ELEMENTS)
        other = jnp.take(inside.reshape(60, 4 * ELEMENTS), global_source, axis=1).reshape(6, 10, 4 * ELEMENTS)
        other = turn_nodes(other, turns, rotations)
        flux = flux_terms(inside, other, flags, normals, scale)
        return assemble(field, curl_e, curl_h, flux, lift, material)
    stacked = basis.reshape(KPREV, -1)
    total = float(stacked.shape[1])
    fresh = jnp.zeros((2, stacked.shape[1]), jnp.float32)
    current = stacked[KPREV - 1]
    columns = []
    for turn in range(2):
        image = operate(current.reshape(components, nodes, ELEMENTS)).reshape(-1)
        first_v = jnp.dot(stacked, image, precision=highest) / total
        first_n = jnp.dot(fresh, image, precision=highest) / total
        image = image - jnp.dot(first_v, stacked, precision=highest) - jnp.dot(first_n, fresh, precision=highest)
        second_v = jnp.dot(stacked, image, precision=highest) / total
        second_n = jnp.dot(fresh, image, precision=highest) / total
        image = image - jnp.dot(second_v, stacked, precision=highest) - jnp.dot(second_n, fresh, precision=highest)
        square = jnp.sum(image * image) / total
        height = jnp.sqrt(square + 1e-06)
        current = image / height
        fresh = fresh.at[turn].set(current)
        column = jnp.concatenate([first_v + second_v, first_n + second_n]).at[KPREV + turn].set(height)
        columns.append(column)
    return (fresh.reshape(2, components, nodes, ELEMENTS), jnp.stack(columns))
```

```python
import functools
import math

import jax
import jax.numpy as jnp
import numpy as np
from jax import lax
from jax.experimental import pallas as pl
from jax.experimental.pallas import tpu as pltpu
from jax.sharding import PartitionSpec as P

MESH = pl.DeviceIdType.MESH
X_CHIPS = 4
OPERANDS = (0, 64, 144, 176)
DIRECTIONS = (0, 1, 2, 3, 5, 6, 7, 8)


def invert(matrix):
    dimension = len(matrix)
    augmented = []
    for row_index in range(dimension):
        augmented.append(
            [float(matrix[row_index][column]) for column in range(dimension)]
            + [1.0 if column == row_index else 0.0 for column in range(dimension)]
        )
    for column in range(dimension):
        pivot_row = column
        for row_index in range(column + 1, dimension):
            if abs(augmented[row_index][column]) > abs(augmented[pivot_row][column]):
                pivot_row = row_index
        augmented[column], augmented[pivot_row] = (augmented[pivot_row], augmented[column])
        leading = augmented[column][column]
        augmented[column] = [value / leading for value in augmented[column]]
        for row_index in range(dimension):
            if row_index != column:
                factor = augmented[row_index][column]
                augmented[row_index] = [
                    left - factor * right
                    for left, right in zip(augmented[row_index], augmented[column])
                ]
    return np.array([entries[dimension:] for entries in augmented])


def locate(face, first, second):
    if face == 0:
        return (first, second, 0)
    if face == 1:
        return (first, 0, second)
    if face == 2:
        return (3 - first - second, first, second)
    return (0, first, second)


def element_tables():
    nodes = [(i, j, k) for k in range(4) for j in range(4) for i in range(4) if i + j + k <= 3]
    points = np.array(nodes) / 3.0
    vander = np.zeros((20, 20))
    slopes = np.zeros((3, 20, 20))
    for row in range(20):
        for column in range(20):
            powers = np.array(nodes[column])
            vander[row, column] = np.prod(points[row] ** powers)
            for axis in range(3):
                if powers[axis] > 0:
                    lowered = powers.copy()
                    lowered[axis] -= 1
                    slopes[axis, row, column] = powers[axis] * np.prod(points[row] ** lowered)
    inverse = invert(vander)
    derivs = np.stack([slopes[axis] @ inverse for axis in range(3)])
    moments = np.zeros((20, 20))
    for row in range(20):
        for column in range(20):
            left = nodes[row]
            right = nodes[column]
            sums = [left[0] + right[0], left[1] + right[1], left[2] + right[2]]
            moments[row, column] = (
                math.factorial(sums[0])
                * math.factorial(sums[1])
                * math.factorial(sums[2])
                / math.factorial(sum(sums) + 3)
            )
    mass = inverse.T @ moments @ inverse
    lattice = [(first, second) for second in range(4) for first in range(4) if first + second <= 3]
    face_nodes = np.array(
        [[nodes.index(locate(face, pair[0], pair[1])) for face in range(4)] for pair in lattice]
    )
    plane = np.array(
        [
            [(pair[0] / 3.0) ** expo[0] * (pair[1] / 3.0) ** expo[1] for expo in lattice]
            for pair in lattice
        ]
    )
    plane_inverse = invert(plane)
    plane_moments = np.zeros((10, 10))
    for row in range(10):
        for column in range(10):
            first = lattice[row][0] + lattice[column][0]
            second = lattice[row][1] + lattice[column][1]
            plane_moments[row, column] = (
                math.factorial(first) * math.factorial(second) / math.factorial(first + second + 2)
            )
    face_mass = plane_inverse.T @ plane_moments @ plane_inverse
    edges = np.zeros((20, 40))
    for face in range(4):
        for row in range(10):
            for column in range(10):
                edges[face_nodes[row, face], column * 4 + face] += face_mass[row, column]
    lift = invert(mass) @ edges
    turned = np.array([lattice.index((pair[1], 3 - pair[0] - pair[1])) for pair in lattice])
    rotations = np.stack([np.arange(10), turned, turned[turned]])
    return (derivs, lift, face_nodes, rotations)


def bf16_parts(values):
    values = np.asarray(values, np.float32)
    high = values.astype(jnp.bfloat16)
    rest = values - high.astype(np.float32)
    middle = rest.astype(jnp.bfloat16)
    low = (rest - middle.astype(np.float32)).astype(jnp.bfloat16)
    return high, middle, low


def packed_row(component, node):
    return 8 * component + node if node < 8 else 48 + 2 * component + node - 8


def left_operands():
    derivs, lift, face_nodes, rotations = element_tables()
    pick = np.zeros((64, 32), np.float32)
    for face in range(4):
        for node in range(10):
            pick[16 * face + node, face_nodes[node, face]] = 1.0
    traces = np.concatenate([pick, pick, pick], axis=1)
    stack = np.zeros((3, 80, 32), np.float32)
    for index, part in enumerate(bf16_parts(derivs)):
        for axis in range(3):
            stack[index, 24 * axis : 24 * axis + 20, :20] = part[axis].astype(np.float32)
    high, middle, low = stack
    volume = np.concatenate([high, high, high, middle, low, middle], axis=1)
    blocks = np.zeros((3, 32, 64), np.float32)
    for index, part in enumerate(bf16_parts(lift)):
        for face in range(4):
            for node in range(10):
                blocks[index, :20, 16 * face + node] = part[:, node * 4 + face].astype(np.float32)
    raise_up = np.concatenate([blocks[0], blocks[1], blocks[0], blocks[0]], axis=1)
    spread = np.zeros((288, 64), np.float32)
    for turn in range(3):
        for component in range(6):
            for node in range(10):
                spread[
                    96 * turn + 16 * component + node,
                    packed_row(component, rotations[turn][node]),
                ] = 1.0
    turned = np.concatenate([spread, spread, spread], axis=1)
    packed = np.zeros((464, 256), np.float32)
    for place, matrix in zip(OPERANDS, (traces, volume, raise_up, turned)):
        packed[place : place + matrix.shape[0], : matrix.shape[1]] = matrix
    return jnp.asarray(packed)


def split(values):
    high = values.astype(jnp.bfloat16)
    rest = values - high.astype(jnp.float32)
    middle = rest.astype(jnp.bfloat16)
    low = (rest - middle.astype(jnp.float32)).astype(jnp.bfloat16)
    return high, middle, low


def iota(shape, axis):
    return lax.broadcasted_iota(jnp.int32, shape, axis)


def dot(left, right):
    return jnp.dot(left, right, preferred_element_type=jnp.float32)


def kernel(
    sizes,
    basis_hbm,
    geometry_hbm,
    normals_hbm,
    scale_hbm,
    material_hbm,
    send_list_hbm,
    source_hbm,
    turns_hbm,
    flags_hbm,
    constants_hbm,
    fresh,
    hessenberg,
    stored,
    geometry,
    normals,
    scale,
    material,
    send_list,
    source,
    turns,
    flags,
    constants_wide,
    constants,
    vector,
    field,
    inside,
    around,
    table,
    image,
    flux,
    pick_out,
    pick_in,
    gram,
    held_bound,
    side_row,
    outgoing,
    arrived,
    sums_a,
    sums_b,
    load_sem,
    halo_send,
    halo_recv,
    sum_send,
    sum_recv,
):
    n_gx, n_gy, total = sizes
    kept = basis_hbm.shape[2]
    gx = lax.axis_index("gx")
    gy = lax.axis_index("gy")
    loads = []
    for source_ref, target_ref in (
        (send_list_hbm, send_list),
        (basis_hbm, stored),
        (constants_hbm, constants_wide),
        (source_hbm, source),
        (turns_hbm, turns),
        (flags_hbm, flags),
        (geometry_hbm, geometry),
        (normals_hbm, normals),
        (scale_hbm, scale),
        (material_hbm, material),
    ):
        loads.append(pltpu.make_async_copy(source_ref, target_ref, load_sem.at[len(loads)]))
        loads[-1].start()

    def turned_on(place, step, size):
        place = place + step
        return jnp.where(place >= size, place - size, place)

    partners = []
    for direction in DIRECTIONS:
        partners.append(
            (
                turned_on(gx, (direction // 3 - 1) % n_gx, n_gx),
                turned_on(gy, (direction % 3 - 1) % n_gy, n_gy),
            )
        )
    across = lax.rem(gx, X_CHIPS)
    up = lax.div(gx, X_CHIPS)
    rows_up = n_gx // X_CHIPS
    on_gy = (n_gy, gy, [(gx, turned_on(gy, step, n_gy)) for step in range(1, n_gy)])
    on_gx = (n_gx, gx, [(turned_on(gx, step, n_gx), gy) for step in range(1, n_gx)])
    on_y = (
        rows_up,
        up,
        [(turned_on(gx, X_CHIPS * step, n_gx), gy) for step in range(1, rows_up)],
    )
    on_x = (
        X_CHIPS,
        across,
        [(gx - across + turned_on(across, step, X_CHIPS), gy) for step in range(1, X_CHIPS)],
    )
    narrow = (on_gy, on_gx)
    broad = (on_gy, on_y, on_x)

    barrier = pltpu.get_barrier_semaphore()
    greeted = [partners[index] for index in (0, 2, 5, 7)] + on_gy[2] + on_gx[2]
    for peer in greeted:
        pl.semaphore_signal(barrier, inc=1, device_id=peer, device_id_type=MESH)

    loads[0].wait()
    rows = iota((128, 128), 0)
    for tile in range(4):
        first, second = DIRECTIONS[2 * tile], DIRECTIONS[2 * tile + 1]
        wanted = jnp.concatenate(
            [
                send_list[first // 3, pl.ds(first % 3, 1), :],
                send_list[second // 3, pl.ds(second % 3, 1), :],
            ],
            axis=1,
        )
        for chunk in range(4):
            pick_out[pl.ds(128 * chunk, 128), pl.ds(128 * tile, 128)] = jnp.where(
                rows == wanted - 128 * chunk, 1.0, 0.0
            ).astype(jnp.bfloat16)

    def fill_pick_in():
        for face in range(4):
            named = source[pl.ds(face, 1), :]
            named = jnp.where(named >= 512 + 4 * 64, named - 64, named)
            for chunk in range(8):
                pick_in[pl.ds(128 * chunk, 128), pl.ds(128 * face, 128)] = jnp.where(
                    rows == named - 128 * chunk, 1.0, 0.0
                ).astype(jnp.bfloat16)

    half = iota((32, 128), 1) < 64

    def apply(turn, beside):
        for component in range(6):
            field[pl.ds(0, 20), pl.ds(128 * component, 128)] = vector[component]
        high, middle, low = split(field[...])
        inside[...] = dot(constants[pl.ds(0, 64), pl.ds(0, 96)], jnp.concatenate([high, middle, low], axis=0))
        for component in range(6):
            for face in range(4):
                lane = pl.ds(128 * face, 128)
                column = pl.ds(128 * component, 128)
                table[pl.ds(8 * component, 8), lane] = inside[pl.ds(16 * face, 8), column]
                table[pl.ds(48 + 2 * component, 2), lane] = inside[
                    pl.ds(16 * face + 8, 2), column
                ]
        parts = jnp.concatenate(split(table[...]), axis=0)
        sent = dot(parts, pick_out[...])
        sent = sent[0:64] + sent[64:128] + sent[128:192]
        for tile in range(4):
            top = sent[0:32, 128 * tile : 128 * tile + 128]
            bottom = sent[32:64, 128 * tile : 128 * tile + 128]
            outgoing[turn, 2 * tile] = jnp.where(half, top, pltpu.roll(bottom, 64, 1))
            outgoing[turn, 2 * tile + 1] = jnp.where(half, pltpu.roll(top, 64, 1), bottom)
        for index in range(8):
            pltpu.make_async_remote_copy(
                src_ref=outgoing.at[turn, index],
                dst_ref=arrived.at[turn, 7 - index],
                send_sem=halo_send.at[turn],
                recv_sem=halo_recv.at[turn],
                device_id=partners[index],
                device_id_type=MESH,
            ).start()
        around[...] = dot(
            constants[pl.ds(64, 80), pl.ds(0, 192)],
            jnp.concatenate([high, middle, low, high, high, middle], axis=0)
        )
        beside()
        found = dot(parts, pick_in[pl.ds(0, 512), :])
        pltpu.make_async_copy(arrived.at[turn], arrived.at[turn], halo_recv.at[turn]).wait()
        tops = []
        bottoms = []
        for tile in range(4):
            even = arrived[turn, 2 * tile]
            odd = arrived[turn, 2 * tile + 1]
            tops.append(jnp.where(half, even, pltpu.roll(odd, 64, 1)))
            bottoms.append(jnp.where(half, pltpu.roll(even, 64, 1), odd))
        far = jnp.concatenate(
            [jnp.concatenate(tops, axis=1), jnp.concatenate(bottoms, axis=1)], axis=0
        )
        far = jnp.concatenate(split(far), axis=0)
        found = found + dot(far, pick_in[pl.ds(512, 512), :])
        turned = dot(constants[pl.ds(176, 288), pl.ds(0, 192)], found.astype(jnp.bfloat16))
        for face in range(4):
            lane = slice(128 * face, 128 * face + 128)
            spin = turns[pl.ds(face, 1), :]
            wall = flags[pl.ds(face, 1), :] == 1
            weight = 0.5 * scale[pl.ds(face, 1), :]
            n_x = normals[0, pl.ds(face, 1), :]
            n_y = normals[1, pl.ds(face, 1), :]
            n_z = normals[2, pl.ds(face, 1), :]
            jumps = []
            for component in range(6):
                here = inside[pl.ds(16 * face, 16), pl.ds(128 * component, 128)]
                other = jnp.where(
                    spin == 0,
                    turned[16 * component : 16 * component + 16, lane],
                    jnp.where(
                        spin == 1,
                        turned[96 + 16 * component : 112 + 16 * component, lane],
                        turned[192 + 16 * component : 208 + 16 * component, lane],
                    ),
                )
                other = jnp.where(wall, -here if component < 3 else here, other)
                jumps.append(other - here)
            e_x, e_y, e_z, h_x, h_y, h_z = jumps
            along_e = n_x * e_x + n_y * e_y + n_z * e_z
            along_h = n_x * h_x + n_y * h_y + n_z * h_z
            terms = [
                n_y * h_z - n_z * h_y + e_x - along_e * n_x,
                n_z * h_x - n_x * h_z + e_y - along_e * n_y,
                n_x * h_y - n_y * h_x + e_z - along_e * n_z,
                n_z * e_y - n_y * e_z + h_x - along_h * n_x,
                n_x * e_z - n_z * e_x + h_y - along_h * n_y,
                n_y * e_x - n_x * e_y + h_z - along_h * n_z,
            ]
            for component in range(6):
                flux[pl.ds(16 * face, 16), pl.ds(128 * component, 128)] = (
                    terms[component] * weight
                )
        high, middle, low = split(flux[...])
        lifted = dot(constants[pl.ds(144, 32), :], jnp.concatenate([high, high, middle, low], axis=0))

        def gradient(axis, component):
            column = pl.ds(128 * component, 128)
            return (
                around[pl.ds(0, 20), column] * geometry[pl.ds(axis, 1), :]
                + around[pl.ds(24, 20), column] * geometry[pl.ds(3 + axis, 1), :]
                + around[pl.ds(48, 20), column] * geometry[pl.ds(6 + axis, 1), :]
            )

        for component in range(3):
            after, before = (component + 1) % 3, (component + 2) % 3
            curl_e = gradient(after, before) - gradient(before, after)
            curl_h = gradient(after, 3 + before) - gradient(before, 3 + after)
            raised = lifted[0:20, 128 * component : 128 * component + 128]
            image[component] = (
                material[pl.ds(0, 1), :] * (curl_h + raised)
                - material[pl.ds(2, 1), :] * vector[component]
            )
            raised = lifted[0:20, 384 + 128 * component : 512 + 128 * component]
            image[3 + component] = material[pl.ds(1, 1), :] * (raised - curl_e)

    sub8 = iota((8, 128), 0)
    sub24 = iota((24, 128), 0)
    lane24 = iota((24, 128), 1)
    lane1 = iota((1, 128), 1)
    eye = sub24 == lane24
    sub_k = iota((kept, 128), 0)
    lane_k = iota((kept, 128), 1)

    def inner(vector_ref):
        def some(step, held):
            held = list(held)
            for inner_step in range(4):
                node = 4 * step + inner_step
                for component in range(6):
                    held[component % 3] += (
                        stored[component, node] * vector_ref[component, pl.ds(node, 1), :]
                    )
            return tuple(held)

        zero = jnp.zeros((kept, 128), jnp.float32)
        one, two, three = lax.fori_loop(0, 5, some, (zero, zero, zero))
        column = jnp.sum(one + two + three, axis=1, keepdims=True)
        return jnp.sum(jnp.where(sub_k == lane_k, column, 0.0), axis=0, keepdims=True)

    def to_row(column):
        return jnp.sum(jnp.where(eye, column, 0.0), axis=0, keepdims=True)

    def to_column(row):
        return jnp.sum(jnp.where(eye, row, 0.0), axis=1, keepdims=True)

    def fill_gram():
        def upper(node, held):
            held = list(held)
            for component in range(6):
                tile = stored[component, node]
                for index in range(8):
                    held[index] += tile * stored[component, node, pl.ds(index, 1), :]
            return tuple(held)

        def lower(node, held):
            held = list(held)
            for component in range(6):
                tile = stored[component, node, pl.ds(8, kept - 8), :]
                for index in range(8, 16):
                    held[index - 8] += tile * stored[component, node, pl.ds(index, 1), :]
                tile = tile[8:]
                for index in range(16, kept):
                    held[index - 8] += tile * stored[component, node, pl.ds(index, 1), :]
            return tuple(held)

        def zeros(count, number):
            return (jnp.zeros((count, 128), jnp.float32),) * number

        found = list(lax.fori_loop(0, 20, upper, zeros(kept, 8)))
        found += lax.fori_loop(
            0, 20, lower, zeros(kept - 8, 8) + zeros(kept - 16, kept - 16)
        )
        gram[...] = jnp.zeros((24, 128), jnp.float32)
        for first in (0, 8, 16):
            count = kept - first
            sub = iota((count, 128), 0)
            lane = iota((count, 128), 1)
            held = jnp.zeros((count, 128), jnp.float32)
            for index in range(first, min(first + 8, kept)):
                column = jnp.sum(found[index], axis=1, keepdims=True)
                held = jnp.where(lane == index, column, held)
                row = jnp.sum(jnp.where(sub + first == lane, column, 0.0), axis=0, keepdims=True)
                held = jnp.where((sub == index - first) & (lane >= first), row, held)
            if first == 0:
                gram[pl.ds(0, kept), :] = held
            else:
                old = gram[pl.ds(first, count), :]
                gram[pl.ds(first, count), :] = jnp.where(lane >= first, held, old)

    def begin(value, buffer, groups, which, stage):
        size, mine, peers = groups[stage]
        buffer[stage, mine] = value
        for peer in peers:
            pltpu.make_async_remote_copy(
                src_ref=buffer.at[stage, mine],
                dst_ref=buffer.at[stage, mine],
                send_sem=sum_send.at[which, stage],
                recv_sem=sum_recv.at[which, stage],
                device_id=peer,
                device_id_type=MESH,
            ).start()

    def finish(buffer, groups, which, stage):
        size, mine, peers = groups[stage]
        if size > 1:
            others = buffer.at[stage, pl.ds(0, size - 1)]
            pltpu.make_async_copy(others, others, sum_recv.at[which, stage]).wait()
        values = [buffer[stage, member] for member in range(size)]
        while len(values) > 1:
            values = [sum(values[at : at + 2]) for at in range(0, len(values), 2)]
        return values[0]

    def project(column):
        weights = jnp.broadcast_to(column[0:kept], (kept, 128))
        return [jnp.sum(stored[component] * weights, axis=1) for component in range(6)]

    def whole(values):
        return jnp.sum(jnp.sum(values, axis=0), keepdims=True)

    field[pl.ds(16, 16), :] = jnp.zeros((16, 768), jnp.float32)
    table[pl.ds(56, 8), :] = jnp.zeros((8, 512), jnp.float32)
    held_bound[...] = jnp.ones((1, 128), jnp.float32)
    side_row[...] = jnp.zeros((1, 128), jnp.float32)
    hessenberg[...] = jnp.zeros((2, kept + 2), jnp.float32)
    loads[1].wait()
    loads[2].wait()
    constants[...] = constants_wide[...].astype(jnp.bfloat16)
    for component in range(6):
        vector[component] = stored[component, :, kept - 1, :]
    pl.semaphore_wait(barrier, len(greeted))

    def step(turn, carry):
        first_step = turn == 0
        sums = sums_b.at[turn]

        def beside():
            @pl.when(first_step)
            def _():
                for load in loads[3:]:
                    load.wait()
                fill_pick_in()
                fill_gram()
                packed = (
                    gram[pl.ds(0, 8), :]
                    + pltpu.roll(gram[pl.ds(8, 8), :], 32, 1)
                    + pltpu.roll(gram[pl.ds(16, 8), :], 64, 1)
                )
                begin(packed, sums_a, broad, 2, 0)

            @pl.when(jnp.logical_not(first_step))
            def _():
                side = inner(vector)
                square = whole(vector[...] * vector[...])
                side_row[...] = pltpu.roll(jnp.where(lane1 == kept, square, side), 32, 1)

        apply(turn, beside)

        @pl.when(first_step)
        def _():
            begin(finish(sums_a, broad, 2, 0), sums_a, broad, 2, 1)

        row = inner(image)
        square = whole(image[...] * image[...])
        cross = whole(vector[...] * image[...])
        row = jnp.where(lane1 == 24, square, jnp.where(lane1 == kept, cross, row))
        begin(row + side_row[...], sums, narrow, turn, 0)

        @pl.when(first_step)
        def _():
            begin(finish(sums_a, broad, 2, 1), sums_a, broad, 2, 2)

        begin(finish(sums, narrow, turn, 0), sums, narrow, turn, 1)

        @pl.when(first_step)
        def _():
            packed = finish(sums_a, broad, 2, 2) * (1.0 / total)
            products = jnp.concatenate(
                [packed, pltpu.roll(packed, 96, 1), pltpu.roll(packed, 64, 1)], axis=0
            )
            gram[...] = jnp.where(lane24 < 24, products, 0.0)

        products = gram[...]
        own = jnp.sum(jnp.where(eye, products, 0.0), axis=1, keepdims=True)
        message = finish(sums, narrow, turn, 1) * (1.0 / total)

        bound = held_bound[...][:, 0:1]
        row = jnp.where(lane1 < kept + turn, message, 0.0)
        side = jnp.where(lane1 < kept + 1, pltpu.roll(message, 96, 1), 0.0)
        square = jnp.sum(jnp.where(lane1 == 24, message, 0.0), keepdims=True)
        length = jnp.sum(jnp.where(lane1 == kept, side, 0.0), keepdims=True)
        height = jnp.sqrt(length * (bound * bound) + 1e-06)
        grow = jnp.where(first_step, 1.0, bound / height)
        side = side * jnp.where(lane1 == kept, grow * grow, grow)
        row = row * jnp.where(lane1 == kept, grow * grow, grow)
        extended = kept + turn - 1
        products = jnp.where((lane24 == kept) & (extended == kept), to_column(side), products)
        products = jnp.where((sub24 == kept) & (extended == kept), side, products)
        column = jnp.sum((jnp.where(eye, 2.0, 0.0) - products) * row, axis=1, keepdims=True)
        column_row = to_row(column)

        @pl.when(jnp.logical_not(first_step))
        def _():
            before = hessenberg[pl.ds(0, 1), :]
            hessenberg[pl.ds(0, 1), :] = jnp.where(
                lane1[:, 0:24] == kept, height, before
            )

        square = square * (grow * grow)
        length = square + jnp.sum(
            column * (products * column_row - jnp.where(eye, 2.0, 0.0) * row), keepdims=True
        )
        height = jnp.sqrt(jnp.maximum(length, 0.0) + 1e-06)
        bound = jnp.sum(jnp.abs(column) * jnp.sqrt(own), keepdims=True) + jnp.sqrt(square) + 1e-3
        held_bound[...] = jnp.broadcast_to(bound, (1, 128))
        shrink = 1.0 / jnp.where(first_step, bound, height)
        taken = project(column * shrink)
        on_own = column[kept : kept + 1] * (grow * shrink)
        for component in range(6):
            current = vector[component]
            new = image[component] * (grow * shrink) - current * on_own - taken[component]
            fresh[0, component] = current * grow
            fresh[1, component] = new
            vector[component] = new
        hessenberg[pl.ds(turn, 1), :] = jnp.where(
            lane1 == kept + 1, jnp.where(first_step, 0.0, height), column_row
        )[:, 0:24]
        return carry

    lax.fori_loop(0, 2, step, 0)
    for turn in range(2):
        pltpu.make_async_copy(outgoing.at[turn], outgoing.at[turn], halo_send.at[turn]).wait()
    for which in range(3):
        for stage, (size, _, _) in enumerate(broad if which == 2 else narrow):
            if size > 1:
                buffer = sums_a if which == 2 else sums_b.at[which]
                others = buffer.at[stage, pl.ds(0, size - 1)]
                pltpu.make_async_copy(others, others, sum_send.at[which, stage]).wait()


def body(
    n_gx,
    n_gy,
    basis,
    geometry,
    face_normals,
    face_scale,
    material,
    send_list,
    neighbour_source,
    node_rotation,
    boundary_flag,
):
    kept, components, nodes, local_count = basis.shape
    total = float(components * nodes * local_count * n_gx * n_gy)
    f32, bf16 = jnp.float32, jnp.bfloat16
    anywhere = pl.BlockSpec(memory_space=pl.ANY)
    vmem = pl.BlockSpec(memory_space=pltpu.VMEM)
    return pl.pallas_call(
        functools.partial(kernel, (n_gx, n_gy, total)),
        out_shape=(
            pltpu.VMEM((2, components, nodes, local_count), f32),
            pltpu.VMEM((2, kept + 2), f32),
        ),
        in_specs=[anywhere] * 10,
        out_specs=(vmem, vmem),
        scratch_shapes=[
            pltpu.VMEM((components, nodes, kept, local_count), f32),
            pltpu.VMEM(geometry.shape, f32),
            pltpu.VMEM(face_normals.shape, f32),
            pltpu.VMEM(face_scale.shape, f32),
            pltpu.VMEM(material.shape, f32),
            pltpu.VMEM(send_list.shape, jnp.int32),
            pltpu.VMEM(neighbour_source.shape, jnp.int32),
            pltpu.VMEM(node_rotation.shape, jnp.int32),
            pltpu.VMEM(boundary_flag.shape, jnp.int32),
            pltpu.VMEM((464, 256), f32),
            pltpu.VMEM((464, 256), bf16),
            pltpu.VMEM((components, nodes, local_count), f32),
            pltpu.VMEM((32, 768), f32),
            pltpu.VMEM((64, 768), f32),
            pltpu.VMEM((80, 768), f32),
            pltpu.VMEM((64, 512), f32),
            pltpu.VMEM((components, nodes, local_count), f32),
            pltpu.VMEM((64, 768), f32),
            pltpu.VMEM((512, 512), bf16),
            pltpu.VMEM((1024, 512), bf16),
            pltpu.VMEM((24, 128), f32),
            pltpu.VMEM((1, 128), f32),
            pltpu.VMEM((1, 128), f32),
            pltpu.VMEM((2, 8, 32, 128), f32),
            pltpu.VMEM((2, 8, 32, 128), f32),
            pltpu.VMEM((3, max(n_gx // X_CHIPS, n_gy, X_CHIPS), 8, 128), f32),
            pltpu.VMEM((2, 2, max(n_gx, n_gy), 1, 128), f32),
            pltpu.SemaphoreType.DMA((10,)),
            pltpu.SemaphoreType.DMA((2,)),
            pltpu.SemaphoreType.DMA((2,)),
            pltpu.SemaphoreType.DMA((3, 3)),
            pltpu.SemaphoreType.DMA((3, 3)),
        ],
        compiler_params=pltpu.CompilerParams(
            collective_id=0, has_side_effects=True, vmem_limit_bytes=32 * 1024 * 1024
        ),
    )(
        *[
            pltpu.with_memory_space_constraint(operand, pltpu.HBM)
            for operand in (
                jnp.transpose(basis, (1, 2, 0, 3)),
                geometry,
                face_normals,
                face_scale,
                material,
                send_list,
                neighbour_source,
                node_rotation,
                boundary_flag,
                left_operands(),
            )
        ]
    )


def solution(mesh):
    placed = (
        P(None, None, None, ("gx", "gy")),
        P(None, ("gx", "gy")),
        P(None, None, ("gx", "gy")),
        P(None, ("gx", "gy")),
        P(None, ("gx", "gy")),
        P("gx", "gy", None),
        P(None, ("gx", "gy")),
        P(None, ("gx", "gy")),
        P(None, ("gx", "gy")),
    )
    return jax.shard_map(
        functools.partial(body, mesh.shape["gx"], mesh.shape["gy"]),
        mesh=mesh,
        in_specs=placed,
        out_specs=(P(None, None, None, ("gx", "gy")), P()),
        check_vma=False,
    )
```

```python
import functools
import math

import jax
import jax.numpy as jnp
import numpy as np
from jax import lax
from jax.experimental import pallas as pl
from jax.experimental.pallas import tpu as pltpu
from jax.sharding import PartitionSpec as P

MESH = pl.DeviceIdType.MESH
X_CHIPS = 4
OPERANDS = (0, 64, 144, 176)
DIRECTIONS = (0, 1, 2, 3, 5, 6, 7, 8)


def invert(matrix):
    dimension = len(matrix)
    augmented = []
    for row_index in range(dimension):
        augmented.append(
            [float(matrix[row_index][column]) for column in range(dimension)]
            + [1.0 if column == row_index else 0.0 for column in range(dimension)]
        )
    for column in range(dimension):
        pivot_row = column
        for row_index in range(column + 1, dimension):
            if abs(augmented[row_index][column]) > abs(augmented[pivot_row][column]):
                pivot_row = row_index
        augmented[column], augmented[pivot_row] = (augmented[pivot_row], augmented[column])
        leading = augmented[column][column]
        augmented[column] = [value / leading for value in augmented[column]]
        for row_index in range(dimension):
            if row_index != column:
                factor = augmented[row_index][column]
                augmented[row_index] = [
                    left - factor * right
                    for left, right in zip(augmented[row_index], augmented[column])
                ]
    return np.array([entries[dimension:] for entries in augmented])


def locate(face, first, second):
    if face == 0:
        return (first, second, 0)
    if face == 1:
        return (first, 0, second)
    if face == 2:
        return (3 - first - second, first, second)
    return (0, first, second)


def element_tables():
    nodes = [(i, j, k) for k in range(4) for j in range(4) for i in range(4) if i + j + k <= 3]
    points = np.array(nodes) / 3.0
    vander = np.zeros((20, 20))
    slopes = np.zeros((3, 20, 20))
    for row in range(20):
        for column in range(20):
            powers = np.array(nodes[column])
            vander[row, column] = np.prod(points[row] ** powers)
            for axis in range(3):
                if powers[axis] > 0:
                    lowered = powers.copy()
                    lowered[axis] -= 1
                    slopes[axis, row, column] = powers[axis] * np.prod(points[row] ** lowered)
    inverse = invert(vander)
    derivs = np.stack([slopes[axis] @ inverse for axis in range(3)])
    moments = np.zeros((20, 20))
    for row in range(20):
        for column in range(20):
            left = nodes[row]
            right = nodes[column]
            sums = [left[0] + right[0], left[1] + right[1], left[2] + right[2]]
            moments[row, column] = (
                math.factorial(sums[0])
                * math.factorial(sums[1])
                * math.factorial(sums[2])
                / math.factorial(sum(sums) + 3)
            )
    mass = inverse.T @ moments @ inverse
    lattice = [(first, second) for second in range(4) for first in range(4) if first + second <= 3]
    face_nodes = np.array(
        [[nodes.index(locate(face, pair[0], pair[1])) for face in range(4)] for pair in lattice]
    )
    plane = np.array(
        [
            [(pair[0] / 3.0) ** expo[0] * (pair[1] / 3.0) ** expo[1] for expo in lattice]
            for pair in lattice
        ]
    )
    plane_inverse = invert(plane)
    plane_moments = np.zeros((10, 10))
    for row in range(10):
        for column in range(10):
            first = lattice[row][0] + lattice[column][0]
            second = lattice[row][1] + lattice[column][1]
            plane_moments[row, column] = (
                math.factorial(first) * math.factorial(second) / math.factorial(first + second + 2)
            )
    face_mass = plane_inverse.T @ plane_moments @ plane_inverse
    edges = np.zeros((20, 40))
    for face in range(4):
        for row in range(10):
            for column in range(10):
                edges[face_nodes[row, face], column * 4 + face] += face_mass[row, column]
    lift = invert(mass) @ edges
    turned = np.array([lattice.index((pair[1], 3 - pair[0] - pair[1])) for pair in lattice])
    rotations = np.stack([np.arange(10), turned, turned[turned]])
    return (derivs, lift, face_nodes, rotations)


def bf16_parts(values):
    values = np.asarray(values, np.float32)
    high = values.astype(jnp.bfloat16)
    rest = values - high.astype(np.float32)
    middle = rest.astype(jnp.bfloat16)
    low = (rest - middle.astype(np.float32)).astype(jnp.bfloat16)
    return high, middle, low


def packed_row(component, node):
    return 8 * component + node if node < 8 else 48 + 2 * component + node - 8


def left_operands():
    derivs, lift, face_nodes, rotations = element_tables()
    pick = np.zeros((64, 32), np.float32)
    for face in range(4):
        for node in range(10):
            pick[16 * face + node, face_nodes[node, face]] = 1.0
    traces = np.concatenate([pick, pick, pick], axis=1)
    stack = np.zeros((3, 80, 32), np.float32)
    for index, part in enumerate(bf16_parts(derivs)):
        for axis in range(3):
            stack[index, 24 * axis : 24 * axis + 20, :20] = part[axis].astype(np.float32)
    high, middle, low = stack
    volume = np.concatenate([high, high, high, middle, low, middle], axis=1)
    blocks = np.zeros((3, 32, 64), np.float32)
    for index, part in enumerate(bf16_parts(lift)):
        for face in range(4):
            for node in range(10):
                blocks[index, :20, 16 * face + node] = part[:, node * 4 + face].astype(np.float32)
    raise_up = np.concatenate([blocks[0], blocks[1], blocks[0], blocks[0]], axis=1)
    spread = np.zeros((288, 64), np.float32)
    for turn in range(3):
        for component in range(6):
            for node in range(10):
                spread[
                    96 * turn + 16 * component + node,
                    packed_row(component, rotations[turn][node]),
                ] = 1.0
    turned = np.concatenate([spread, spread, spread], axis=1)
    packed = np.zeros((464, 256), np.float32)
    for place, matrix in zip(OPERANDS, (traces, volume, raise_up, turned)):
        packed[place : place + matrix.shape[0], : matrix.shape[1]] = matrix
    return jnp.asarray(packed)


def split(values):
    high = values.astype(jnp.bfloat16)
    rest = values - high.astype(jnp.float32)
    middle = rest.astype(jnp.bfloat16)
    low = (rest - middle.astype(jnp.float32)).astype(jnp.bfloat16)
    return high, middle, low


def iota(shape, axis):
    return lax.broadcasted_iota(jnp.int32, shape, axis)


def dot(left, right):
    return jnp.dot(left, right, preferred_element_type=jnp.float32)


def kernel(
    sizes,
    basis_hbm,
    geometry_hbm,
    normals_hbm,
    scale_hbm,
    material_hbm,
    send_list_hbm,
    source_hbm,
    turns_hbm,
    flags_hbm,
    constants_hbm,
    fresh,
    hessenberg,
    stored,
    geometry,
    normals,
    scale,
    material,
    send_list,
    source,
    turns,
    flags,
    constants_wide,
    constants,
    vector,
    field,
    inside,
    around,
    table,
    parts,
    image,
    flux,
    pick_out,
    pick_in,
    gram,
    held_bound,
    side_row,
    work,
    outgoing,
    arrived,
    sums_a,
    sums_b,
    load_sem,
    halo_send,
    halo_recv,
    sum_send,
    sum_recv,
):
    n_gx, n_gy, total = sizes
    kept = basis_hbm.shape[2]
    gx = lax.axis_index("gx")
    gy = lax.axis_index("gy")
    loads = []
    for source_ref, target_ref in (
        (send_list_hbm, send_list),
        (basis_hbm, stored),
        (constants_hbm, constants_wide),
        (source_hbm, source),
        (turns_hbm, turns),
        (flags_hbm, flags),
        (geometry_hbm, geometry),
        (normals_hbm, normals),
        (scale_hbm, scale),
        (material_hbm, material),
    ):
        loads.append(pltpu.make_async_copy(source_ref, target_ref, load_sem.at[len(loads)]))
        loads[-1].start()

    def turned_on(place, step, size):
        place = place + step
        return jnp.where(place >= size, place - size, place)

    partners = []
    for direction in DIRECTIONS:
        partners.append(
            (
                turned_on(gx, (direction // 3 - 1) % n_gx, n_gx),
                turned_on(gy, (direction % 3 - 1) % n_gy, n_gy),
            )
        )
    across = lax.rem(gx, X_CHIPS)
    up = lax.div(gx, X_CHIPS)
    rows_up = n_gx // X_CHIPS

    def farthest_first(size):
        return sorted(range(1, size), key=lambda step: -min(step, size - step))

    on_gy = (n_gy, gy, [(gx, turned_on(gy, step, n_gy)) for step in farthest_first(n_gy)])
    on_gx = (n_gx, gx, [(turned_on(gx, step, n_gx), gy) for step in farthest_first(n_gx)])
    on_y = (
        rows_up,
        up,
        [(turned_on(gx, X_CHIPS * step, n_gx), gy) for step in farthest_first(rows_up)],
    )
    on_x = (
        X_CHIPS,
        across,
        [(gx - across + turned_on(across, step, X_CHIPS), gy) for step in range(1, X_CHIPS)],
    )
    narrow = (on_gy, on_gx)
    broad = (on_y, on_gy, on_x)

    barrier = pltpu.get_barrier_semaphore()
    greeted = [partners[index] for index in (0, 2, 5, 7)] + on_gy[2] + on_gx[2]
    for peer in greeted:
        pl.semaphore_signal(barrier, inc=1, device_id=peer, device_id_type=MESH)

    loads[0].wait()
    rows = iota((128, 128), 0)
    for tile in range(4):
        first, second = DIRECTIONS[2 * tile], DIRECTIONS[2 * tile + 1]
        wanted = jnp.concatenate(
            [
                send_list[first // 3, pl.ds(first % 3, 1), :],
                send_list[second // 3, pl.ds(second % 3, 1), :],
            ],
            axis=1,
        )
        for chunk in range(4):
            pick_out[pl.ds(128 * chunk, 128), pl.ds(128 * tile, 128)] = jnp.where(
                rows == wanted - 128 * chunk, 1.0, 0.0
            ).astype(jnp.bfloat16)

    def fill_pick_in():
        for face in range(4):
            named = source[pl.ds(face, 1), :]
            named = jnp.where(named >= 512 + 4 * 64, named - 64, named)
            for chunk in range(8):
                pick_in[pl.ds(128 * chunk, 128), pl.ds(128 * face, 128)] = jnp.where(
                    rows == named - 128 * chunk, 1.0, 0.0
                ).astype(jnp.bfloat16)

    half = iota((32, 128), 1) < 64

    def prepare(turn):
        for component in range(6):
            field[pl.ds(0, 20), pl.ds(128 * component, 128)] = vector[component]
        high, middle, low = split(field[...])
        inside[...] = dot(constants[pl.ds(0, 64), pl.ds(0, 96)], jnp.concatenate([high, middle, low], axis=0))
        for component in range(6):
            for face in range(4):
                lane = pl.ds(128 * face, 128)
                column = pl.ds(128 * component, 128)
                table[pl.ds(8 * component, 8), lane] = inside[pl.ds(16 * face, 8), column]
                table[pl.ds(48 + 2 * component, 2), lane] = inside[
                    pl.ds(16 * face + 8, 2), column
                ]
        parts[...] = jnp.concatenate(split(table[...]), axis=0)
        sent = dot(parts[...], pick_out[...])
        sent = sent[0:64] + sent[64:128] + sent[128:192]
        for tile in range(4):
            top = sent[0:32, 128 * tile : 128 * tile + 128]
            bottom = sent[32:64, 128 * tile : 128 * tile + 128]
            outgoing[turn, 2 * tile] = jnp.where(half, top, pltpu.roll(bottom, 64, 1))
            outgoing[turn, 2 * tile + 1] = jnp.where(half, pltpu.roll(top, 64, 1), bottom)

    def apply(turn, beside):
        for index in (0, 2, 5, 7, 1, 6, 3, 4):
            pltpu.make_async_remote_copy(
                src_ref=outgoing.at[turn, index],
                dst_ref=arrived.at[turn, 7 - index],
                send_sem=halo_send.at[turn],
                recv_sem=halo_recv.at[turn],
                device_id=partners[index],
                device_id_type=MESH,
            ).start()
        high, middle, low = split(field[...])
        around[...] = dot(
            constants[pl.ds(64, 80), pl.ds(0, 192)],
            jnp.concatenate([high, middle, low, high, high, middle], axis=0)
        )
        beside()
        found = dot(parts[...], pick_in[pl.ds(0, 512), :])
        pltpu.make_async_copy(arrived.at[turn], arrived.at[turn], halo_recv.at[turn]).wait()
        tops = []
        bottoms = []
        for tile in range(4):
            even = arrived[turn, 2 * tile]
            odd = arrived[turn, 2 * tile + 1]
            tops.append(jnp.where(half, even, pltpu.roll(odd, 64, 1)))
            bottoms.append(jnp.where(half, pltpu.roll(even, 64, 1), odd))
        far = jnp.concatenate(
            [jnp.concatenate(tops, axis=1), jnp.concatenate(bottoms, axis=1)], axis=0
        )
        far = jnp.concatenate(split(far), axis=0)
        found = found + dot(far, pick_in[pl.ds(512, 512), :])
        turned = dot(constants[pl.ds(176, 288), pl.ds(0, 192)], found.astype(jnp.bfloat16))
        for face in range(4):
            lane = slice(128 * face, 128 * face + 128)
            spin = turns[pl.ds(face, 1), :]
            wall = flags[pl.ds(face, 1), :] == 1
            weight = 0.5 * scale[pl.ds(face, 1), :]
            n_x = normals[0, pl.ds(face, 1), :]
            n_y = normals[1, pl.ds(face, 1), :]
            n_z = normals[2, pl.ds(face, 1), :]
            jumps = []
            for component in range(6):
                here = inside[pl.ds(16 * face, 16), pl.ds(128 * component, 128)]
                other = jnp.where(
                    spin == 0,
                    turned[16 * component : 16 * component + 16, lane],
                    jnp.where(
                        spin == 1,
                        turned[96 + 16 * component : 112 + 16 * component, lane],
                        turned[192 + 16 * component : 208 + 16 * component, lane],
                    ),
                )
                other = jnp.where(wall, -here if component < 3 else here, other)
                jumps.append(other - here)
            e_x, e_y, e_z, h_x, h_y, h_z = jumps
            along_e = n_x * e_x + n_y * e_y + n_z * e_z
            along_h = n_x * h_x + n_y * h_y + n_z * h_z
            terms = [
                n_y * h_z - n_z * h_y + e_x - along_e * n_x,
                n_z * h_x - n_x * h_z + e_y - along_e * n_y,
                n_x * h_y - n_y * h_x + e_z - along_e * n_z,
                n_z * e_y - n_y * e_z + h_x - along_h * n_x,
                n_x * e_z - n_z * e_x + h_y - along_h * n_y,
                n_y * e_x - n_x * e_y + h_z - along_h * n_z,
            ]
            for component in range(6):
                flux[pl.ds(16 * face, 16), pl.ds(128 * component, 128)] = (
                    terms[component] * weight
                )
        high, middle, low = split(flux[...])
        lifted = dot(constants[pl.ds(144, 32), :], jnp.concatenate([high, high, middle, low], axis=0))

        def gradient(axis, component):
            column = pl.ds(128 * component, 128)
            return (
                around[pl.ds(0, 20), column] * geometry[pl.ds(axis, 1), :]
                + around[pl.ds(24, 20), column] * geometry[pl.ds(3 + axis, 1), :]
                + around[pl.ds(48, 20), column] * geometry[pl.ds(6 + axis, 1), :]
            )

        for component in range(3):
            after, before = (component + 1) % 3, (component + 2) % 3
            curl_e = gradient(after, before) - gradient(before, after)
            curl_h = gradient(after, 3 + before) - gradient(before, 3 + after)
            raised = lifted[0:20, 128 * component : 128 * component + 128]
            image[component] = (
                material[pl.ds(0, 1), :] * (curl_h + raised)
                - material[pl.ds(2, 1), :] * vector[component]
            )
            raised = lifted[0:20, 384 + 128 * component : 512 + 128 * component]
            image[3 + component] = material[pl.ds(1, 1), :] * (raised - curl_e)

    sub8 = iota((8, 128), 0)
    sub24 = iota((24, 128), 0)
    lane24 = iota((24, 128), 1)
    lane1 = iota((1, 128), 1)
    eye = sub24 == lane24

    def inner(vector_ref, *pairs):
        def some(step, held):
            held = list(held)
            for inner_step in range(4):
                node = 4 * step + inner_step
                for component in range(6):
                    held[component % 3] += (
                        stored[component, node] * vector_ref[component, pl.ds(node, 1), :]
                    )
            return tuple(held)

        zero = jnp.zeros((kept, 128), jnp.float32)
        for place, (left, right) in enumerate(pairs):
            partial = jnp.sum(left[...] * right[...], axis=0)
            work[pl.ds(kept + place, 1), :] = jnp.sum(partial, axis=0, keepdims=True)
        one, two, three = lax.fori_loop(0, 5, some, (zero, zero, zero))
        work[pl.ds(0, kept), :] = one + two + three
        return to_row(jnp.sum(work[...], axis=1, keepdims=True))

    def to_row(column):
        return jnp.sum(jnp.where(eye, column, 0.0), axis=0, keepdims=True)

    def to_column(row):
        return jnp.sum(jnp.where(eye, row, 0.0), axis=1, keepdims=True)

    def fill_gram():
        def upper(node, held):
            held = list(held)
            for component in range(6):
                tile = stored[component, node]
                for index in range(8):
                    held[index] += tile * stored[component, node, pl.ds(index, 1), :]
            return tuple(held)

        def lower(node, held):
            held = list(held)
            for component in range(6):
                tile = stored[component, node, pl.ds(8, kept - 8), :]
                for index in range(8, 16):
                    held[index - 8] += tile * stored[component, node, pl.ds(index, 1), :]
                tile = tile[8:]
                for index in range(16, kept):
                    held[index - 8] += tile * stored[component, node, pl.ds(index, 1), :]
            return tuple(held)

        def zeros(count, number):
            return (jnp.zeros((count, 128), jnp.float32),) * number

        found = list(lax.fori_loop(0, 20, upper, zeros(kept, 8)))
        found += lax.fori_loop(
            0, 20, lower, zeros(kept - 8, 8) + zeros(kept - 16, kept - 16)
        )
        gram[...] = jnp.zeros((24, 128), jnp.float32)
        for first in (0, 8, 16):
            count = kept - first
            sub = iota((count, 128), 0)
            lane = iota((count, 128), 1)
            held = jnp.zeros((count, 128), jnp.float32)
            for index in range(first, min(first + 8, kept)):
                column = jnp.sum(found[index], axis=1, keepdims=True)
                held = jnp.where(lane == index, column, held)
                row = jnp.sum(jnp.where(sub + first == lane, column, 0.0), axis=0, keepdims=True)
                held = jnp.where((sub == index - first) & (lane >= first), row, held)
            if first == 0:
                gram[pl.ds(0, kept), :] = held
            else:
                old = gram[pl.ds(first, count), :]
                gram[pl.ds(first, count), :] = jnp.where(lane >= first, held, old)

    def begin(value, buffer, groups, which, stage):
        size, mine, peers = groups[stage]
        buffer[stage, mine] = value
        for peer in peers:
            pltpu.make_async_remote_copy(
                src_ref=buffer.at[stage, mine],
                dst_ref=buffer.at[stage, mine],
                send_sem=sum_send.at[which, stage],
                recv_sem=sum_recv.at[which, stage],
                device_id=peer,
                device_id_type=MESH,
            ).start()

    def finish(buffer, groups, which, stage):
        size, mine, peers = groups[stage]
        if size > 1:
            others = buffer.at[stage, pl.ds(0, size - 1)]
            pltpu.make_async_copy(others, others, sum_recv.at[which, stage]).wait()
        values = [buffer[stage, member] for member in range(size)]
        while len(values) > 1:
            values = [sum(values[at : at + 2]) for at in range(0, len(values), 2)]
        return values[0]

    def project(column):
        weights = jnp.broadcast_to(column[0:kept], (kept, 128))
        return [jnp.sum(stored[component] * weights, axis=1) for component in range(6)]

    field[pl.ds(16, 16), :] = jnp.zeros((16, 768), jnp.float32)
    table[pl.ds(56, 8), :] = jnp.zeros((8, 512), jnp.float32)
    held_bound[...] = jnp.ones((1, 128), jnp.float32)
    side_row[...] = jnp.zeros((1, 128), jnp.float32)
    work[...] = jnp.zeros((24, 128), jnp.float32)
    hessenberg[...] = jnp.zeros((2, kept + 2), jnp.float32)
    loads[1].wait()
    loads[2].wait()
    constants[...] = constants_wide[...].astype(jnp.bfloat16)
    for component in range(6):
        vector[component] = stored[component, :, kept - 1, :]
    prepare(0)
    pl.semaphore_wait(barrier, len(greeted))

    def step(turn, carry):
        first_step = turn == 0
        sums = sums_b.at[turn]

        def beside():
            @pl.when(first_step)
            def _():
                for load in loads[3:]:
                    load.wait()
                fill_pick_in()
                fill_gram()
                packed = (
                    gram[pl.ds(0, 8), :]
                    + pltpu.roll(gram[pl.ds(8, 8), :], 32, 1)
                    + pltpu.roll(gram[pl.ds(16, 8), :], 64, 1)
                )
                begin(packed, sums_a, broad, 2, 0)

            @pl.when(jnp.logical_not(first_step))
            def _():
                side_row[...] = pltpu.roll(inner(vector, (vector, vector)), 32, 1)

        apply(turn, beside)

        row = inner(image, (vector, image), (image, image))
        begin(row + side_row[...], sums, narrow, turn, 0)

        @pl.when(first_step)
        def _():
            begin(finish(sums_a, broad, 2, 0), sums_a, broad, 2, 1)

        begin(finish(sums, narrow, turn, 0), sums, narrow, turn, 1)

        @pl.when(first_step)
        def _():
            begin(finish(sums_a, broad, 2, 1), sums_a, broad, 2, 2)
            packed = finish(sums_a, broad, 2, 2) * (1.0 / total)
            products = jnp.concatenate(
                [packed, pltpu.roll(packed, 96, 1), pltpu.roll(packed, 64, 1)], axis=0
            )
            gram[...] = jnp.where(lane24 < 24, products, 0.0)

        products = gram[...]
        own = jnp.sum(jnp.where(eye, products, 0.0), axis=1, keepdims=True)
        message = finish(sums, narrow, turn, 1) * (1.0 / total)

        bound = held_bound[...][:, 0:1]
        row = jnp.where(lane1 < kept + turn, message, 0.0)
        side = jnp.where(lane1 < kept + 1, pltpu.roll(message, 96, 1), 0.0)
        square = jnp.sum(jnp.where(lane1 == kept + 1, message, 0.0), keepdims=True)
        length = jnp.sum(jnp.where(lane1 == kept, side, 0.0), keepdims=True)
        height = jnp.sqrt(length * (bound * bound) + 1e-06)
        grow = jnp.where(first_step, 1.0, bound / height)
        side = side * jnp.where(lane1 == kept, grow * grow, grow)
        row = row * jnp.where(lane1 == kept, grow * grow, grow)
        extended = kept + turn - 1
        products = jnp.where((lane24 == kept) & (extended == kept), to_column(side), products)
        products = jnp.where((sub24 == kept) & (extended == kept), side, products)
        column = jnp.sum((jnp.where(eye, 2.0, 0.0) - products) * row, axis=1, keepdims=True)
        column_row = to_row(column)

        @pl.when(jnp.logical_not(first_step))
        def _():
            before = hessenberg[pl.ds(0, 1), :]
            hessenberg[pl.ds(0, 1), :] = jnp.where(
                lane1[:, 0:24] == kept, height, before
            )

        square = square * (grow * grow)
        length = square + jnp.sum(
            column * (products * column_row - jnp.where(eye, 2.0, 0.0) * row), keepdims=True
        )
        height = jnp.sqrt(jnp.maximum(length, 0.0) + 1e-06)
        bound = jnp.sum(jnp.abs(column) * jnp.sqrt(own), keepdims=True) + jnp.sqrt(square) + 1e-3
        held_bound[...] = jnp.broadcast_to(bound, (1, 128))
        shrink = 1.0 / jnp.where(first_step, bound, height)
        taken = project(column)
        on_own = column[kept : kept + 1] * grow
        for component in range(6):
            current = vector[component]
            new = (image[component] * grow - current * on_own - taken[component]) * shrink
            fresh[0, component] = current * grow
            fresh[1, component] = new
            vector[component] = new
        hessenberg[pl.ds(turn, 1), :] = jnp.where(
            lane1 == kept + 1, jnp.where(first_step, 0.0, height), column_row
        )[:, 0:24]

        @pl.when(first_step)
        def _():
            prepare(1)

        return carry

    lax.fori_loop(0, 2, step, 0)
    for turn in range(2):
        pltpu.make_async_copy(outgoing.at[turn], outgoing.at[turn], halo_send.at[turn]).wait()
    for which in range(3):
        for stage, (size, _, _) in enumerate(broad if which == 2 else narrow):
            if size > 1:
                buffer = sums_a if which == 2 else sums_b.at[which]
                others = buffer.at[stage, pl.ds(0, size - 1)]
                pltpu.make_async_copy(others, others, sum_send.at[which, stage]).wait()


def body(
    n_gx,
    n_gy,
    basis,
    geometry,
    face_normals,
    face_scale,
    material,
    send_list,
    neighbour_source,
    node_rotation,
    boundary_flag,
):
    kept, components, nodes, local_count = basis.shape
    total = float(components * nodes * local_count * n_gx * n_gy)
    f32, bf16 = jnp.float32, jnp.bfloat16
    anywhere = pl.BlockSpec(memory_space=pl.ANY)
    vmem = pl.BlockSpec(memory_space=pltpu.VMEM)
    return pl.pallas_call(
        functools.partial(kernel, (n_gx, n_gy, total)),
        out_shape=(
            pltpu.VMEM((2, components, nodes, local_count), f32),
            pltpu.VMEM((2, kept + 2), f32),
        ),
        in_specs=[anywhere] * 10,
        out_specs=(vmem, vmem),
        scratch_shapes=[
            pltpu.VMEM((components, nodes, kept, local_count), f32),
            pltpu.VMEM(geometry.shape, f32),
            pltpu.VMEM(face_normals.shape, f32),
            pltpu.VMEM(face_scale.shape, f32),
            pltpu.VMEM(material.shape, f32),
            pltpu.VMEM(send_list.shape, jnp.int32),
            pltpu.VMEM(neighbour_source.shape, jnp.int32),
            pltpu.VMEM(node_rotation.shape, jnp.int32),
            pltpu.VMEM(boundary_flag.shape, jnp.int32),
            pltpu.VMEM((464, 256), f32),
            pltpu.VMEM((464, 256), bf16),
            pltpu.VMEM((components, nodes, local_count), f32),
            pltpu.VMEM((32, 768), f32),
            pltpu.VMEM((64, 768), f32),
            pltpu.VMEM((80, 768), f32),
            pltpu.VMEM((64, 512), f32),
            pltpu.VMEM((192, 512), bf16),
            pltpu.VMEM((components, nodes, local_count), f32),
            pltpu.VMEM((64, 768), f32),
            pltpu.VMEM((512, 512), bf16),
            pltpu.VMEM((1024, 512), bf16),
            pltpu.VMEM((24, 128), f32),
            pltpu.VMEM((1, 128), f32),
            pltpu.VMEM((1, 128), f32),
            pltpu.VMEM((24, 128), f32),
            pltpu.VMEM((2, 8, 32, 128), f32),
            pltpu.VMEM((2, 8, 32, 128), f32),
            pltpu.VMEM((3, max(n_gx // X_CHIPS, n_gy, X_CHIPS), 8, 128), f32),
            pltpu.VMEM((2, 2, max(n_gx, n_gy), 1, 128), f32),
            pltpu.SemaphoreType.DMA((10,)),
            pltpu.SemaphoreType.DMA((2,)),
            pltpu.SemaphoreType.DMA((2,)),
            pltpu.SemaphoreType.DMA((3, 3)),
            pltpu.SemaphoreType.DMA((3, 3)),
        ],
        compiler_params=pltpu.CompilerParams(
            collective_id=0, has_side_effects=True, vmem_limit_bytes=32 * 1024 * 1024
        ),
    )(
        *[
            pltpu.with_memory_space_constraint(operand, pltpu.HBM)
            for operand in (
                jnp.transpose(basis, (1, 2, 0, 3)),
                geometry,
                face_normals,
                face_scale,
                material,
                send_list,
                neighbour_source,
                node_rotation,
                boundary_flag,
                left_operands(),
            )
        ]
    )


def solution(mesh):
    placed = (
        P(None, None, None, ("gx", "gy")),
        P(None, ("gx", "gy")),
        P(None, None, ("gx", "gy")),
        P(None, ("gx", "gy")),
        P(None, ("gx", "gy")),
        P("gx", "gy", None),
        P(None, ("gx", "gy")),
        P(None, ("gx", "gy")),
        P(None, ("gx", "gy")),
    )
    return jax.shard_map(
        functools.partial(body, mesh.shape["gx"], mesh.shape["gy"]),
        mesh=mesh,
        in_specs=placed,
        out_specs=(P(None, None, None, ("gx", "gy")), P()),
        check_vma=False,
    )
```

```python
import functools
import math

import jax
import jax.numpy as jnp
import numpy as np
from jax import lax
from jax.experimental import pallas as pl
from jax.experimental.pallas import tpu as pltpu
from jax.sharding import PartitionSpec as P

MESH = pl.DeviceIdType.MESH
X_CHIPS = 4
OPERANDS = (0, 64, 144, 176)
DIRECTIONS = (0, 1, 2, 3, 5, 6, 7, 8)


def invert(matrix):
    dimension = len(matrix)
    augmented = []
    for row_index in range(dimension):
        augmented.append(
            [float(matrix[row_index][column]) for column in range(dimension)]
            + [1.0 if column == row_index else 0.0 for column in range(dimension)]
        )
    for column in range(dimension):
        pivot_row = column
        for row_index in range(column + 1, dimension):
            if abs(augmented[row_index][column]) > abs(augmented[pivot_row][column]):
                pivot_row = row_index
        augmented[column], augmented[pivot_row] = (augmented[pivot_row], augmented[column])
        leading = augmented[column][column]
        augmented[column] = [value / leading for value in augmented[column]]
        for row_index in range(dimension):
            if row_index != column:
                factor = augmented[row_index][column]
                augmented[row_index] = [
                    left - factor * right
                    for left, right in zip(augmented[row_index], augmented[column])
                ]
    return np.array([entries[dimension:] for entries in augmented])


def locate(face, first, second):
    if face == 0:
        return (first, second, 0)
    if face == 1:
        return (first, 0, second)
    if face == 2:
        return (3 - first - second, first, second)
    return (0, first, second)


def element_tables():
    nodes = [(i, j, k) for k in range(4) for j in range(4) for i in range(4) if i + j + k <= 3]
    points = np.array(nodes) / 3.0
    vander = np.zeros((20, 20))
    slopes = np.zeros((3, 20, 20))
    for row in range(20):
        for column in range(20):
            powers = np.array(nodes[column])
            vander[row, column] = np.prod(points[row] ** powers)
            for axis in range(3):
                if powers[axis] > 0:
                    lowered = powers.copy()
                    lowered[axis] -= 1
                    slopes[axis, row, column] = powers[axis] * np.prod(points[row] ** lowered)
    inverse = invert(vander)
    derivs = np.stack([slopes[axis] @ inverse for axis in range(3)])
    moments = np.zeros((20, 20))
    for row in range(20):
        for column in range(20):
            left = nodes[row]
            right = nodes[column]
            sums = [left[0] + right[0], left[1] + right[1], left[2] + right[2]]
            moments[row, column] = (
                math.factorial(sums[0])
                * math.factorial(sums[1])
                * math.factorial(sums[2])
                / math.factorial(sum(sums) + 3)
            )
    mass = inverse.T @ moments @ inverse
    lattice = [(first, second) for second in range(4) for first in range(4) if first + second <= 3]
    face_nodes = np.array(
        [[nodes.index(locate(face, pair[0], pair[1])) for face in range(4)] for pair in lattice]
    )
    plane = np.array(
        [
            [(pair[0] / 3.0) ** expo[0] * (pair[1] / 3.0) ** expo[1] for expo in lattice]
            for pair in lattice
        ]
    )
    plane_inverse = invert(plane)
    plane_moments = np.zeros((10, 10))
    for row in range(10):
        for column in range(10):
            first = lattice[row][0] + lattice[column][0]
            second = lattice[row][1] + lattice[column][1]
            plane_moments[row, column] = (
                math.factorial(first) * math.factorial(second) / math.factorial(first + second + 2)
            )
    face_mass = plane_inverse.T @ plane_moments @ plane_inverse
    edges = np.zeros((20, 40))
    for face in range(4):
        for row in range(10):
            for column in range(10):
                edges[face_nodes[row, face], column * 4 + face] += face_mass[row, column]
    lift = invert(mass) @ edges
    turned = np.array([lattice.index((pair[1], 3 - pair[0] - pair[1])) for pair in lattice])
    rotations = np.stack([np.arange(10), turned, turned[turned]])
    return (derivs, lift, face_nodes, rotations)


def bf16_parts(values):
    values = np.asarray(values, np.float32)
    high = values.astype(jnp.bfloat16)
    rest = values - high.astype(np.float32)
    middle = rest.astype(jnp.bfloat16)
    low = (rest - middle.astype(np.float32)).astype(jnp.bfloat16)
    return high, middle, low


def packed_row(component, node):
    return 8 * component + node if node < 8 else 48 + 2 * component + node - 8


def left_operands():
    derivs, lift, face_nodes, rotations = element_tables()
    pick = np.zeros((64, 32), np.float32)
    for face in range(4):
        for node in range(10):
            pick[16 * face + node, face_nodes[node, face]] = 1.0
    traces = np.concatenate([pick, pick, pick], axis=1)
    stack = np.zeros((3, 80, 32), np.float32)
    for index, part in enumerate(bf16_parts(derivs)):
        for axis in range(3):
            stack[index, 24 * axis : 24 * axis + 20, :20] = part[axis].astype(np.float32)
    high, middle, low = stack
    volume = np.concatenate([high, high, high, middle, low, middle], axis=1)
    blocks = np.zeros((3, 32, 64), np.float32)
    for index, part in enumerate(bf16_parts(lift)):
        for face in range(4):
            for node in range(10):
                blocks[index, :20, 16 * face + node] = part[:, node * 4 + face].astype(np.float32)
    raise_up = np.concatenate([blocks[0], blocks[1], blocks[0], blocks[0]], axis=1)
    spread = np.zeros((288, 64), np.float32)
    for turn in range(3):
        for component in range(6):
            for node in range(10):
                spread[
                    96 * turn + 16 * component + node,
                    packed_row(component, rotations[turn][node]),
                ] = 1.0
    turned = np.concatenate([spread, spread, spread], axis=1)
    packed = np.zeros((464, 256), np.float32)
    for place, matrix in zip(OPERANDS, (traces, volume, raise_up, turned)):
        packed[place : place + matrix.shape[0], : matrix.shape[1]] = matrix
    return jnp.asarray(packed)


def split(values):
    high = values.astype(jnp.bfloat16)
    rest = values - high.astype(jnp.float32)
    middle = rest.astype(jnp.bfloat16)
    low = (rest - middle.astype(jnp.float32)).astype(jnp.bfloat16)
    return high, middle, low


def iota(shape, axis):
    return lax.broadcasted_iota(jnp.int32, shape, axis)


def dot(left, right):
    return jnp.dot(left, right, preferred_element_type=jnp.float32)


def kernel(
    sizes,
    basis_hbm,
    geometry_hbm,
    normals_hbm,
    scale_hbm,
    material_hbm,
    send_list_hbm,
    source_hbm,
    turns_hbm,
    flags_hbm,
    constants_hbm,
    fresh,
    hessenberg,
    stored,
    geometry,
    normals,
    scale,
    material,
    send_list,
    source,
    turns,
    flags,
    constants_wide,
    constants,
    vector,
    field,
    inside,
    around,
    table,
    parts,
    image,
    flux,
    pick_out,
    pick_in,
    gram,
    held_bound,
    side_row,
    work,
    spread,
    taken,
    outgoing,
    arrived,
    sums_a,
    sums_b,
    load_sem,
    halo_send,
    halo_recv,
    sum_send,
    sum_recv,
):
    n_gx, n_gy, total = sizes
    kept = basis_hbm.shape[2]
    gx = lax.axis_index("gx")
    gy = lax.axis_index("gy")
    last = kept // 8 * 8
    block = (slice(None), slice(None), pl.ds(last, kept - last))
    rest = (slice(None), slice(None), pl.ds(0, last))
    loads = []
    for source_ref, target_ref in (
        (send_list_hbm, send_list),
        (basis_hbm.at[block], stored.at[block]),
        (constants_hbm.at[pl.ds(0, 64)], constants_wide.at[pl.ds(0, 64)]),
        (constants_hbm.at[pl.ds(64, 400)], constants_wide.at[pl.ds(64, 400)]),
        (basis_hbm.at[rest], stored.at[rest]),
        (source_hbm, source),
        (turns_hbm, turns),
        (flags_hbm, flags),
        (geometry_hbm, geometry),
        (normals_hbm, normals),
        (scale_hbm, scale),
        (material_hbm, material),
    ):
        loads.append(pltpu.make_async_copy(source_ref, target_ref, load_sem.at[len(loads)]))
    for load in loads[:3]:
        load.start()

    def turned_on(place, step, size):
        place = place + step
        return jnp.where(place >= size, place - size, place)

    partners = []
    for direction in DIRECTIONS:
        partners.append(
            (
                turned_on(gx, (direction // 3 - 1) % n_gx, n_gx),
                turned_on(gy, (direction % 3 - 1) % n_gy, n_gy),
            )
        )
    across = lax.rem(gx, X_CHIPS)
    up = lax.div(gx, X_CHIPS)
    rows_up = n_gx // X_CHIPS

    def farthest_first(size):
        return sorted(range(1, size), key=lambda step: -min(step, size - step))

    on_gy = (n_gy, gy, [(gx, turned_on(gy, step, n_gy)) for step in farthest_first(n_gy)])
    on_gx = (n_gx, gx, [(turned_on(gx, step, n_gx), gy) for step in farthest_first(n_gx)])
    on_y = (
        rows_up,
        up,
        [(turned_on(gx, X_CHIPS * step, n_gx), gy) for step in farthest_first(rows_up)],
    )
    on_x = (
        X_CHIPS,
        across,
        [(gx - across + turned_on(across, step, X_CHIPS), gy) for step in range(1, X_CHIPS)],
    )
    narrow = (on_gy, on_gx)
    broad = (on_y, on_gy, on_x)

    barrier = pltpu.get_barrier_semaphore()
    greeted = list(partners)
    greeted += [(gx, turned_on(gy, step, n_gy)) for step in range(2, n_gy - 1)]
    greeted += [(turned_on(gx, step, n_gx), gy) for step in range(2, n_gx - 1)]
    for peer in greeted:
        pl.semaphore_signal(barrier, inc=1, device_id=peer, device_id_type=MESH)

    loads[0].wait()
    rows = iota((128, 128), 0)
    for tile in range(4):
        first, second = DIRECTIONS[2 * tile], DIRECTIONS[2 * tile + 1]
        wanted = jnp.concatenate(
            [
                send_list[first // 3, pl.ds(first % 3, 1), :],
                send_list[second // 3, pl.ds(second % 3, 1), :],
            ],
            axis=1,
        )
        for chunk in range(4):
            pick_out[pl.ds(128 * chunk, 128), pl.ds(128 * tile, 128)] = jnp.where(
                rows == wanted - 128 * chunk, 1.0, 0.0
            ).astype(jnp.bfloat16)

    def fill_pick_in():
        for face in range(4):
            named = source[pl.ds(face, 1), :]
            named = jnp.where(named >= 512 + 4 * 64, named - 64, named)
            for chunk in range(8):
                pick_in[pl.ds(128 * chunk, 128), pl.ds(128 * face, 128)] = jnp.where(
                    rows == named - 128 * chunk, 1.0, 0.0
                ).astype(jnp.bfloat16)

    half = iota((32, 128), 1) < 64

    def prepare(turn):
        for component in range(6):
            field[pl.ds(0, 20), pl.ds(128 * component, 128)] = vector[component]
        high, middle, low = split(field[...])
        inside[...] = dot(constants[pl.ds(0, 64), pl.ds(0, 96)], jnp.concatenate([high, middle, low], axis=0))
        for component in range(6):
            for face in range(4):
                lane = pl.ds(128 * face, 128)
                column = pl.ds(128 * component, 128)
                table[pl.ds(8 * component, 8), lane] = inside[pl.ds(16 * face, 8), column]
                table[pl.ds(48 + 2 * component, 2), lane] = inside[
                    pl.ds(16 * face + 8, 2), column
                ]
        parts[...] = jnp.concatenate(split(table[...]), axis=0)
        sent = dot(parts[...], pick_out[...])
        sent = sent[0:64] + sent[64:128] + sent[128:192]
        for tile in range(4):
            top = sent[0:32, 128 * tile : 128 * tile + 128]
            bottom = sent[32:64, 128 * tile : 128 * tile + 128]
            outgoing[turn, 2 * tile] = jnp.where(half, top, pltpu.roll(bottom, 64, 1))
            outgoing[turn, 2 * tile + 1] = jnp.where(half, pltpu.roll(top, 64, 1), bottom)

    def apply(turn, beside):
        for index in (0, 2, 5, 7, 1, 6, 3, 4):
            pltpu.make_async_remote_copy(
                src_ref=outgoing.at[turn, index],
                dst_ref=arrived.at[turn, 7 - index],
                send_sem=halo_send.at[turn],
                recv_sem=halo_recv.at[turn],
                device_id=partners[index],
                device_id_type=MESH,
            ).start()
        high, middle, low = split(field[...])
        around[...] = dot(
            constants[pl.ds(64, 80), pl.ds(0, 192)],
            jnp.concatenate([high, middle, low, high, high, middle], axis=0)
        )
        beside()
        found = dot(parts[...], pick_in[pl.ds(0, 512), :])
        pltpu.make_async_copy(arrived.at[turn], arrived.at[turn], halo_recv.at[turn]).wait()
        tops = []
        bottoms = []
        for tile in range(4):
            even = arrived[turn, 2 * tile]
            odd = arrived[turn, 2 * tile + 1]
            tops.append(jnp.where(half, even, pltpu.roll(odd, 64, 1)))
            bottoms.append(jnp.where(half, pltpu.roll(even, 64, 1), odd))
        far = jnp.concatenate(
            [jnp.concatenate(tops, axis=1), jnp.concatenate(bottoms, axis=1)], axis=0
        )
        far = jnp.concatenate(split(far), axis=0)
        found = found + dot(far, pick_in[pl.ds(512, 512), :])
        turned = dot(constants[pl.ds(176, 288), pl.ds(0, 192)], found.astype(jnp.bfloat16))
        for face in range(4):
            lane = slice(128 * face, 128 * face + 128)
            spin = turns[pl.ds(face, 1), :]
            wall = flags[pl.ds(face, 1), :] == 1
            weight = 0.5 * scale[pl.ds(face, 1), :]
            n_x = normals[0, pl.ds(face, 1), :]
            n_y = normals[1, pl.ds(face, 1), :]
            n_z = normals[2, pl.ds(face, 1), :]
            jumps = []
            for component in range(6):
                here = inside[pl.ds(16 * face, 16), pl.ds(128 * component, 128)]
                other = jnp.where(
                    spin == 0,
                    turned[16 * component : 16 * component + 16, lane],
                    jnp.where(
                        spin == 1,
                        turned[96 + 16 * component : 112 + 16 * component, lane],
                        turned[192 + 16 * component : 208 + 16 * component, lane],
                    ),
                )
                other = jnp.where(wall, -here if component < 3 else here, other)
                jumps.append(other - here)
            e_x, e_y, e_z, h_x, h_y, h_z = jumps
            along_e = n_x * e_x + n_y * e_y + n_z * e_z
            along_h = n_x * h_x + n_y * h_y + n_z * h_z
            terms = [
                n_y * h_z - n_z * h_y + e_x - along_e * n_x,
                n_z * h_x - n_x * h_z + e_y - along_e * n_y,
                n_x * h_y - n_y * h_x + e_z - along_e * n_z,
                n_z * e_y - n_y * e_z + h_x - along_h * n_x,
                n_x * e_z - n_z * e_x + h_y - along_h * n_y,
                n_y * e_x - n_x * e_y + h_z - along_h * n_z,
            ]
            for component in range(6):
                flux[pl.ds(16 * face, 16), pl.ds(128 * component, 128)] = (
                    terms[component] * weight
                )
        high, middle, low = split(flux[...])
        lifted = dot(constants[pl.ds(144, 32), :], jnp.concatenate([high, high, middle, low], axis=0))

        def gradient(axis, component):
            column = pl.ds(128 * component, 128)
            return (
                around[pl.ds(0, 20), column] * geometry[pl.ds(axis, 1), :]
                + around[pl.ds(24, 20), column] * geometry[pl.ds(3 + axis, 1), :]
                + around[pl.ds(48, 20), column] * geometry[pl.ds(6 + axis, 1), :]
            )

        for component in range(3):
            after, before = (component + 1) % 3, (component + 2) % 3
            curl_e = gradient(after, before) - gradient(before, after)
            curl_h = gradient(after, 3 + before) - gradient(before, 3 + after)
            raised = lifted[0:20, 128 * component : 128 * component + 128]
            image[component] = (
                material[pl.ds(0, 1), :] * (curl_h + raised)
                - material[pl.ds(2, 1), :] * vector[component]
            )
            raised = lifted[0:20, 384 + 128 * component : 512 + 128 * component]
            image[3 + component] = material[pl.ds(1, 1), :] * (raised - curl_e)

    sub8 = iota((8, 128), 0)
    sub24 = iota((24, 128), 0)
    lane24 = iota((24, 128), 1)
    lane1 = iota((1, 128), 1)
    eye = sub24 == lane24

    def inner(vector_ref, *pairs):
        def some(step, held):
            held = list(held)
            for inner_step in range(4):
                node = 4 * step + inner_step
                for component in range(6):
                    held[component % 3] += (
                        stored[component, node] * vector_ref[component, pl.ds(node, 1), :]
                    )
            return tuple(held)

        zero = jnp.zeros((kept, 128), jnp.float32)
        for place, (left, right) in enumerate(pairs):
            partial = jnp.sum(left[...] * right[...], axis=0)
            work[pl.ds(kept + place, 1), :] = jnp.sum(partial, axis=0, keepdims=True)
        one, two, three = lax.fori_loop(0, 5, some, (zero, zero, zero))
        work[pl.ds(0, kept), :] = one + two + three
        return to_row(jnp.sum(work[...], axis=1, keepdims=True))

    def to_row(column):
        return jnp.sum(jnp.where(eye, column, 0.0), axis=0, keepdims=True)

    def to_column(row):
        return jnp.sum(jnp.where(eye, row, 0.0), axis=1, keepdims=True)

    def fill_gram():
        def upper(node, held):
            held = list(held)
            for component in range(6):
                tile = stored[component, node]
                for index in range(8):
                    held[index] += tile * stored[component, node, pl.ds(index, 1), :]
            return tuple(held)

        def lower(node, held):
            held = list(held)
            for component in range(6):
                tile = stored[component, node, pl.ds(8, kept - 8), :]
                for index in range(8, 16):
                    held[index - 8] += tile * stored[component, node, pl.ds(index, 1), :]
                tile = tile[8:]
                for index in range(16, kept):
                    held[index - 8] += tile * stored[component, node, pl.ds(index, 1), :]
            return tuple(held)

        def zeros(count, number):
            return (jnp.zeros((count, 128), jnp.float32),) * number

        found = list(lax.fori_loop(0, 20, upper, zeros(kept, 8)))
        found += lax.fori_loop(
            0, 20, lower, zeros(kept - 8, 8) + zeros(kept - 16, kept - 16)
        )
        gram[...] = jnp.zeros((24, 128), jnp.float32)
        for first in (0, 8, 16):
            count = kept - first
            sub = iota((count, 128), 0)
            lane = iota((count, 128), 1)
            held = jnp.zeros((count, 128), jnp.float32)
            for index in range(first, min(first + 8, kept)):
                column = jnp.sum(found[index], axis=1, keepdims=True)
                held = jnp.where(lane == index, column, held)
                row = jnp.sum(jnp.where(sub + first == lane, column, 0.0), axis=0, keepdims=True)
                held = jnp.where((sub == index - first) & (lane >= first), row, held)
            if first == 0:
                gram[pl.ds(0, kept), :] = held
            else:
                old = gram[pl.ds(first, count), :]
                gram[pl.ds(first, count), :] = jnp.where(lane >= first, held, old)

    def begin(value, buffer, groups, which, stage):
        size, mine, peers = groups[stage]
        buffer[stage, mine] = value
        for peer in peers:
            pltpu.make_async_remote_copy(
                src_ref=buffer.at[stage, mine],
                dst_ref=buffer.at[stage, mine],
                send_sem=sum_send.at[which, stage],
                recv_sem=sum_recv.at[which, stage],
                device_id=peer,
                device_id_type=MESH,
            ).start()

    def finish(buffer, groups, which, stage):
        size, mine, peers = groups[stage]
        if size > 1:
            others = buffer.at[stage, pl.ds(0, size - 1)]
            pltpu.make_async_copy(others, others, sum_recv.at[which, stage]).wait()
        values = [buffer[stage, member] for member in range(size)]
        while len(values) > 1:
            values = [sum(values[at : at + 2]) for at in range(0, len(values), 2)]
        return values[0]

    def project(column):
        weights = jnp.broadcast_to(column[0:kept], (kept, 128))

        def one(component, carry):
            for node in range(20):
                product = stored[component, node] * weights
                short = jnp.concatenate(
                    [product[16:kept], jnp.zeros((24 - kept, 128), jnp.float32)], axis=0
                )
                spread[component, pl.ds(8 * node, 8), :] = product[0:8] + product[8:16] + short
            return carry

        lax.fori_loop(0, 6, one, 0)
        for component in range(6):
            parts_of = [spread[component, pl.ds(at, 20, stride=8), :] for at in range(8)]
            while len(parts_of) > 1:
                parts_of = [sum(parts_of[at : at + 2]) for at in range(0, len(parts_of), 2)]
            taken[component] = parts_of[0]

    field[pl.ds(16, 16), :] = jnp.zeros((16, 768), jnp.float32)
    table[pl.ds(56, 8), :] = jnp.zeros((8, 512), jnp.float32)
    held_bound[...] = jnp.ones((1, 128), jnp.float32)
    side_row[...] = jnp.zeros((1, 128), jnp.float32)
    work[...] = jnp.zeros((24, 128), jnp.float32)
    hessenberg[...] = jnp.zeros((2, kept + 2), jnp.float32)
    loads[1].wait()
    loads[2].wait()
    for load in loads[3:]:
        load.start()
    constants[pl.ds(0, 64), :] = constants_wide[pl.ds(0, 64), :].astype(jnp.bfloat16)
    for component in range(6):
        vector[component] = stored[component, :, kept - 1, :]
    prepare(0)
    for load in loads[3:]:
        load.wait()
    constants[pl.ds(64, 400), :] = constants_wide[pl.ds(64, 400), :].astype(jnp.bfloat16)
    pl.semaphore_wait(barrier, len(greeted))

    def step(turn, carry):
        first_step = turn == 0
        sums = sums_b.at[turn]

        def beside():
            @pl.when(first_step)
            def _():
                fill_pick_in()
                fill_gram()
                packed = (
                    gram[pl.ds(0, 8), :]
                    + pltpu.roll(gram[pl.ds(8, 8), :], 32, 1)
                    + pltpu.roll(gram[pl.ds(16, 8), :], 64, 1)
                )
                begin(packed, sums_a, broad, 2, 0)

            @pl.when(jnp.logical_not(first_step))
            def _():
                side_row[...] = pltpu.roll(inner(vector, (vector, vector)), 32, 1)

        apply(turn, beside)

        row = inner(image, (vector, image), (image, image))
        begin(row + side_row[...], sums, narrow, turn, 0)

        @pl.when(first_step)
        def _():
            begin(finish(sums_a, broad, 2, 0), sums_a, broad, 2, 1)

        begin(finish(sums, narrow, turn, 0), sums, narrow, turn, 1)

        @pl.when(first_step)
        def _():
            begin(finish(sums_a, broad, 2, 1), sums_a, broad, 2, 2)
            packed = finish(sums_a, broad, 2, 2) * (1.0 / total)
            products = jnp.concatenate(
                [packed, pltpu.roll(packed, 96, 1), pltpu.roll(packed, 64, 1)], axis=0
            )
            gram[...] = jnp.where(lane24 < 24, products, 0.0)

        products = gram[...]
        own = jnp.sum(jnp.where(eye, products, 0.0), axis=1, keepdims=True)
        message = finish(sums, narrow, turn, 1) * (1.0 / total)

        bound = held_bound[...][:, 0:1]
        row = jnp.where(lane1 < kept + turn, message, 0.0)
        side = jnp.where(lane1 < kept + 1, pltpu.roll(message, 96, 1), 0.0)
        square = jnp.sum(jnp.where(lane1 == kept + 1, message, 0.0), keepdims=True)
        length = jnp.sum(jnp.where(lane1 == kept, side, 0.0), keepdims=True)
        height = jnp.sqrt(length * (bound * bound) + 1e-06)
        grow = jnp.where(first_step, 1.0, bound / height)
        side = side * jnp.where(lane1 == kept, grow * grow, grow)
        row = row * jnp.where(lane1 == kept, grow * grow, grow)
        extended = kept + turn - 1
        products = jnp.where((lane24 == kept) & (extended == kept), to_column(side), products)
        products = jnp.where((sub24 == kept) & (extended == kept), side, products)
        column = jnp.sum((jnp.where(eye, 2.0, 0.0) - products) * row, axis=1, keepdims=True)
        column_row = to_row(column)

        @pl.when(jnp.logical_not(first_step))
        def _():
            before = hessenberg[pl.ds(0, 1), :]
            hessenberg[pl.ds(0, 1), :] = jnp.where(
                lane1[:, 0:24] == kept, height, before
            )

        square = square * (grow * grow)
        length = square + jnp.sum(
            column * (products * column_row - jnp.where(eye, 2.0, 0.0) * row), keepdims=True
        )
        height = jnp.sqrt(jnp.maximum(length, 0.0) + 1e-06)
        bound = jnp.sum(jnp.abs(column) * jnp.sqrt(own), keepdims=True) + jnp.sqrt(square) + 1e-3
        held_bound[...] = jnp.broadcast_to(bound, (1, 128))
        shrink = 1.0 / jnp.where(first_step, bound, height)
        project(column)
        on_own = column[kept : kept + 1] * grow
        for component in range(6):
            current = vector[component]
            new = (image[component] * grow - current * on_own - taken[component]) * shrink
            fresh[0, component] = current * grow
            fresh[1, component] = new
            vector[component] = new
        hessenberg[pl.ds(turn, 1), :] = jnp.where(
            lane1 == kept + 1, jnp.where(first_step, 0.0, height), column_row
        )[:, 0:24]

        @pl.when(first_step)
        def _():
            prepare(1)

        return carry

    lax.fori_loop(0, 2, step, 0)
    for turn in range(2):
        pltpu.make_async_copy(outgoing.at[turn], outgoing.at[turn], halo_send.at[turn]).wait()
    for which in range(3):
        for stage, (size, _, _) in enumerate(broad if which == 2 else narrow):
            if size > 1:
                buffer = sums_a if which == 2 else sums_b.at[which]
                others = buffer.at[stage, pl.ds(0, size - 1)]
                pltpu.make_async_copy(others, others, sum_send.at[which, stage]).wait()


def body(
    n_gx,
    n_gy,
    basis,
    geometry,
    face_normals,
    face_scale,
    material,
    send_list,
    neighbour_source,
    node_rotation,
    boundary_flag,
):
    kept, components, nodes, local_count = basis.shape
    total = float(components * nodes * local_count * n_gx * n_gy)
    f32, bf16 = jnp.float32, jnp.bfloat16
    anywhere = pl.BlockSpec(memory_space=pl.ANY)
    vmem = pl.BlockSpec(memory_space=pltpu.VMEM)
    return pl.pallas_call(
        functools.partial(kernel, (n_gx, n_gy, total)),
        out_shape=(
            pltpu.VMEM((2, components, nodes, local_count), f32),
            pltpu.VMEM((2, kept + 2), f32),
        ),
        in_specs=[anywhere] * 10,
        out_specs=(vmem, vmem),
        scratch_shapes=[
            pltpu.VMEM((components, nodes, kept, local_count), f32),
            pltpu.VMEM(geometry.shape, f32),
            pltpu.VMEM(face_normals.shape, f32),
            pltpu.VMEM(face_scale.shape, f32),
            pltpu.VMEM(material.shape, f32),
            pltpu.VMEM(send_list.shape, jnp.int32),
            pltpu.VMEM(neighbour_source.shape, jnp.int32),
            pltpu.VMEM(node_rotation.shape, jnp.int32),
            pltpu.VMEM(boundary_flag.shape, jnp.int32),
            pltpu.VMEM((464, 256), f32),
            pltpu.VMEM((464, 256), bf16),
            pltpu.VMEM((components, nodes, local_count), f32),
            pltpu.VMEM((32, 768), f32),
            pltpu.VMEM((64, 768), f32),
            pltpu.VMEM((80, 768), f32),
            pltpu.VMEM((64, 512), f32),
            pltpu.VMEM((192, 512), bf16),
            pltpu.VMEM((components, nodes, local_count), f32),
            pltpu.VMEM((64, 768), f32),
            pltpu.VMEM((512, 512), bf16),
            pltpu.VMEM((1024, 512), bf16),
            pltpu.VMEM((24, 128), f32),
            pltpu.VMEM((1, 128), f32),
            pltpu.VMEM((1, 128), f32),
            pltpu.VMEM((24, 128), f32),
            pltpu.VMEM((components, 8 * nodes, local_count), f32),
            pltpu.VMEM((components, nodes, local_count), f32),
            pltpu.VMEM((2, 8, 32, 128), f32),
            pltpu.VMEM((2, 8, 32, 128), f32),
            pltpu.VMEM((3, max(n_gx // X_CHIPS, n_gy, X_CHIPS), 8, 128), f32),
            pltpu.VMEM((2, 2, max(n_gx, n_gy), 1, 128), f32),
            pltpu.SemaphoreType.DMA((12,)),
            pltpu.SemaphoreType.DMA((2,)),
            pltpu.SemaphoreType.DMA((2,)),
            pltpu.SemaphoreType.DMA((3, 3)),
            pltpu.SemaphoreType.DMA((3, 3)),
        ],
        compiler_params=pltpu.CompilerParams(
            collective_id=0, has_side_effects=True, vmem_limit_bytes=32 * 1024 * 1024
        ),
    )(
        *[
            pltpu.with_memory_space_constraint(operand, pltpu.HBM)
            for operand in (
                jnp.transpose(basis, (1, 2, 0, 3)),
                geometry,
                face_normals,
                face_scale,
                material,
                send_list,
                neighbour_source,
                node_rotation,
                boundary_flag,
                left_operands(),
            )
        ]
    )


def solution(mesh):
    placed = (
        P(None, None, None, ("gx", "gy")),
        P(None, ("gx", "gy")),
        P(None, None, ("gx", "gy")),
        P(None, ("gx", "gy")),
        P(None, ("gx", "gy")),
        P("gx", "gy", None),
        P(None, ("gx", "gy")),
        P(None, ("gx", "gy")),
        P(None, ("gx", "gy")),
    )
    return jax.shard_map(
        functools.partial(body, mesh.shape["gx"], mesh.shape["gy"]),
        mesh=mesh,
        in_specs=placed,
        out_specs=(P(None, None, None, ("gx", "gy")), P()),
        check_vma=False,
    )
```

```python
import functools
import math

import jax
import jax.numpy as jnp
import numpy as np
from jax import lax
from jax.experimental import pallas as pl
from jax.experimental.pallas import tpu as pltpu
from jax.sharding import PartitionSpec as P

MESH = pl.DeviceIdType.MESH
X_CHIPS = 4
OPERANDS = (0, 80, 112)
DIRECTIONS = (0, 1, 2, 3, 5, 6, 7, 8)


def invert(matrix):
    dimension = len(matrix)
    augmented = []
    for row_index in range(dimension):
        augmented.append(
            [float(matrix[row_index][column]) for column in range(dimension)]
            + [1.0 if column == row_index else 0.0 for column in range(dimension)]
        )
    for column in range(dimension):
        pivot_row = column
        for row_index in range(column + 1, dimension):
            if abs(augmented[row_index][column]) > abs(augmented[pivot_row][column]):
                pivot_row = row_index
        augmented[column], augmented[pivot_row] = (augmented[pivot_row], augmented[column])
        leading = augmented[column][column]
        augmented[column] = [value / leading for value in augmented[column]]
        for row_index in range(dimension):
            if row_index != column:
                factor = augmented[row_index][column]
                augmented[row_index] = [
                    left - factor * right
                    for left, right in zip(augmented[row_index], augmented[column])
                ]
    return np.array([entries[dimension:] for entries in augmented])


def locate(face, first, second):
    if face == 0:
        return (first, second, 0)
    if face == 1:
        return (first, 0, second)
    if face == 2:
        return (3 - first - second, first, second)
    return (0, first, second)


def element_tables():
    nodes = [(i, j, k) for k in range(4) for j in range(4) for i in range(4) if i + j + k <= 3]
    points = np.array(nodes) / 3.0
    vander = np.zeros((20, 20))
    slopes = np.zeros((3, 20, 20))
    for row in range(20):
        for column in range(20):
            powers = np.array(nodes[column])
            vander[row, column] = np.prod(points[row] ** powers)
            for axis in range(3):
                if powers[axis] > 0:
                    lowered = powers.copy()
                    lowered[axis] -= 1
                    slopes[axis, row, column] = powers[axis] * np.prod(points[row] ** lowered)
    inverse = invert(vander)
    derivs = np.stack([slopes[axis] @ inverse for axis in range(3)])
    moments = np.zeros((20, 20))
    for row in range(20):
        for column in range(20):
            left = nodes[row]
            right = nodes[column]
            sums = [left[0] + right[0], left[1] + right[1], left[2] + right[2]]
            moments[row, column] = (
                math.factorial(sums[0])
                * math.factorial(sums[1])
                * math.factorial(sums[2])
                / math.factorial(sum(sums) + 3)
            )
    mass = inverse.T @ moments @ inverse
    lattice = [(first, second) for second in range(4) for first in range(4) if first + second <= 3]
    face_nodes = np.array(
        [[nodes.index(locate(face, pair[0], pair[1])) for face in range(4)] for pair in lattice]
    )
    plane = np.array(
        [
            [(pair[0] / 3.0) ** expo[0] * (pair[1] / 3.0) ** expo[1] for expo in lattice]
            for pair in lattice
        ]
    )
    plane_inverse = invert(plane)
    plane_moments = np.zeros((10, 10))
    for row in range(10):
        for column in range(10):
            first = lattice[row][0] + lattice[column][0]
            second = lattice[row][1] + lattice[column][1]
            plane_moments[row, column] = (
                math.factorial(first) * math.factorial(second) / math.factorial(first + second + 2)
            )
    face_mass = plane_inverse.T @ plane_moments @ plane_inverse
    edges = np.zeros((20, 40))
    for face in range(4):
        for row in range(10):
            for column in range(10):
                edges[face_nodes[row, face], column * 4 + face] += face_mass[row, column]
    lift = invert(mass) @ edges
    turned = np.array([lattice.index((pair[1], 3 - pair[0] - pair[1])) for pair in lattice])
    rotations = np.stack([np.arange(10), turned, turned[turned]])
    return (derivs, lift, face_nodes, rotations)


def bf16_parts(values):
    values = np.asarray(values, np.float32)
    high = values.astype(jnp.bfloat16)
    rest = values - high.astype(np.float32)
    middle = rest.astype(jnp.bfloat16)
    low = (rest - middle.astype(np.float32)).astype(jnp.bfloat16)
    return high, middle, low


def packed_row(component, node):
    return 8 * component + node if node < 8 else 48 + 2 * component + node - 8


def left_operands():
    derivs, lift, face_nodes, rotations = element_tables()
    stack = np.zeros((3, 80, 32), np.float32)
    for index, part in enumerate(bf16_parts(derivs)):
        for axis in range(3):
            stack[index, 24 * axis : 24 * axis + 20, :20] = part[axis].astype(np.float32)
    high, middle, low = stack
    volume = np.concatenate([high, high, high, middle, low, middle], axis=1)
    blocks = np.zeros((3, 32, 64), np.float32)
    for index, part in enumerate(bf16_parts(lift)):
        for face in range(4):
            for node in range(10):
                blocks[index, :20, 16 * face + node] = part[:, node * 4 + face].astype(np.float32)
    raise_up = np.concatenate([blocks[0], blocks[1], blocks[0], blocks[0]], axis=1)
    spread = np.zeros((192, 64), np.float32)
    for turn in range(3):
        for component in range(6):
            for node in range(10):
                spread[
                    64 * turn + packed_row(component, node),
                    packed_row(component, rotations[turn][node]),
                ] = 1.0
    turned = np.concatenate([spread, spread, spread], axis=1)
    packed = np.zeros((304, 256), np.float32)
    for place, matrix in zip(OPERANDS, (volume, raise_up, turned)):
        packed[place : place + matrix.shape[0], : matrix.shape[1]] = matrix
    return jnp.asarray(packed)


def split(values):
    high = values.astype(jnp.bfloat16)
    rest = values - high.astype(jnp.float32)
    middle = rest.astype(jnp.bfloat16)
    low = (rest - middle.astype(jnp.float32)).astype(jnp.bfloat16)
    return high, middle, low


def iota(shape, axis):
    return lax.broadcasted_iota(jnp.int32, shape, axis)


def dot(left, right):
    return jnp.dot(left, right, preferred_element_type=jnp.float32)


def kernel(
    sizes,
    basis_hbm,
    geometry_hbm,
    normals_hbm,
    scale_hbm,
    material_hbm,
    send_list_hbm,
    source_hbm,
    turns_hbm,
    flags_hbm,
    constants_hbm,
    fresh,
    hessenberg,
    stored,
    geometry,
    normals,
    scale,
    material,
    send_list,
    source,
    turns,
    flags,
    constants_wide,
    constants,
    vector,
    field,
    around,
    table,
    others,
    rotated,
    image,
    flux,
    index_out,
    index_in,
    gram,
    held_bound,
    side_row,
    work,
    spread,
    taken,
    outgoing,
    arrived,
    sums_a,
    sums_b,
    load_sem,
    halo_send,
    halo_recv,
    sum_send,
    sum_recv,
):
    n_gx, n_gy, total, face_nodes = sizes
    kept = basis_hbm.shape[2]
    gx = lax.axis_index("gx")
    gy = lax.axis_index("gy")
    last = kept // 8 * 8
    block = (slice(None), slice(None), pl.ds(last, kept - last))
    rest = (slice(None), slice(None), pl.ds(0, last))
    loads = []
    for source_ref, target_ref in (
        (send_list_hbm, send_list),
        (basis_hbm.at[block], stored.at[block]),
        (constants_hbm, constants_wide),
        (basis_hbm.at[rest], stored.at[rest]),
        (source_hbm, source),
        (turns_hbm, turns),
        (flags_hbm, flags),
        (geometry_hbm, geometry),
        (normals_hbm, normals),
        (scale_hbm, scale),
        (material_hbm, material),
    ):
        loads.append(pltpu.make_async_copy(source_ref, target_ref, load_sem.at[len(loads)]))
    for load in loads[:2]:
        load.start()

    def turned_on(place, step, size):
        place = place + step
        return jnp.where(place >= size, place - size, place)

    partners = []
    for direction in DIRECTIONS:
        partners.append(
            (
                turned_on(gx, (direction // 3 - 1) % n_gx, n_gx),
                turned_on(gy, (direction % 3 - 1) % n_gy, n_gy),
            )
        )
    across = lax.rem(gx, X_CHIPS)
    up = lax.div(gx, X_CHIPS)
    rows_up = n_gx // X_CHIPS

    def farthest_first(size):
        return sorted(range(1, size), key=lambda step: -min(step, size - step))

    on_gy = (n_gy, gy, [(gx, turned_on(gy, step, n_gy)) for step in farthest_first(n_gy)])
    on_gx = (n_gx, gx, [(turned_on(gx, step, n_gx), gy) for step in farthest_first(n_gx)])
    on_y = (
        rows_up,
        up,
        [(turned_on(gx, X_CHIPS * step, n_gx), gy) for step in farthest_first(rows_up)],
    )
    on_x = (
        X_CHIPS,
        across,
        [(gx - across + turned_on(across, step, X_CHIPS), gy) for step in range(1, X_CHIPS)],
    )
    narrow = (on_gy, on_gx)
    broad = (on_y, on_gy, on_x)

    barrier = pltpu.get_barrier_semaphore()
    greeted = list(partners)
    greeted += [(gx, turned_on(gy, step, n_gy)) for step in range(2, n_gy - 1)]
    greeted += [(turned_on(gx, step, n_gx), gy) for step in range(2, n_gx - 1)]
    for peer in greeted:
        pl.semaphore_signal(barrier, inc=1, device_id=peer, device_id_type=MESH)

    loads[0].wait()
    for tile in range(4):
        first, second = DIRECTIONS[2 * tile], DIRECTIONS[2 * tile + 1]
        index_out[pl.ds(tile, 1), :] = jnp.concatenate(
            [
                send_list[first // 3, pl.ds(first % 3, 1), :],
                send_list[second // 3, pl.ds(second % 3, 1), :],
            ],
            axis=1,
        )

    def pick(found, sources, index, first):
        lane = jnp.broadcast_to(jnp.bitwise_and(index, 127), (64, 128))
        tile = jnp.broadcast_to(jnp.right_shift(index, 7), (64, 128))
        for place, values in enumerate(sources):
            picked = jnp.take_along_axis(values, lane, axis=1, mode="promise_in_bounds")
            found = picked if found is None else jnp.where(tile == first + place, picked, found)
        return found

    half = iota((32, 128), 1) < 64

    def prepare(turn, greeting):
        for component in range(6):
            for face in range(4):
                for node in range(10):
                    row = pl.ds(packed_row(component, node), 1)
                    table[row, pl.ds(128 * face, 128)] = vector[
                        component, pl.ds(int(face_nodes[node, face]), 1), :
                    ]
        greeting()
        sources = [table[:, pl.ds(128 * tile, 128)] for tile in range(4)]
        for tile in (0, 3, 1, 2):
            sent = pick(None, sources, index_out[pl.ds(tile, 1), :], 0)
            top = sent[0:32]
            bottom = sent[32:64]
            outgoing[turn, 2 * tile] = jnp.where(half, top, pltpu.roll(bottom, 64, 1))
            outgoing[turn, 2 * tile + 1] = jnp.where(half, pltpu.roll(top, 64, 1), bottom)
            for index in (2 * tile, 2 * tile + 1):
                pltpu.make_async_remote_copy(
                    src_ref=outgoing.at[turn, index],
                    dst_ref=arrived.at[turn, 7 - index],
                    send_sem=halo_send.at[turn],
                    recv_sem=halo_recv.at[turn],
                    device_id=partners[index],
                    device_id_type=MESH,
                ).start()

    def apply(turn, ready, beside):
        ready()
        for component in range(6):
            field[pl.ds(0, 20), pl.ds(128 * component, 128)] = vector[component]
        high, middle, low = split(field[...])
        around[...] = dot(
            constants[pl.ds(0, 80), pl.ds(0, 192)],
            jnp.concatenate([high, middle, low, high, high, middle], axis=0)
        )

        def gradient(axis, component):
            column = pl.ds(128 * component, 128)
            return (
                around[pl.ds(0, 20), column] * geometry[pl.ds(axis, 1), :]
                + around[pl.ds(24, 20), column] * geometry[pl.ds(3 + axis, 1), :]
                + around[pl.ds(48, 20), column] * geometry[pl.ds(6 + axis, 1), :]
            )

        for component in range(3):
            after, before = (component + 1) % 3, (component + 2) % 3
            curl_e = gradient(after, before) - gradient(before, after)
            curl_h = gradient(after, 3 + before) - gradient(before, 3 + after)
            image[component] = (
                material[pl.ds(0, 1), :] * curl_h - material[pl.ds(2, 1), :] * vector[component]
            )
            image[3 + component] = -material[pl.ds(1, 1), :] * curl_e
        beside()
        sources = [table[:, pl.ds(128 * tile, 128)] for tile in range(4)]
        for face in range(4):
            lane = pl.ds(128 * face, 128)
            others[:, lane] = pick(None, sources, index_in[pl.ds(face, 1), :], 0)
        pltpu.make_async_copy(arrived.at[turn], arrived.at[turn], halo_recv.at[turn]).wait()
        sources = []
        for tile in range(4):
            even = arrived[turn, 2 * tile]
            odd = arrived[turn, 2 * tile + 1]
            sources.append(
                jnp.concatenate(
                    [
                        jnp.where(half, even, pltpu.roll(odd, 64, 1)),
                        jnp.where(half, pltpu.roll(even, 64, 1), odd),
                    ],
                    axis=0,
                )
            )
        found = jnp.concatenate(
            [
                pick(
                    others[:, pl.ds(128 * face, 128)], sources, index_in[pl.ds(face, 1), :], 4
                )
                for face in range(4)
            ],
            axis=1,
        )
        rotated[...] = dot(
            constants[pl.ds(112, 192), pl.ds(0, 192)], jnp.concatenate(split(found), axis=0)
        )
        for face in range(4):
            lane = pl.ds(128 * face, 128)
            spin = turns[pl.ds(face, 1), :]
            wall = flags[pl.ds(face, 1), :] == 1
            weight = 0.5 * scale[pl.ds(face, 1), :]
            n_x = normals[0, pl.ds(face, 1), :]
            n_y = normals[1, pl.ds(face, 1), :]
            n_z = normals[2, pl.ds(face, 1), :]
            for first_node, count in ((0, 8), (8, 2)):
                jumps = []
                for component in range(6):
                    row = packed_row(component, first_node)
                    here = table[pl.ds(row, count), lane]
                    other = jnp.where(
                        spin == 0,
                        rotated[pl.ds(row, count), lane],
                        jnp.where(
                            spin == 1,
                            rotated[pl.ds(64 + row, count), lane],
                            rotated[pl.ds(128 + row, count), lane],
                        ),
                    )
                    other = jnp.where(wall, -here if component < 3 else here, other)
                    jumps.append(other - here)
                e_x, e_y, e_z, h_x, h_y, h_z = jumps
                along_e = n_x * e_x + n_y * e_y + n_z * e_z
                along_h = n_x * h_x + n_y * h_y + n_z * h_z
                terms = [
                    n_y * h_z - n_z * h_y + e_x - along_e * n_x,
                    n_z * h_x - n_x * h_z + e_y - along_e * n_y,
                    n_x * h_y - n_y * h_x + e_z - along_e * n_z,
                    n_z * e_y - n_y * e_z + h_x - along_h * n_x,
                    n_x * e_z - n_z * e_x + h_y - along_h * n_y,
                    n_y * e_x - n_x * e_y + h_z - along_h * n_z,
                ]
                for component in range(6):
                    place = pl.ds(16 * face + first_node, count)
                    flux[place, pl.ds(128 * component, 128)] = terms[component] * weight
        high, middle, low = split(flux[...])
        lifted = dot(constants[pl.ds(80, 32), :], jnp.concatenate([high, high, middle, low], axis=0))
        for component in range(6):
            raised = lifted[0:20, 128 * component : 128 * component + 128]
            image[component] += material[pl.ds(component // 3, 1), :] * raised

    sub8 = iota((8, 128), 0)
    sub24 = iota((24, 128), 0)
    lane24 = iota((24, 128), 1)
    lane1 = iota((1, 128), 1)
    eye = sub24 == lane24

    def inner(vector_ref, *pairs):
        def some(component, held):
            held = list(held)
            for node in range(20):
                held[node % 3] += (
                    stored[component, node] * vector_ref[component, pl.ds(node, 1), :]
                )
            return tuple(held)

        zero = jnp.zeros((kept, 128), jnp.float32)
        for place, (left, right) in enumerate(pairs):
            partial = jnp.sum(left[...] * right[...], axis=0)
            work[pl.ds(kept + place, 1), :] = jnp.sum(partial, axis=0, keepdims=True)
        one, two, three = lax.fori_loop(0, 6, some, (zero, zero, zero))
        work[pl.ds(0, kept), :] = one + two + three
        return to_row(jnp.sum(work[...], axis=1, keepdims=True))

    def to_row(column):
        return jnp.sum(jnp.where(eye, column, 0.0), axis=0, keepdims=True)

    def to_column(row):
        return jnp.sum(jnp.where(eye, row, 0.0), axis=1, keepdims=True)

    def fill_gram():
        def upper(node, held):
            held = list(held)
            for component in range(6):
                tile = stored[component, node]
                for index in range(8):
                    held[index] += tile * stored[component, node, pl.ds(index, 1), :]
            return tuple(held)

        def lower(node, held):
            held = list(held)
            for component in range(6):
                tile = stored[component, node, pl.ds(8, kept - 8), :]
                for index in range(8, 16):
                    held[index - 8] += tile * stored[component, node, pl.ds(index, 1), :]
                tile = tile[8:]
                for index in range(16, kept):
                    held[index - 8] += tile * stored[component, node, pl.ds(index, 1), :]
            return tuple(held)

        def zeros(count, number):
            return (jnp.zeros((count, 128), jnp.float32),) * number

        found = list(lax.fori_loop(0, 20, upper, zeros(kept, 8)))
        found += lax.fori_loop(
            0, 20, lower, zeros(kept - 8, 8) + zeros(kept - 16, kept - 16)
        )
        gram[...] = jnp.zeros((24, 128), jnp.float32)
        for first in (0, 8, 16):
            count = kept - first
            sub = iota((count, 128), 0)
            lane = iota((count, 128), 1)
            held = jnp.zeros((count, 128), jnp.float32)
            for index in range(first, min(first + 8, kept)):
                column = jnp.sum(found[index], axis=1, keepdims=True)
                held = jnp.where(lane == index, column, held)
                row = jnp.sum(jnp.where(sub + first == lane, column, 0.0), axis=0, keepdims=True)
                held = jnp.where((sub == index - first) & (lane >= first), row, held)
            if first == 0:
                gram[pl.ds(0, kept), :] = held
            else:
                old = gram[pl.ds(first, count), :]
                gram[pl.ds(first, count), :] = jnp.where(lane >= first, held, old)

    def begin(value, buffer, groups, which, stage):
        size, mine, peers = groups[stage]
        buffer[stage, mine] = value
        for peer in peers:
            pltpu.make_async_remote_copy(
                src_ref=buffer.at[stage, mine],
                dst_ref=buffer.at[stage, mine],
                send_sem=sum_send.at[which, stage],
                recv_sem=sum_recv.at[which, stage],
                device_id=peer,
                device_id_type=MESH,
            ).start()

    def finish(buffer, groups, which, stage):
        size, mine, peers = groups[stage]
        if size > 1:
            others = buffer.at[stage, pl.ds(0, size - 1)]
            pltpu.make_async_copy(others, others, sum_recv.at[which, stage]).wait()
        values = [buffer[stage, member] for member in range(size)]
        while len(values) > 1:
            values = [sum(values[at : at + 2]) for at in range(0, len(values), 2)]
        return values[0]

    def project(column):
        weights = jnp.broadcast_to(column[0:kept], (kept, 128))

        def one(component, carry):
            for node in range(20):
                product = stored[component, node] * weights
                short = jnp.concatenate(
                    [product[16:kept], jnp.zeros((24 - kept, 128), jnp.float32)], axis=0
                )
                spread[component, pl.ds(8 * node, 8), :] = product[0:8] + product[8:16] + short
            return carry

        lax.fori_loop(0, 6, one, 0)
        for component in range(6):
            parts_of = [spread[component, pl.ds(at, 20, stride=8), :] for at in range(8)]
            while len(parts_of) > 1:
                parts_of = [sum(parts_of[at : at + 2]) for at in range(0, len(parts_of), 2)]
            taken[component] = parts_of[0]

    field[pl.ds(16, 16), :] = jnp.zeros((16, 768), jnp.float32)
    table[pl.ds(56, 8), :] = jnp.zeros((8, 512), jnp.float32)
    flux[...] = jnp.zeros((64, 768), jnp.float32)
    held_bound[...] = jnp.ones((1, 128), jnp.float32)
    side_row[...] = jnp.zeros((1, 128), jnp.float32)
    work[...] = jnp.zeros((24, 128), jnp.float32)
    hessenberg[...] = jnp.zeros((2, kept + 2), jnp.float32)
    loads[1].wait()
    for load in loads[2:]:
        load.start()
    for component in range(6):
        vector[component] = stored[component, :, kept - 1, :]

    def step(turn, carry):
        first_step = turn == 0
        sums = sums_b.at[turn]

        def ready():
            @pl.when(first_step)
            def _():
                for load in loads[2:]:
                    load.wait()
                constants[...] = constants_wide[...].astype(jnp.bfloat16)

        def beside():
            @pl.when(first_step)
            def _():
                for face in range(4):
                    named = source[pl.ds(face, 1), :]
                    index_in[pl.ds(face, 1), :] = jnp.where(
                        named >= 512 + 4 * 64, named - 64, named
                    )
                fill_gram()
                packed = (
                    gram[pl.ds(0, 8), :]
                    + pltpu.roll(gram[pl.ds(8, 8), :], 32, 1)
                    + pltpu.roll(gram[pl.ds(16, 8), :], 64, 1)
                )
                begin(packed, sums_a, broad, 2, 0)

            @pl.when(jnp.logical_not(first_step))
            def _():
                side_row[...] = pltpu.roll(inner(vector, (vector, vector)), 32, 1)

        def greeting():
            @pl.when(first_step)
            def _():
                pl.semaphore_wait(barrier, len(greeted))

        prepare(turn, greeting)
        apply(turn, ready, beside)

        row = inner(image, (vector, image), (image, image))
        begin(row + side_row[...], sums, narrow, turn, 0)

        @pl.when(first_step)
        def _():
            begin(finish(sums_a, broad, 2, 0), sums_a, broad, 2, 1)

        begin(finish(sums, narrow, turn, 0), sums, narrow, turn, 1)

        @pl.when(first_step)
        def _():
            begin(finish(sums_a, broad, 2, 1), sums_a, broad, 2, 2)
            packed = finish(sums_a, broad, 2, 2) * (1.0 / total)
            products = jnp.concatenate(
                [packed, pltpu.roll(packed, 96, 1), pltpu.roll(packed, 64, 1)], axis=0
            )
            gram[...] = jnp.where(lane24 < 24, products, 0.0)

        products = gram[...]
        own = jnp.sum(jnp.where(eye, products, 0.0), axis=1, keepdims=True)
        message = finish(sums, narrow, turn, 1) * (1.0 / total)

        bound = held_bound[...][:, 0:1]
        row = jnp.where(lane1 < kept + turn, message, 0.0)
        side = jnp.where(lane1 < kept + 1, pltpu.roll(message, 96, 1), 0.0)
        square = jnp.sum(jnp.where(lane1 == kept + 1, message, 0.0), keepdims=True)
        length = jnp.sum(jnp.where(lane1 == kept, side, 0.0), keepdims=True)
        height = jnp.sqrt(length * (bound * bound) + 1e-06)
        grow = jnp.where(first_step, 1.0, bound / height)
        side = side * jnp.where(lane1 == kept, grow * grow, grow)
        row = row * jnp.where(lane1 == kept, grow * grow, grow)
        extended = kept + turn - 1
        products = jnp.where((lane24 == kept) & (extended == kept), to_column(side), products)
        products = jnp.where((sub24 == kept) & (extended == kept), side, products)
        column = jnp.sum((jnp.where(eye, 2.0, 0.0) - products) * row, axis=1, keepdims=True)
        column_row = to_row(column)

        @pl.when(jnp.logical_not(first_step))
        def _():
            before = hessenberg[pl.ds(0, 1), :]
            hessenberg[pl.ds(0, 1), :] = jnp.where(
                lane1[:, 0:24] == kept, height, before
            )

        square = square * (grow * grow)
        length = square + jnp.sum(
            column * (products * column_row - jnp.where(eye, 2.0, 0.0) * row), keepdims=True
        )
        height = jnp.sqrt(jnp.maximum(length, 0.0) + 1e-06)
        bound = jnp.sum(jnp.abs(column) * jnp.sqrt(own), keepdims=True) + jnp.sqrt(square) + 1e-3
        held_bound[...] = jnp.broadcast_to(bound, (1, 128))
        shrink = 1.0 / jnp.where(first_step, bound, height)
        project(column)
        on_own = column[kept : kept + 1] * grow
        for component in range(6):
            current = vector[component]
            new = (image[component] * grow - current * on_own - taken[component]) * shrink
            fresh[0, component] = current * grow
            fresh[1, component] = new
            vector[component] = new
        hessenberg[pl.ds(turn, 1), :] = jnp.where(
            lane1 == kept + 1, jnp.where(first_step, 0.0, height), column_row
        )[:, 0:24]
        return carry

    lax.fori_loop(0, 2, step, 0)
    for turn in range(2):
        pltpu.make_async_copy(outgoing.at[turn], outgoing.at[turn], halo_send.at[turn]).wait()
    for which in range(3):
        for stage, (size, _, _) in enumerate(broad if which == 2 else narrow):
            if size > 1:
                buffer = sums_a if which == 2 else sums_b.at[which]
                others = buffer.at[stage, pl.ds(0, size - 1)]
                pltpu.make_async_copy(others, others, sum_send.at[which, stage]).wait()


def body(
    n_gx,
    n_gy,
    basis,
    geometry,
    face_normals,
    face_scale,
    material,
    send_list,
    neighbour_source,
    node_rotation,
    boundary_flag,
):
    kept, components, nodes, local_count = basis.shape
    total = float(components * nodes * local_count * n_gx * n_gy)
    f32, bf16 = jnp.float32, jnp.bfloat16
    anywhere = pl.BlockSpec(memory_space=pl.ANY)
    vmem = pl.BlockSpec(memory_space=pltpu.VMEM)
    return pl.pallas_call(
        functools.partial(kernel, (n_gx, n_gy, total, element_tables()[2])),
        out_shape=(
            pltpu.VMEM((2, components, nodes, local_count), f32),
            pltpu.VMEM((2, kept + 2), f32),
        ),
        in_specs=[anywhere] * 10,
        out_specs=(vmem, vmem),
        scratch_shapes=[
            pltpu.VMEM((components, nodes, kept, local_count), f32),
            pltpu.VMEM(geometry.shape, f32),
            pltpu.VMEM(face_normals.shape, f32),
            pltpu.VMEM(face_scale.shape, f32),
            pltpu.VMEM(material.shape, f32),
            pltpu.VMEM(send_list.shape, jnp.int32),
            pltpu.VMEM(neighbour_source.shape, jnp.int32),
            pltpu.VMEM(node_rotation.shape, jnp.int32),
            pltpu.VMEM(boundary_flag.shape, jnp.int32),
            pltpu.VMEM((304, 256), f32),
            pltpu.VMEM((304, 256), bf16),
            pltpu.VMEM((components, nodes, local_count), f32),
            pltpu.VMEM((32, 768), f32),
            pltpu.VMEM((80, 768), f32),
            pltpu.VMEM((64, 512), f32),
            pltpu.VMEM((64, 512), f32),
            pltpu.VMEM((192, 512), f32),
            pltpu.VMEM((components, nodes, local_count), f32),
            pltpu.VMEM((64, 768), f32),
            pltpu.VMEM((4, 128), jnp.int32),
            pltpu.VMEM((4, 128), jnp.int32),
            pltpu.VMEM((24, 128), f32),
            pltpu.VMEM((1, 128), f32),
            pltpu.VMEM((1, 128), f32),
            pltpu.VMEM((24, 128), f32),
            pltpu.VMEM((components, 8 * nodes, local_count), f32),
            pltpu.VMEM((components, nodes, local_count), f32),
            pltpu.VMEM((2, 8, 32, 128), f32),
            pltpu.VMEM((2, 8, 32, 128), f32),
            pltpu.VMEM((3, max(n_gx // X_CHIPS, n_gy, X_CHIPS), 8, 128), f32),
            pltpu.VMEM((2, 2, max(n_gx, n_gy), 1, 128), f32),
            pltpu.SemaphoreType.DMA((12,)),
            pltpu.SemaphoreType.DMA((2,)),
            pltpu.SemaphoreType.DMA((2,)),
            pltpu.SemaphoreType.DMA((3, 3)),
            pltpu.SemaphoreType.DMA((3, 3)),
        ],
        compiler_params=pltpu.CompilerParams(
            collective_id=0, has_side_effects=True, vmem_limit_bytes=32 * 1024 * 1024
        ),
    )(
        *[
            pltpu.with_memory_space_constraint(operand, pltpu.HBM)
            for operand in (
                jnp.transpose(basis, (1, 2, 0, 3)),
                geometry,
                face_normals,
                face_scale,
                material,
                send_list,
                neighbour_source,
                node_rotation,
                boundary_flag,
                left_operands(),
            )
        ]
    )


def solution(mesh):
    placed = (
        P(None, None, None, ("gx", "gy")),
        P(None, ("gx", "gy")),
        P(None, None, ("gx", "gy")),
        P(None, ("gx", "gy")),
        P(None, ("gx", "gy")),
        P("gx", "gy", None),
        P(None, ("gx", "gy")),
        P(None, ("gx", "gy")),
        P(None, ("gx", "gy")),
    )
    return jax.shard_map(
        functools.partial(body, mesh.shape["gx"], mesh.shape["gy"]),
        mesh=mesh,
        in_specs=placed,
        out_specs=(P(None, None, None, ("gx", "gy")), P()),
        check_vma=False,
    )
```

```python
import functools
import math

import jax
import jax.numpy as jnp
import numpy as np
from jax import lax
from jax.experimental import pallas as pl
from jax.experimental.pallas import tpu as pltpu
from jax.sharding import PartitionSpec as P

MESH = pl.DeviceIdType.MESH
OPERANDS = (0, 80, 112)
DIRECTIONS = (0, 1, 2, 3, 5, 6, 7, 8)


def invert(matrix):
    dimension = len(matrix)
    augmented = []
    for row_index in range(dimension):
        augmented.append(
            [float(matrix[row_index][column]) for column in range(dimension)]
            + [1.0 if column == row_index else 0.0 for column in range(dimension)]
        )
    for column in range(dimension):
        pivot_row = column
        for row_index in range(column + 1, dimension):
            if abs(augmented[row_index][column]) > abs(augmented[pivot_row][column]):
                pivot_row = row_index
        augmented[column], augmented[pivot_row] = (augmented[pivot_row], augmented[column])
        leading = augmented[column][column]
        augmented[column] = [value / leading for value in augmented[column]]
        for row_index in range(dimension):
            if row_index != column:
                factor = augmented[row_index][column]
                augmented[row_index] = [
                    left - factor * right
                    for left, right in zip(augmented[row_index], augmented[column])
                ]
    return np.array([entries[dimension:] for entries in augmented])


def locate(face, first, second):
    if face == 0:
        return (first, second, 0)
    if face == 1:
        return (first, 0, second)
    if face == 2:
        return (3 - first - second, first, second)
    return (0, first, second)


def element_tables():
    nodes = [(i, j, k) for k in range(4) for j in range(4) for i in range(4) if i + j + k <= 3]
    points = np.array(nodes) / 3.0
    vander = np.zeros((20, 20))
    slopes = np.zeros((3, 20, 20))
    for row in range(20):
        for column in range(20):
            powers = np.array(nodes[column])
            vander[row, column] = np.prod(points[row] ** powers)
            for axis in range(3):
                if powers[axis] > 0:
                    lowered = powers.copy()
                    lowered[axis] -= 1
                    slopes[axis, row, column] = powers[axis] * np.prod(points[row] ** lowered)
    inverse = invert(vander)
    derivs = np.stack([slopes[axis] @ inverse for axis in range(3)])
    moments = np.zeros((20, 20))
    for row in range(20):
        for column in range(20):
            left = nodes[row]
            right = nodes[column]
            sums = [left[0] + right[0], left[1] + right[1], left[2] + right[2]]
            moments[row, column] = (
                math.factorial(sums[0])
                * math.factorial(sums[1])
                * math.factorial(sums[2])
                / math.factorial(sum(sums) + 3)
            )
    mass = inverse.T @ moments @ inverse
    lattice = [(first, second) for second in range(4) for first in range(4) if first + second <= 3]
    face_nodes = np.array(
        [[nodes.index(locate(face, pair[0], pair[1])) for face in range(4)] for pair in lattice]
    )
    plane = np.array(
        [
            [(pair[0] / 3.0) ** expo[0] * (pair[1] / 3.0) ** expo[1] for expo in lattice]
            for pair in lattice
        ]
    )
    plane_inverse = invert(plane)
    plane_moments = np.zeros((10, 10))
    for row in range(10):
        for column in range(10):
            first = lattice[row][0] + lattice[column][0]
            second = lattice[row][1] + lattice[column][1]
            plane_moments[row, column] = (
                math.factorial(first) * math.factorial(second) / math.factorial(first + second + 2)
            )
    face_mass = plane_inverse.T @ plane_moments @ plane_inverse
    edges = np.zeros((20, 40))
    for face in range(4):
        for row in range(10):
            for column in range(10):
                edges[face_nodes[row, face], column * 4 + face] += face_mass[row, column]
    lift = invert(mass) @ edges
    turned = np.array([lattice.index((pair[1], 3 - pair[0] - pair[1])) for pair in lattice])
    rotations = np.stack([np.arange(10), turned, turned[turned]])
    return (derivs, lift, face_nodes, rotations)


def bf16_parts(values):
    values = np.asarray(values, np.float32)
    high = values.astype(jnp.bfloat16)
    rest = values - high.astype(np.float32)
    middle = rest.astype(jnp.bfloat16)
    low = (rest - middle.astype(np.float32)).astype(jnp.bfloat16)
    return high, middle, low


def packed_row(component, node):
    return 8 * component + node if node < 8 else 48 + 2 * component + node - 8


def left_operands():
    derivs, lift, face_nodes, rotations = element_tables()
    stack = np.zeros((3, 80, 32), np.float32)
    for index, part in enumerate(bf16_parts(derivs)):
        for axis in range(3):
            stack[index, 24 * axis : 24 * axis + 20, :20] = part[axis].astype(np.float32)
    high, middle, low = stack
    volume = np.concatenate([high, high, high, middle, low, middle], axis=1)
    blocks = np.zeros((3, 32, 64), np.float32)
    for index, part in enumerate(bf16_parts(lift)):
        for face in range(4):
            for node in range(10):
                blocks[index, :20, 16 * face + node] = part[:, node * 4 + face].astype(np.float32)
    raise_up = np.concatenate([blocks[0], blocks[1], blocks[0], blocks[0]], axis=1)
    spread = np.zeros((192, 64), np.float32)
    for turn in range(3):
        for component in range(6):
            for node in range(10):
                spread[
                    64 * turn + packed_row(component, node),
                    packed_row(component, rotations[turn][node]),
                ] = 1.0
    turned = np.concatenate([spread, spread, spread], axis=1)
    packed = np.zeros((304, 256), np.float32)
    for place, matrix in zip(OPERANDS, (volume, raise_up, turned)):
        packed[place : place + matrix.shape[0], : matrix.shape[1]] = matrix
    return jnp.asarray(packed)


def split(values):
    high = values.astype(jnp.bfloat16)
    rest = values - high.astype(jnp.float32)
    middle = rest.astype(jnp.bfloat16)
    low = (rest - middle.astype(jnp.float32)).astype(jnp.bfloat16)
    return high, middle, low


def iota(shape, axis):
    return lax.broadcasted_iota(jnp.int32, shape, axis)


def dot(left, right):
    return jnp.dot(left, right, preferred_element_type=jnp.float32)


def kernel(
    sizes,
    basis_hbm,
    geometry_hbm,
    normals_hbm,
    scale_hbm,
    material_hbm,
    send_list_hbm,
    source_hbm,
    turns_hbm,
    flags_hbm,
    constants_hbm,
    fresh,
    hessenberg,
    stored,
    geometry,
    normals,
    scale,
    material,
    send_list,
    source,
    turns,
    flags,
    constants_wide,
    constants,
    vector,
    field,
    around,
    table,
    others,
    rotated,
    image,
    flux,
    index_out,
    index_in,
    gram,
    held_bound,
    side_row,
    work,
    spread,
    taken,
    outgoing,
    arrived,
    sums_a,
    sums_b,
    load_sem,
    halo_send,
    halo_recv,
    sum_send,
    sum_recv,
):
    n_gx, n_gy, total, face_nodes = sizes
    kept = basis_hbm.shape[2]
    gx = lax.axis_index("gx")
    gy = lax.axis_index("gy")
    last = kept // 8 * 8
    block = (slice(None), slice(None), pl.ds(last, kept - last))
    rest = (slice(None), slice(None), pl.ds(0, last))
    loads = []
    for source_ref, target_ref in (
        (send_list_hbm, send_list),
        (basis_hbm.at[block], stored.at[block]),
        (constants_hbm, constants_wide),
        (basis_hbm.at[rest], stored.at[rest]),
        (source_hbm, source),
        (turns_hbm, turns),
        (flags_hbm, flags),
        (geometry_hbm, geometry),
        (normals_hbm, normals),
        (scale_hbm, scale),
        (material_hbm, material),
    ):
        loads.append(pltpu.make_async_copy(source_ref, target_ref, load_sem.at[len(loads)]))
    for load in loads[:2]:
        load.start()

    def turned_on(place, step, size):
        place = place + step
        return jnp.where(place >= size, place - size, place)

    partners = []
    for direction in DIRECTIONS:
        partners.append(
            (
                turned_on(gx, (direction // 3 - 1) % n_gx, n_gx),
                turned_on(gy, (direction % 3 - 1) % n_gy, n_gy),
            )
        )

    def farthest_first(size):
        return sorted(range(1, size), key=lambda step: -min(step, size - step))

    on_gy = (n_gy, gy, [(gx, turned_on(gy, step, n_gy)) for step in farthest_first(n_gy)])
    on_gx = (n_gx, gx, [(turned_on(gx, step, n_gx), gy) for step in farthest_first(n_gx)])
    groups = (on_gy, on_gx)

    barrier = pltpu.get_barrier_semaphore()
    greeted = list(partners)
    greeted += [(gx, turned_on(gy, step, n_gy)) for step in range(2, n_gy - 1)]
    greeted += [(turned_on(gx, step, n_gx), gy) for step in range(2, n_gx - 1)]
    for peer in greeted:
        pl.semaphore_signal(barrier, inc=1, device_id=peer, device_id_type=MESH)

    loads[0].wait()
    for tile in range(4):
        first, second = DIRECTIONS[2 * tile], DIRECTIONS[2 * tile + 1]
        index_out[pl.ds(tile, 1), :] = jnp.concatenate(
            [
                send_list[first // 3, pl.ds(first % 3, 1), :],
                send_list[second // 3, pl.ds(second % 3, 1), :],
            ],
            axis=1,
        )

    def pick(found, sources, index, first):
        lane = jnp.broadcast_to(jnp.bitwise_and(index, 127), (64, 128))
        tile = jnp.broadcast_to(jnp.right_shift(index, 7), (64, 128))
        for place, values in enumerate(sources):
            picked = jnp.take_along_axis(values, lane, axis=1, mode="promise_in_bounds")
            found = picked if found is None else jnp.where(tile == first + place, picked, found)
        return found

    half = iota((32, 128), 1) < 64

    def prepare(turn, greeting):
        for component in range(6):
            for face in range(4):
                for node in range(10):
                    row = pl.ds(packed_row(component, node), 1)
                    table[row, pl.ds(128 * face, 128)] = vector[
                        component, pl.ds(int(face_nodes[node, face]), 1), :
                    ]
        greeting()
        sources = [table[:, pl.ds(128 * tile, 128)] for tile in range(4)]
        for tile in (0, 3, 1, 2):
            sent = pick(None, sources, index_out[pl.ds(tile, 1), :], 0)
            top = sent[0:32]
            bottom = sent[32:64]
            outgoing[turn, 2 * tile] = jnp.where(half, top, pltpu.roll(bottom, 64, 1))
            outgoing[turn, 2 * tile + 1] = jnp.where(half, pltpu.roll(top, 64, 1), bottom)
            for index in (2 * tile, 2 * tile + 1):
                pltpu.make_async_remote_copy(
                    src_ref=outgoing.at[turn, index],
                    dst_ref=arrived.at[turn, 7 - index],
                    send_sem=halo_send.at[turn],
                    recv_sem=halo_recv.at[turn],
                    device_id=partners[index],
                    device_id_type=MESH,
                ).start()

    def apply(turn, ready, beside):
        ready()
        for component in range(6):
            field[pl.ds(0, 20), pl.ds(128 * component, 128)] = vector[component]
        high, middle, low = split(field[...])
        around[...] = dot(
            constants[pl.ds(0, 80), pl.ds(0, 192)],
            jnp.concatenate([high, middle, low, high, high, middle], axis=0)
        )

        def gradient(axis, component):
            column = pl.ds(128 * component, 128)
            return (
                around[pl.ds(0, 20), column] * geometry[pl.ds(axis, 1), :]
                + around[pl.ds(24, 20), column] * geometry[pl.ds(3 + axis, 1), :]
                + around[pl.ds(48, 20), column] * geometry[pl.ds(6 + axis, 1), :]
            )

        for component in range(3):
            after, before = (component + 1) % 3, (component + 2) % 3
            curl_e = gradient(after, before) - gradient(before, after)
            curl_h = gradient(after, 3 + before) - gradient(before, 3 + after)
            image[component] = (
                material[pl.ds(0, 1), :] * curl_h - material[pl.ds(2, 1), :] * vector[component]
            )
            image[3 + component] = -material[pl.ds(1, 1), :] * curl_e
        beside()
        sources = [table[:, pl.ds(128 * tile, 128)] for tile in range(4)]
        for face in range(4):
            lane = pl.ds(128 * face, 128)
            others[:, lane] = pick(None, sources, index_in[pl.ds(face, 1), :], 0)
        pltpu.make_async_copy(arrived.at[turn], arrived.at[turn], halo_recv.at[turn]).wait()
        sources = []
        for tile in range(4):
            even = arrived[turn, 2 * tile]
            odd = arrived[turn, 2 * tile + 1]
            sources.append(
                jnp.concatenate(
                    [
                        jnp.where(half, even, pltpu.roll(odd, 64, 1)),
                        jnp.where(half, pltpu.roll(even, 64, 1), odd),
                    ],
                    axis=0,
                )
            )
        found = jnp.concatenate(
            [
                pick(
                    others[:, pl.ds(128 * face, 128)], sources, index_in[pl.ds(face, 1), :], 4
                )
                for face in range(4)
            ],
            axis=1,
        )
        rotated[...] = dot(
            constants[pl.ds(112, 192), pl.ds(0, 192)], jnp.concatenate(split(found), axis=0)
        )
        for face in range(4):
            lane = pl.ds(128 * face, 128)
            spin = turns[pl.ds(face, 1), :]
            wall = flags[pl.ds(face, 1), :] == 1
            weight = 0.5 * scale[pl.ds(face, 1), :]
            n_x = normals[0, pl.ds(face, 1), :]
            n_y = normals[1, pl.ds(face, 1), :]
            n_z = normals[2, pl.ds(face, 1), :]
            for first_node, count in ((0, 8), (8, 2)):
                jumps = []
                for component in range(6):
                    row = packed_row(component, first_node)
                    here = table[pl.ds(row, count), lane]
                    other = jnp.where(
                        spin == 0,
                        rotated[pl.ds(row, count), lane],
                        jnp.where(
                            spin == 1,
                            rotated[pl.ds(64 + row, count), lane],
                            rotated[pl.ds(128 + row, count), lane],
                        ),
                    )
                    other = jnp.where(wall, -here if component < 3 else here, other)
                    jumps.append(other - here)
                e_x, e_y, e_z, h_x, h_y, h_z = jumps
                along_e = n_x * e_x + n_y * e_y + n_z * e_z
                along_h = n_x * h_x + n_y * h_y + n_z * h_z
                terms = [
                    n_y * h_z - n_z * h_y + e_x - along_e * n_x,
                    n_z * h_x - n_x * h_z + e_y - along_e * n_y,
                    n_x * h_y - n_y * h_x + e_z - along_e * n_z,
                    n_z * e_y - n_y * e_z + h_x - along_h * n_x,
                    n_x * e_z - n_z * e_x + h_y - along_h * n_y,
                    n_y * e_x - n_x * e_y + h_z - along_h * n_z,
                ]
                for component in range(6):
                    place = pl.ds(16 * face + first_node, count)
                    flux[place, pl.ds(128 * component, 128)] = terms[component] * weight
        high, middle, low = split(flux[...])
        lifted = dot(constants[pl.ds(80, 32), :], jnp.concatenate([high, high, middle, low], axis=0))
        for component in range(6):
            raised = lifted[0:20, 128 * component : 128 * component + 128]
            image[component] += material[pl.ds(component // 3, 1), :] * raised

    sub8 = iota((8, 128), 0)
    sub24 = iota((24, 128), 0)
    lane24 = iota((24, 128), 1)
    lane1 = iota((1, 128), 1)
    eye = sub24 == lane24

    def inner(vector_ref, *pairs):
        def some(component, held):
            held = list(held)
            for node in range(20):
                held[node % 3] += (
                    stored[component, node] * vector_ref[component, pl.ds(node, 1), :]
                )
            return tuple(held)

        zero = jnp.zeros((kept, 128), jnp.float32)
        for place, (left, right) in enumerate(pairs):
            partial = jnp.sum(left[...] * right[...], axis=0)
            work[pl.ds(kept + place, 1), :] = jnp.sum(partial, axis=0, keepdims=True)
        one, two, three = lax.fori_loop(0, 6, some, (zero, zero, zero))
        work[pl.ds(0, kept), :] = one + two + three
        return to_row(jnp.sum(work[...], axis=1, keepdims=True))

    def to_row(column):
        return jnp.sum(jnp.where(eye, column, 0.0), axis=0, keepdims=True)

    def to_column(row):
        return jnp.sum(jnp.where(eye, row, 0.0), axis=1, keepdims=True)

    def fill_gram():
        def upper(node, held):
            held = list(held)
            for component in range(6):
                tile = stored[component, node]
                for index in range(8):
                    held[index] += tile * stored[component, node, pl.ds(index, 1), :]
            return tuple(held)

        def lower(node, held):
            held = list(held)
            for component in range(6):
                tile = stored[component, node, pl.ds(8, kept - 8), :]
                for index in range(8, 16):
                    held[index - 8] += tile * stored[component, node, pl.ds(index, 1), :]
                tile = tile[8:]
                for index in range(16, kept):
                    held[index - 8] += tile * stored[component, node, pl.ds(index, 1), :]
            return tuple(held)

        def zeros(count, number):
            return (jnp.zeros((count, 128), jnp.float32),) * number

        found = list(lax.fori_loop(0, 20, upper, zeros(kept, 8)))
        found += lax.fori_loop(
            0, 20, lower, zeros(kept - 8, 8) + zeros(kept - 16, kept - 16)
        )
        gram[...] = jnp.zeros((24, 128), jnp.float32)
        for first in (0, 8, 16):
            count = kept - first
            sub = iota((count, 128), 0)
            lane = iota((count, 128), 1)
            held = jnp.zeros((count, 128), jnp.float32)
            for index in range(first, min(first + 8, kept)):
                column = jnp.sum(found[index], axis=1, keepdims=True)
                held = jnp.where(lane == index, column, held)
                row = jnp.sum(jnp.where(sub + first == lane, column, 0.0), axis=0, keepdims=True)
                held = jnp.where((sub == index - first) & (lane >= first), row, held)
            if first == 0:
                gram[pl.ds(0, kept), :] = held
            else:
                old = gram[pl.ds(first, count), :]
                gram[pl.ds(first, count), :] = jnp.where(lane >= first, held, old)

    def begin(value, buffer, which, stage):
        size, mine, peers = groups[stage]
        buffer[stage, mine] = value
        for peer in peers:
            pltpu.make_async_remote_copy(
                src_ref=buffer.at[stage, mine],
                dst_ref=buffer.at[stage, mine],
                send_sem=sum_send.at[which, stage],
                recv_sem=sum_recv.at[which, stage],
                device_id=peer,
                device_id_type=MESH,
            ).start()

    def finish(buffer, which, stage):
        size, mine, peers = groups[stage]
        if size > 1:
            others = buffer.at[stage, pl.ds(0, size - 1)]
            pltpu.make_async_copy(others, others, sum_recv.at[which, stage]).wait()
        values = [buffer[stage, member] for member in range(size)]
        while len(values) > 1:
            values = [sum(values[at : at + 2]) for at in range(0, len(values), 2)]
        return values[0]

    def project(column):
        weights = jnp.broadcast_to(column[0:kept], (kept, 128))

        def one(component, carry):
            for node in range(20):
                product = stored[component, node] * weights
                short = jnp.concatenate(
                    [product[16:kept], jnp.zeros((24 - kept, 128), jnp.float32)], axis=0
                )
                spread[component, pl.ds(8 * node, 8), :] = product[0:8] + product[8:16] + short
            return carry

        lax.fori_loop(0, 6, one, 0)
        for component in range(6):
            parts_of = [spread[component, pl.ds(at, 20, stride=8), :] for at in range(8)]
            while len(parts_of) > 1:
                parts_of = [sum(parts_of[at : at + 2]) for at in range(0, len(parts_of), 2)]
            taken[component] = parts_of[0]

    field[pl.ds(16, 16), :] = jnp.zeros((16, 768), jnp.float32)
    table[pl.ds(56, 8), :] = jnp.zeros((8, 512), jnp.float32)
    flux[...] = jnp.zeros((64, 768), jnp.float32)
    held_bound[...] = jnp.ones((1, 128), jnp.float32)
    side_row[...] = jnp.zeros((1, 128), jnp.float32)
    work[...] = jnp.zeros((24, 128), jnp.float32)
    hessenberg[...] = jnp.zeros((2, kept + 2), jnp.float32)
    loads[1].wait()
    for load in loads[2:]:
        load.start()
    for component in range(6):
        vector[component] = stored[component, :, kept - 1, :]

    def step(turn, carry):
        first_step = turn == 0
        sums = sums_b.at[turn]

        def ready():
            @pl.when(first_step)
            def _():
                for load in loads[2:]:
                    load.wait()
                constants[...] = constants_wide[...].astype(jnp.bfloat16)

        def beside():
            @pl.when(first_step)
            def _():
                for face in range(4):
                    named = source[pl.ds(face, 1), :]
                    index_in[pl.ds(face, 1), :] = jnp.where(
                        named >= 512 + 4 * 64, named - 64, named
                    )
                fill_gram()
                packed = (
                    gram[pl.ds(0, 8), :]
                    + pltpu.roll(gram[pl.ds(8, 8), :], 32, 1)
                    + pltpu.roll(gram[pl.ds(16, 8), :], 64, 1)
                )
                begin(packed, sums_a, 2, 0)

            @pl.when(jnp.logical_not(first_step))
            def _():
                side_row[...] = pltpu.roll(inner(vector, (vector, vector)), 32, 1)

        def greeting():
            @pl.when(first_step)
            def _():
                pl.semaphore_wait(barrier, len(greeted))

        prepare(turn, greeting)
        apply(turn, ready, beside)

        row = inner(image, (vector, image), (image, image))
        begin(row + side_row[...], sums, turn, 0)

        @pl.when(first_step)
        def _():
            begin(finish(sums_a, 2, 0), sums_a, 2, 1)

        begin(finish(sums, turn, 0), sums, turn, 1)

        @pl.when(first_step)
        def _():
            packed = finish(sums_a, 2, 1) * (1.0 / total)
            products = jnp.concatenate(
                [packed, pltpu.roll(packed, 96, 1), pltpu.roll(packed, 64, 1)], axis=0
            )
            gram[...] = jnp.where(lane24 < 24, products, 0.0)

        products = gram[...]
        own = jnp.sum(jnp.where(eye, products, 0.0), axis=1, keepdims=True)
        message = finish(sums, turn, 1) * (1.0 / total)

        bound = held_bound[...][:, 0:1]
        row = jnp.where(lane1 < kept + turn, message, 0.0)
        side = jnp.where(lane1 < kept + 1, pltpu.roll(message, 96, 1), 0.0)
        square = jnp.sum(jnp.where(lane1 == kept + 1, message, 0.0), keepdims=True)
        length = jnp.sum(jnp.where(lane1 == kept, side, 0.0), keepdims=True)
        height = jnp.sqrt(length * (bound * bound) + 1e-06)
        grow = jnp.where(first_step, 1.0, bound / height)
        side = side * jnp.where(lane1 == kept, grow * grow, grow)
        row = row * jnp.where(lane1 == kept, grow * grow, grow)
        extended = kept + turn - 1
        products = jnp.where((lane24 == kept) & (extended == kept), to_column(side), products)
        products = jnp.where((sub24 == kept) & (extended == kept), side, products)
        column = jnp.sum((jnp.where(eye, 2.0, 0.0) - products) * row, axis=1, keepdims=True)
        column_row = to_row(column)

        @pl.when(jnp.logical_not(first_step))
        def _():
            before = hessenberg[pl.ds(0, 1), :]
            hessenberg[pl.ds(0, 1), :] = jnp.where(
                lane1[:, 0:24] == kept, height, before
            )

        square = square * (grow * grow)
        length = square + jnp.sum(
            column * (products * column_row - jnp.where(eye, 2.0, 0.0) * row), keepdims=True
        )
        height = jnp.sqrt(jnp.maximum(length, 0.0) + 1e-06)
        bound = jnp.sum(jnp.abs(column) * jnp.sqrt(own), keepdims=True) + jnp.sqrt(square) + 1e-3
        held_bound[...] = jnp.broadcast_to(bound, (1, 128))
        shrink = 1.0 / jnp.where(first_step, bound, height)
        project(column)
        on_own = column[kept : kept + 1] * grow
        for component in range(6):
            current = vector[component]
            new = (image[component] * grow - current * on_own - taken[component]) * shrink
            fresh[0, component] = current * grow
            fresh[1, component] = new
            vector[component] = new
        hessenberg[pl.ds(turn, 1), :] = jnp.where(
            lane1 == kept + 1, jnp.where(first_step, 0.0, height), column_row
        )[:, 0:24]
        return carry

    lax.fori_loop(0, 2, step, 0)
    for turn in range(2):
        pltpu.make_async_copy(outgoing.at[turn], outgoing.at[turn], halo_send.at[turn]).wait()
    for which in range(3):
        for stage, (size, _, _) in enumerate(groups):
            if size > 1:
                buffer = sums_a if which == 2 else sums_b.at[which]
                others = buffer.at[stage, pl.ds(0, size - 1)]
                pltpu.make_async_copy(others, others, sum_send.at[which, stage]).wait()


def body(
    n_gx,
    n_gy,
    basis,
    geometry,
    face_normals,
    face_scale,
    material,
    send_list,
    neighbour_source,
    node_rotation,
    boundary_flag,
):
    kept, components, nodes, local_count = basis.shape
    total = float(components * nodes * local_count * n_gx * n_gy)
    f32, bf16 = jnp.float32, jnp.bfloat16
    anywhere = pl.BlockSpec(memory_space=pl.ANY)
    vmem = pl.BlockSpec(memory_space=pltpu.VMEM)
    return pl.pallas_call(
        functools.partial(kernel, (n_gx, n_gy, total, element_tables()[2])),
        out_shape=(
            pltpu.VMEM((2, components, nodes, local_count), f32),
            pltpu.VMEM((2, kept + 2), f32),
        ),
        in_specs=[anywhere] * 10,
        out_specs=(vmem, vmem),
        scratch_shapes=[
            pltpu.VMEM((components, nodes, kept, local_count), f32),
            pltpu.VMEM(geometry.shape, f32),
            pltpu.VMEM(face_normals.shape, f32),
            pltpu.VMEM(face_scale.shape, f32),
            pltpu.VMEM(material.shape, f32),
            pltpu.VMEM(send_list.shape, jnp.int32),
            pltpu.VMEM(neighbour_source.shape, jnp.int32),
            pltpu.VMEM(node_rotation.shape, jnp.int32),
            pltpu.VMEM(boundary_flag.shape, jnp.int32),
            pltpu.VMEM((304, 256), f32),
            pltpu.VMEM((304, 256), bf16),
            pltpu.VMEM((components, nodes, local_count), f32),
            pltpu.VMEM((32, 768), f32),
            pltpu.VMEM((80, 768), f32),
            pltpu.VMEM((64, 512), f32),
            pltpu.VMEM((64, 512), f32),
            pltpu.VMEM((192, 512), f32),
            pltpu.VMEM((components, nodes, local_count), f32),
            pltpu.VMEM((64, 768), f32),
            pltpu.VMEM((4, 128), jnp.int32),
            pltpu.VMEM((4, 128), jnp.int32),
            pltpu.VMEM((24, 128), f32),
            pltpu.VMEM((1, 128), f32),
            pltpu.VMEM((1, 128), f32),
            pltpu.VMEM((24, 128), f32),
            pltpu.VMEM((components, 8 * nodes, local_count), f32),
            pltpu.VMEM((components, nodes, local_count), f32),
            pltpu.VMEM((2, 8, 32, 128), f32),
            pltpu.VMEM((2, 8, 32, 128), f32),
            pltpu.VMEM((2, max(n_gx, n_gy), 8, 128), f32),
            pltpu.VMEM((2, 2, max(n_gx, n_gy), 1, 128), f32),
            pltpu.SemaphoreType.DMA((12,)),
            pltpu.SemaphoreType.DMA((2,)),
            pltpu.SemaphoreType.DMA((2,)),
            pltpu.SemaphoreType.DMA((3, 3)),
            pltpu.SemaphoreType.DMA((3, 3)),
        ],
        compiler_params=pltpu.CompilerParams(
            collective_id=0, has_side_effects=True, vmem_limit_bytes=32 * 1024 * 1024
        ),
    )(
        *[
            pltpu.with_memory_space_constraint(operand, pltpu.HBM)
            for operand in (
                jnp.transpose(basis, (1, 2, 0, 3)),
                geometry,
                face_normals,
                face_scale,
                material,
                send_list,
                neighbour_source,
                node_rotation,
                boundary_flag,
                left_operands(),
            )
        ]
    )


def solution(mesh):
    placed = (
        P(None, None, None, ("gx", "gy")),
        P(None, ("gx", "gy")),
        P(None, None, ("gx", "gy")),
        P(None, ("gx", "gy")),
        P(None, ("gx", "gy")),
        P("gx", "gy", None),
        P(None, ("gx", "gy")),
        P(None, ("gx", "gy")),
        P(None, ("gx", "gy")),
    )
    return jax.shard_map(
        functools.partial(body, mesh.shape["gx"], mesh.shape["gy"]),
        mesh=mesh,
        in_specs=placed,
        out_specs=(P(None, None, None, ("gx", "gy")), P()),
        check_vma=False,
    )
```

```python
import functools
import math

import jax
import jax.numpy as jnp
import numpy as np
from jax import lax
from jax.experimental import pallas as pl
from jax.experimental.pallas import tpu as pltpu
from jax.sharding import PartitionSpec as P

MESH = pl.DeviceIdType.MESH
X_CHIPS = 4
CORES = 2
OPERANDS = (0, 80, 112)
DIRECTIONS = (0, 1, 2, 3, 5, 6, 7, 8)


def invert(matrix):
    dimension = len(matrix)
    augmented = []
    for row_index in range(dimension):
        augmented.append(
            [float(matrix[row_index][column]) for column in range(dimension)]
            + [1.0 if column == row_index else 0.0 for column in range(dimension)]
        )
    for column in range(dimension):
        pivot_row = column
        for row_index in range(column + 1, dimension):
            if abs(augmented[row_index][column]) > abs(augmented[pivot_row][column]):
                pivot_row = row_index
        augmented[column], augmented[pivot_row] = (augmented[pivot_row], augmented[column])
        leading = augmented[column][column]
        augmented[column] = [value / leading for value in augmented[column]]
        for row_index in range(dimension):
            if row_index != column:
                factor = augmented[row_index][column]
                augmented[row_index] = [
                    left - factor * right
                    for left, right in zip(augmented[row_index], augmented[column])
                ]
    return np.array([entries[dimension:] for entries in augmented])


def locate(face, first, second):
    if face == 0:
        return (first, second, 0)
    if face == 1:
        return (first, 0, second)
    if face == 2:
        return (3 - first - second, first, second)
    return (0, first, second)


def element_tables():
    nodes = [(i, j, k) for k in range(4) for j in range(4) for i in range(4) if i + j + k <= 3]
    points = np.array(nodes) / 3.0
    vander = np.zeros((20, 20))
    slopes = np.zeros((3, 20, 20))
    for row in range(20):
        for column in range(20):
            powers = np.array(nodes[column])
            vander[row, column] = np.prod(points[row] ** powers)
            for axis in range(3):
                if powers[axis] > 0:
                    lowered = powers.copy()
                    lowered[axis] -= 1
                    slopes[axis, row, column] = powers[axis] * np.prod(points[row] ** lowered)
    inverse = invert(vander)
    derivs = np.stack([slopes[axis] @ inverse for axis in range(3)])
    moments = np.zeros((20, 20))
    for row in range(20):
        for column in range(20):
            left = nodes[row]
            right = nodes[column]
            sums = [left[0] + right[0], left[1] + right[1], left[2] + right[2]]
            moments[row, column] = (
                math.factorial(sums[0])
                * math.factorial(sums[1])
                * math.factorial(sums[2])
                / math.factorial(sum(sums) + 3)
            )
    mass = inverse.T @ moments @ inverse
    lattice = [(first, second) for second in range(4) for first in range(4) if first + second <= 3]
    face_nodes = np.array(
        [[nodes.index(locate(face, pair[0], pair[1])) for face in range(4)] for pair in lattice]
    )
    plane = np.array(
        [
            [(pair[0] / 3.0) ** expo[0] * (pair[1] / 3.0) ** expo[1] for expo in lattice]
            for pair in lattice
        ]
    )
    plane_inverse = invert(plane)
    plane_moments = np.zeros((10, 10))
    for row in range(10):
        for column in range(10):
            first = lattice[row][0] + lattice[column][0]
            second = lattice[row][1] + lattice[column][1]
            plane_moments[row, column] = (
                math.factorial(first) * math.factorial(second) / math.factorial(first + second + 2)
            )
    face_mass = plane_inverse.T @ plane_moments @ plane_inverse
    edges = np.zeros((20, 40))
    for face in range(4):
        for row in range(10):
            for column in range(10):
                edges[face_nodes[row, face], column * 4 + face] += face_mass[row, column]
    lift = invert(mass) @ edges
    turned = np.array([lattice.index((pair[1], 3 - pair[0] - pair[1])) for pair in lattice])
    rotations = np.stack([np.arange(10), turned, turned[turned]])
    return (derivs, lift, face_nodes, rotations)


def bf16_parts(values):
    values = np.asarray(values, np.float32)
    high = values.astype(jnp.bfloat16)
    rest = values - high.astype(np.float32)
    middle = rest.astype(jnp.bfloat16)
    low = (rest - middle.astype(np.float32)).astype(jnp.bfloat16)
    return high, middle, low


def packed_row(component, node):
    return 8 * component + node if node < 8 else 48 + 2 * component + node - 8


def left_operands():
    derivs, lift, face_nodes, rotations = element_tables()
    stack = np.zeros((3, 80, 32), np.float32)
    for index, part in enumerate(bf16_parts(derivs)):
        for axis in range(3):
            stack[index, 24 * axis : 24 * axis + 20, :20] = part[axis].astype(np.float32)
    high, middle, low = stack
    volume = np.concatenate([high, high, high, middle, low, middle], axis=1)
    blocks = np.zeros((3, 32, 64), np.float32)
    for index, part in enumerate(bf16_parts(lift)):
        for face in range(4):
            for node in range(10):
                blocks[index, :20, 16 * face + node] = part[:, node * 4 + face].astype(np.float32)
    raise_up = np.concatenate([blocks[0], blocks[1], blocks[0], blocks[0]], axis=1)
    spread = np.zeros((192, 64), np.float32)
    for turn in range(3):
        for component in range(6):
            for node in range(10):
                spread[
                    64 * turn + packed_row(component, node),
                    packed_row(component, rotations[turn][node]),
                ] = 1.0
    turned = np.concatenate([spread, spread, spread], axis=1)
    packed = np.zeros((304, 256), np.float32)
    for place, matrix in zip(OPERANDS, (volume, raise_up, turned)):
        packed[place : place + matrix.shape[0], : matrix.shape[1]] = matrix
    return jnp.asarray(packed)


def split(values):
    high = values.astype(jnp.bfloat16)
    rest = values - high.astype(jnp.float32)
    middle = rest.astype(jnp.bfloat16)
    low = (rest - middle.astype(jnp.float32)).astype(jnp.bfloat16)
    return high, middle, low


def iota(shape, axis):
    return lax.broadcasted_iota(jnp.int32, shape, axis)


def dot(left, right):
    return jnp.dot(left, right, preferred_element_type=jnp.float32)


def kernel(
    sizes,
    basis_hbm,
    geometry_hbm,
    normals_hbm,
    scale_hbm,
    material_hbm,
    send_list_hbm,
    source_hbm,
    turns_hbm,
    flags_hbm,
    constants_hbm,
    fresh,
    hessenberg,
    stored,
    geometry,
    normals,
    scale,
    material,
    send_list,
    source,
    turns,
    flags,
    constants_wide,
    constants,
    vector,
    field,
    around,
    table,
    others,
    rotated,
    image,
    flux,
    index_out,
    index_in,
    gram,
    held_bound,
    side_row,
    work,
    spread,
    taken,
    outgoing,
    arrived,
    sums_a,
    sums_b,
    load_sem,
    halo_send,
    halo_recv,
    sum_send,
    sum_recv,
):
    n_gx, n_gy, total, face_nodes = sizes
    kept = basis_hbm.shape[2]
    gx = lax.axis_index("gx")
    gy = lax.axis_index("gy")
    last = kept // 8 * 8
    block = (slice(None), slice(None), pl.ds(last, kept - last))
    rest = (slice(None), slice(None), pl.ds(0, last))
    loads = []
    for source_ref, target_ref in (
        (send_list_hbm, send_list),
        (basis_hbm.at[block], stored.at[block]),
        (constants_hbm, constants_wide),
        (basis_hbm.at[rest], stored.at[rest]),
        (source_hbm, source),
        (turns_hbm, turns),
        (flags_hbm, flags),
        (geometry_hbm, geometry),
        (normals_hbm, normals),
        (scale_hbm, scale),
        (material_hbm, material),
    ):
        loads.append(pltpu.make_async_copy(source_ref, target_ref, load_sem.at[len(loads)]))
    for load in loads[:2]:
        load.start()

    def turned_on(place, step, size):
        place = place + step
        return jnp.where(place >= size, place - size, place)

    partners = []
    for direction in DIRECTIONS:
        partners.append(
            (
                turned_on(gx, (direction // 3 - 1) % n_gx, n_gx),
                turned_on(gy, (direction % 3 - 1) % n_gy, n_gy),
            )
        )

    across = lax.rem(gx, X_CHIPS)
    up = lax.div(gx, X_CHIPS)
    core = lax.rem(gy, CORES)
    along = lax.div(gy, CORES)
    odd = lax.rem(across, 2)
    rows_up = n_gx // X_CHIPS
    layers = n_gy // CORES
    beside_x = gx + 1 - 2 * odd
    facing_x = gx + X_CHIPS - 1 - 2 * across
    hops_first = []
    for step in range(layers):
        for other in range(2):
            hops_first.append((min(step, layers - step) + other, step, other))
    hops_second = []
    for step in range(rows_up):
        for other in range(2):
            for flip in range(CORES):
                hops_second.append((min(step, rows_up - step) + other + flip / 2, step, other, flip))
    first_peers = [
        (hops, (beside_x if other else gx, turned_on(gy, CORES * step, n_gy)))
        for hops, step, other in sorted(hops_first, reverse=True)
        if hops > 0
    ]
    second_peers = [
        (
            hops,
            (
                turned_on(facing_x if other else gx, X_CHIPS * step, n_gx),
                turned_on(core, flip, CORES) + gy - core,
            ),
        )
        for hops, step, other, flip in sorted(hops_second, reverse=True)
        if hops > 0
    ]
    groups = (
        (2 * layers, 2 * along + odd, [peer for _, peer in first_peers]),
        (
            2 * CORES * rows_up,
            (lax.div(across, 2) * rows_up + up) * CORES + core,
            [peer for _, peer in second_peers],
        ),
    )

    barrier = pltpu.get_barrier_semaphore()
    greeted = sorted(first_peers + second_peers, key=lambda entry: -entry[0])
    greeted = [peer for _, peer in greeted] + partners
    for peer in greeted:
        pl.semaphore_signal(barrier, inc=1, device_id=peer, device_id_type=MESH)

    loads[0].wait()
    for tile in range(4):
        first, second = DIRECTIONS[2 * tile], DIRECTIONS[2 * tile + 1]
        index_out[pl.ds(tile, 1), :] = jnp.concatenate(
            [
                send_list[first // 3, pl.ds(first % 3, 1), :],
                send_list[second // 3, pl.ds(second % 3, 1), :],
            ],
            axis=1,
        )

    def pick(found, sources, index, first):
        lane = jnp.broadcast_to(jnp.bitwise_and(index, 127), (64, 128))
        tile = jnp.broadcast_to(jnp.right_shift(index, 7), (64, 128))
        for place, values in enumerate(sources):
            picked = jnp.take_along_axis(values, lane, axis=1, mode="promise_in_bounds")
            found = picked if found is None else jnp.where(tile == first + place, picked, found)
        return found

    half = iota((32, 128), 1) < 64

    def prepare(turn, greeting):
        for component in range(6):
            for face in range(4):
                for node in range(10):
                    row = pl.ds(packed_row(component, node), 1)
                    table[row, pl.ds(128 * face, 128)] = vector[
                        component, pl.ds(int(face_nodes[node, face]), 1), :
                    ]
        greeting()
        sources = [table[:, pl.ds(128 * tile, 128)] for tile in range(4)]
        for tile in (0, 3, 1, 2):
            sent = pick(None, sources, index_out[pl.ds(tile, 1), :], 0)
            top = sent[0:32]
            bottom = sent[32:64]
            outgoing[turn, 2 * tile] = jnp.where(half, top, pltpu.roll(bottom, 64, 1))
            outgoing[turn, 2 * tile + 1] = jnp.where(half, pltpu.roll(top, 64, 1), bottom)
            for index in (2 * tile, 2 * tile + 1):
                pltpu.make_async_remote_copy(
                    src_ref=outgoing.at[turn, index],
                    dst_ref=arrived.at[turn, 7 - index],
                    send_sem=halo_send.at[turn],
                    recv_sem=halo_recv.at[turn],
                    device_id=partners[index],
                    device_id_type=MESH,
                ).start()

    def apply(turn, ready, beside):
        ready()
        for component in range(6):
            field[pl.ds(0, 20), pl.ds(128 * component, 128)] = vector[component]
        high, middle, low = split(field[...])
        around[...] = dot(
            constants[pl.ds(0, 80), pl.ds(0, 192)],
            jnp.concatenate([high, middle, low, high, high, middle], axis=0)
        )

        def gradient(axis, component):
            column = pl.ds(128 * component, 128)
            return (
                around[pl.ds(0, 20), column] * geometry[pl.ds(axis, 1), :]
                + around[pl.ds(24, 20), column] * geometry[pl.ds(3 + axis, 1), :]
                + around[pl.ds(48, 20), column] * geometry[pl.ds(6 + axis, 1), :]
            )

        for component in range(3):
            after, before = (component + 1) % 3, (component + 2) % 3
            curl_e = gradient(after, before) - gradient(before, after)
            curl_h = gradient(after, 3 + before) - gradient(before, 3 + after)
            image[component] = (
                material[pl.ds(0, 1), :] * curl_h - material[pl.ds(2, 1), :] * vector[component]
            )
            image[3 + component] = -material[pl.ds(1, 1), :] * curl_e
        beside()
        sources = [table[:, pl.ds(128 * tile, 128)] for tile in range(4)]
        for face in range(4):
            lane = pl.ds(128 * face, 128)
            others[:, lane] = pick(None, sources, index_in[pl.ds(face, 1), :], 0)
        pltpu.make_async_copy(arrived.at[turn], arrived.at[turn], halo_recv.at[turn]).wait()
        sources = []
        for tile in range(4):
            even = arrived[turn, 2 * tile]
            odd = arrived[turn, 2 * tile + 1]
            sources.append(
                jnp.concatenate(
                    [
                        jnp.where(half, even, pltpu.roll(odd, 64, 1)),
                        jnp.where(half, pltpu.roll(even, 64, 1), odd),
                    ],
                    axis=0,
                )
            )
        found = jnp.concatenate(
            [
                pick(
                    others[:, pl.ds(128 * face, 128)], sources, index_in[pl.ds(face, 1), :], 4
                )
                for face in range(4)
            ],
            axis=1,
        )
        rotated[...] = dot(
            constants[pl.ds(112, 192), pl.ds(0, 192)], jnp.concatenate(split(found), axis=0)
        )
        for face in range(4):
            lane = pl.ds(128 * face, 128)
            spin = turns[pl.ds(face, 1), :]
            wall = flags[pl.ds(face, 1), :] == 1
            weight = 0.5 * scale[pl.ds(face, 1), :]
            n_x = normals[0, pl.ds(face, 1), :]
            n_y = normals[1, pl.ds(face, 1), :]
            n_z = normals[2, pl.ds(face, 1), :]
            for first_node, count in ((0, 8), (8, 2)):
                jumps = []
                for component in range(6):
                    row = packed_row(component, first_node)
                    here = table[pl.ds(row, count), lane]
                    other = jnp.where(
                        spin == 0,
                        rotated[pl.ds(row, count), lane],
                        jnp.where(
                            spin == 1,
                            rotated[pl.ds(64 + row, count), lane],
                            rotated[pl.ds(128 + row, count), lane],
                        ),
                    )
                    other = jnp.where(wall, -here if component < 3 else here, other)
                    jumps.append(other - here)
                e_x, e_y, e_z, h_x, h_y, h_z = jumps
                along_e = n_x * e_x + n_y * e_y + n_z * e_z
                along_h = n_x * h_x + n_y * h_y + n_z * h_z
                terms = [
                    n_y * h_z - n_z * h_y + e_x - along_e * n_x,
                    n_z * h_x - n_x * h_z + e_y - along_e * n_y,
                    n_x * h_y - n_y * h_x + e_z - along_e * n_z,
                    n_z * e_y - n_y * e_z + h_x - along_h * n_x,
                    n_x * e_z - n_z * e_x + h_y - along_h * n_y,
                    n_y * e_x - n_x * e_y + h_z - along_h * n_z,
                ]
                for component in range(6):
                    place = pl.ds(16 * face + first_node, count)
                    flux[place, pl.ds(128 * component, 128)] = terms[component] * weight
        high, middle, low = split(flux[...])
        lifted = dot(constants[pl.ds(80, 32), :], jnp.concatenate([high, high, middle, low], axis=0))
        for component in range(6):
            raised = lifted[0:20, 128 * component : 128 * component + 128]
            image[component] += material[pl.ds(component // 3, 1), :] * raised

    sub8 = iota((8, 128), 0)
    sub24 = iota((24, 128), 0)
    lane24 = iota((24, 128), 1)
    lane1 = iota((1, 128), 1)
    eye = sub24 == lane24

    def inner(vector_ref, *pairs):
        def some(component, held):
            held = list(held)
            for node in range(20):
                held[node % 3] += (
                    stored[component, node] * vector_ref[component, pl.ds(node, 1), :]
                )
            return tuple(held)

        zero = jnp.zeros((kept, 128), jnp.float32)
        for place, (left, right) in enumerate(pairs):
            partial = jnp.sum(left[...] * right[...], axis=0)
            work[pl.ds(kept + place, 1), :] = jnp.sum(partial, axis=0, keepdims=True)
        one, two, three = lax.fori_loop(0, 6, some, (zero, zero, zero))
        work[pl.ds(0, kept), :] = one + two + three
        return to_row(jnp.sum(work[...], axis=1, keepdims=True))

    def to_row(column):
        return jnp.sum(jnp.where(eye, column, 0.0), axis=0, keepdims=True)

    def to_column(row):
        return jnp.sum(jnp.where(eye, row, 0.0), axis=1, keepdims=True)

    def fill_gram():
        def upper(node, held):
            held = list(held)
            for component in range(6):
                tile = stored[component, node]
                for index in range(8):
                    held[index] += tile * stored[component, node, pl.ds(index, 1), :]
            return tuple(held)

        def lower(node, held):
            held = list(held)
            for component in range(6):
                tile = stored[component, node, pl.ds(8, kept - 8), :]
                for index in range(8, 16):
                    held[index - 8] += tile * stored[component, node, pl.ds(index, 1), :]
                tile = tile[8:]
                for index in range(16, kept):
                    held[index - 8] += tile * stored[component, node, pl.ds(index, 1), :]
            return tuple(held)

        def zeros(count, number):
            return (jnp.zeros((count, 128), jnp.float32),) * number

        found = list(lax.fori_loop(0, 20, upper, zeros(kept, 8)))
        found += lax.fori_loop(
            0, 20, lower, zeros(kept - 8, 8) + zeros(kept - 16, kept - 16)
        )
        gram[...] = jnp.zeros((24, 128), jnp.float32)
        for first in (0, 8, 16):
            count = kept - first
            sub = iota((count, 128), 0)
            lane = iota((count, 128), 1)
            held = jnp.zeros((count, 128), jnp.float32)
            for index in range(first, min(first + 8, kept)):
                column = jnp.sum(found[index], axis=1, keepdims=True)
                held = jnp.where(lane == index, column, held)
                row = jnp.sum(jnp.where(sub + first == lane, column, 0.0), axis=0, keepdims=True)
                held = jnp.where((sub == index - first) & (lane >= first), row, held)
            if first == 0:
                gram[pl.ds(0, kept), :] = held
            else:
                old = gram[pl.ds(first, count), :]
                gram[pl.ds(first, count), :] = jnp.where(lane >= first, held, old)

    def begin(value, buffer, which, stage):
        size, mine, peers = groups[stage]
        buffer[stage, mine] = value
        for peer in peers:
            pltpu.make_async_remote_copy(
                src_ref=buffer.at[stage, mine],
                dst_ref=buffer.at[stage, mine],
                send_sem=sum_send.at[which, stage],
                recv_sem=sum_recv.at[which, stage],
                device_id=peer,
                device_id_type=MESH,
            ).start()

    def finish(buffer, which, stage):
        size, mine, peers = groups[stage]
        if size > 1:
            others = buffer.at[stage, pl.ds(0, size - 1)]
            pltpu.make_async_copy(others, others, sum_recv.at[which, stage]).wait()
        values = [buffer[stage, member] for member in range(size)]
        while len(values) > 1:
            values = [sum(values[at : at + 2]) for at in range(0, len(values), 2)]
        return values[0]

    def project(column):
        weights = jnp.broadcast_to(column[0:kept], (kept, 128))

        def one(component, carry):
            for node in range(20):
                product = stored[component, node] * weights
                short = jnp.concatenate(
                    [product[16:kept], jnp.zeros((24 - kept, 128), jnp.float32)], axis=0
                )
                spread[component, pl.ds(8 * node, 8), :] = product[0:8] + product[8:16] + short
            return carry

        lax.fori_loop(0, 6, one, 0)
        for component in range(6):
            parts_of = [spread[component, pl.ds(at, 20, stride=8), :] for at in range(8)]
            while len(parts_of) > 1:
                parts_of = [sum(parts_of[at : at + 2]) for at in range(0, len(parts_of), 2)]
            taken[component] = parts_of[0]

    field[pl.ds(16, 16), :] = jnp.zeros((16, 768), jnp.float32)
    table[pl.ds(56, 8), :] = jnp.zeros((8, 512), jnp.float32)
    flux[...] = jnp.zeros((64, 768), jnp.float32)
    held_bound[...] = jnp.ones((1, 128), jnp.float32)
    side_row[...] = jnp.zeros((1, 128), jnp.float32)
    work[...] = jnp.zeros((24, 128), jnp.float32)
    hessenberg[...] = jnp.zeros((2, kept + 2), jnp.float32)
    loads[1].wait()
    for load in loads[2:]:
        load.start()
    for component in range(6):
        vector[component] = stored[component, :, kept - 1, :]

    def step(turn, carry):
        first_step = turn == 0
        sums = sums_b.at[turn]

        def ready():
            @pl.when(first_step)
            def _():
                for load in loads[2:]:
                    load.wait()
                constants[...] = constants_wide[...].astype(jnp.bfloat16)

        def beside():
            @pl.when(first_step)
            def _():
                for face in range(4):
                    named = source[pl.ds(face, 1), :]
                    index_in[pl.ds(face, 1), :] = jnp.where(
                        named >= 512 + 4 * 64, named - 64, named
                    )
                fill_gram()
                packed = (
                    gram[pl.ds(0, 8), :]
                    + pltpu.roll(gram[pl.ds(8, 8), :], 32, 1)
                    + pltpu.roll(gram[pl.ds(16, 8), :], 64, 1)
                )
                begin(packed, sums_a, 2, 0)

            @pl.when(jnp.logical_not(first_step))
            def _():
                side_row[...] = pltpu.roll(inner(vector, (vector, vector)), 32, 1)

        def greeting():
            @pl.when(first_step)
            def _():
                pl.semaphore_wait(barrier, len(greeted))

        prepare(turn, greeting)
        apply(turn, ready, beside)

        row = inner(image, (vector, image), (image, image))
        begin(row + side_row[...], sums, turn, 0)

        @pl.when(first_step)
        def _():
            begin(finish(sums_a, 2, 0), sums_a, 2, 1)

        begin(finish(sums, turn, 0), sums, turn, 1)

        @pl.when(first_step)
        def _():
            packed = finish(sums_a, 2, 1) * (1.0 / total)
            products = jnp.concatenate(
                [packed, pltpu.roll(packed, 96, 1), pltpu.roll(packed, 64, 1)], axis=0
            )
            gram[...] = jnp.where(lane24 < 24, products, 0.0)

        products = gram[...]
        own = jnp.sum(jnp.where(eye, products, 0.0), axis=1, keepdims=True)
        message = finish(sums, turn, 1) * (1.0 / total)

        bound = held_bound[...][:, 0:1]
        row = jnp.where(lane1 < kept + turn, message, 0.0)
        side = jnp.where(lane1 < kept + 1, pltpu.roll(message, 96, 1), 0.0)
        square = jnp.sum(jnp.where(lane1 == kept + 1, message, 0.0), keepdims=True)
        length = jnp.sum(jnp.where(lane1 == kept, side, 0.0), keepdims=True)
        height = jnp.sqrt(length * (bound * bound) + 1e-06)
        grow = jnp.where(first_step, 1.0, bound / height)
        side = side * jnp.where(lane1 == kept, grow * grow, grow)
        row = row * jnp.where(lane1 == kept, grow * grow, grow)
        extended = kept + turn - 1
        products = jnp.where((lane24 == kept) & (extended == kept), to_column(side), products)
        products = jnp.where((sub24 == kept) & (extended == kept), side, products)
        column = jnp.sum((jnp.where(eye, 2.0, 0.0) - products) * row, axis=1, keepdims=True)
        column_row = to_row(column)

        @pl.when(jnp.logical_not(first_step))
        def _():
            before = hessenberg[pl.ds(0, 1), :]
            hessenberg[pl.ds(0, 1), :] = jnp.where(
                lane1[:, 0:24] == kept, height, before
            )

        square = square * (grow * grow)
        length = square + jnp.sum(
            column * (products * column_row - jnp.where(eye, 2.0, 0.0) * row), keepdims=True
        )
        height = jnp.sqrt(jnp.maximum(length, 0.0) + 1e-06)
        bound = jnp.sum(jnp.abs(column) * jnp.sqrt(own), keepdims=True) + jnp.sqrt(square) + 1e-3
        held_bound[...] = jnp.broadcast_to(bound, (1, 128))
        shrink = 1.0 / jnp.where(first_step, bound, height)
        project(column)
        on_own = column[kept : kept + 1] * grow
        for component in range(6):
            current = vector[component]
            new = (image[component] * grow - current * on_own - taken[component]) * shrink
            fresh[0, component] = current * grow
            fresh[1, component] = new
            vector[component] = new
        hessenberg[pl.ds(turn, 1), :] = jnp.where(
            lane1 == kept + 1, jnp.where(first_step, 0.0, height), column_row
        )[:, 0:24]
        return carry

    lax.fori_loop(0, 2, step, 0)
    for turn in range(2):
        pltpu.make_async_copy(outgoing.at[turn], outgoing.at[turn], halo_send.at[turn]).wait()
    for which in range(3):
        for stage, (size, _, _) in enumerate(groups):
            if size > 1:
                buffer = sums_a if which == 2 else sums_b.at[which]
                others = buffer.at[stage, pl.ds(0, size - 1)]
                pltpu.make_async_copy(others, others, sum_send.at[which, stage]).wait()


def body(
    n_gx,
    n_gy,
    basis,
    geometry,
    face_normals,
    face_scale,
    material,
    send_list,
    neighbour_source,
    node_rotation,
    boundary_flag,
):
    kept, components, nodes, local_count = basis.shape
    total = float(components * nodes * local_count * n_gx * n_gy)
    f32, bf16 = jnp.float32, jnp.bfloat16
    members = max(2 * n_gy // CORES, 2 * CORES * n_gx // X_CHIPS)
    anywhere = pl.BlockSpec(memory_space=pl.ANY)
    vmem = pl.BlockSpec(memory_space=pltpu.VMEM)
    return pl.pallas_call(
        functools.partial(kernel, (n_gx, n_gy, total, element_tables()[2])),
        out_shape=(
            pltpu.VMEM((2, components, nodes, local_count), f32),
            pltpu.VMEM((2, kept + 2), f32),
        ),
        in_specs=[anywhere] * 10,
        out_specs=(vmem, vmem),
        scratch_shapes=[
            pltpu.VMEM((components, nodes, kept, local_count), f32),
            pltpu.VMEM(geometry.shape, f32),
            pltpu.VMEM(face_normals.shape, f32),
            pltpu.VMEM(face_scale.shape, f32),
            pltpu.VMEM(material.shape, f32),
            pltpu.VMEM(send_list.shape, jnp.int32),
            pltpu.VMEM(neighbour_source.shape, jnp.int32),
            pltpu.VMEM(node_rotation.shape, jnp.int32),
            pltpu.VMEM(boundary_flag.shape, jnp.int32),
            pltpu.VMEM((304, 256), f32),
            pltpu.VMEM((304, 256), bf16),
            pltpu.VMEM((components, nodes, local_count), f32),
            pltpu.VMEM((32, 768), f32),
            pltpu.VMEM((80, 768), f32),
            pltpu.VMEM((64, 512), f32),
            pltpu.VMEM((64, 512), f32),
            pltpu.VMEM((192, 512), f32),
            pltpu.VMEM((components, nodes, local_count), f32),
            pltpu.VMEM((64, 768), f32),
            pltpu.VMEM((4, 128), jnp.int32),
            pltpu.VMEM((4, 128), jnp.int32),
            pltpu.VMEM((24, 128), f32),
            pltpu.VMEM((1, 128), f32),
            pltpu.VMEM((1, 128), f32),
            pltpu.VMEM((24, 128), f32),
            pltpu.VMEM((components, 8 * nodes, local_count), f32),
            pltpu.VMEM((components, nodes, local_count), f32),
            pltpu.VMEM((2, 8, 32, 128), f32),
            pltpu.VMEM((2, 8, 32, 128), f32),
            pltpu.VMEM((2, members, 8, 128), f32),
            pltpu.VMEM((2, 2, members, 1, 128), f32),
            pltpu.SemaphoreType.DMA((12,)),
            pltpu.SemaphoreType.DMA((2,)),
            pltpu.SemaphoreType.DMA((2,)),
            pltpu.SemaphoreType.DMA((3, 3)),
            pltpu.SemaphoreType.DMA((3, 3)),
        ],
        compiler_params=pltpu.CompilerParams(
            collective_id=0, has_side_effects=True, vmem_limit_bytes=32 * 1024 * 1024
        ),
    )(
        *[
            pltpu.with_memory_space_constraint(operand, pltpu.HBM)
            for operand in (
                jnp.transpose(basis, (1, 2, 0, 3)),
                geometry,
                face_normals,
                face_scale,
                material,
                send_list,
                neighbour_source,
                node_rotation,
                boundary_flag,
                left_operands(),
            )
        ]
    )


def solution(mesh):
    placed = (
        P(None, None, None, ("gx", "gy")),
        P(None, ("gx", "gy")),
        P(None, None, ("gx", "gy")),
        P(None, ("gx", "gy")),
        P(None, ("gx", "gy")),
        P("gx", "gy", None),
        P(None, ("gx", "gy")),
        P(None, ("gx", "gy")),
        P(None, ("gx", "gy")),
    )
    return jax.shard_map(
        functools.partial(body, mesh.shape["gx"], mesh.shape["gy"]),
        mesh=mesh,
        in_specs=placed,
        out_specs=(P(None, None, None, ("gx", "gy")), P()),
        check_vma=False,
    )
```

```python
import functools
import math

import jax
import jax.numpy as jnp
import numpy as np
from jax import lax
from jax.experimental import pallas as pl
from jax.experimental.pallas import tpu as pltpu
from jax.sharding import PartitionSpec as P

MESH = pl.DeviceIdType.MESH
X_CHIPS = 4
CORES = 2
OPERANDS = (0, 80, 112)
DIRECTIONS = (0, 1, 2, 3, 5, 6, 7, 8)


def invert(matrix):
    dimension = len(matrix)
    augmented = []
    for row_index in range(dimension):
        augmented.append(
            [float(matrix[row_index][column]) for column in range(dimension)]
            + [1.0 if column == row_index else 0.0 for column in range(dimension)]
        )
    for column in range(dimension):
        pivot_row = column
        for row_index in range(column + 1, dimension):
            if abs(augmented[row_index][column]) > abs(augmented[pivot_row][column]):
                pivot_row = row_index
        augmented[column], augmented[pivot_row] = (augmented[pivot_row], augmented[column])
        leading = augmented[column][column]
        augmented[column] = [value / leading for value in augmented[column]]
        for row_index in range(dimension):
            if row_index != column:
                factor = augmented[row_index][column]
                augmented[row_index] = [
                    left - factor * right
                    for left, right in zip(augmented[row_index], augmented[column])
                ]
    return np.array([entries[dimension:] for entries in augmented])


def locate(face, first, second):
    if face == 0:
        return (first, second, 0)
    if face == 1:
        return (first, 0, second)
    if face == 2:
        return (3 - first - second, first, second)
    return (0, first, second)


def element_tables():
    nodes = [(i, j, k) for k in range(4) for j in range(4) for i in range(4) if i + j + k <= 3]
    points = np.array(nodes) / 3.0
    vander = np.zeros((20, 20))
    slopes = np.zeros((3, 20, 20))
    for row in range(20):
        for column in range(20):
            powers = np.array(nodes[column])
            vander[row, column] = np.prod(points[row] ** powers)
            for axis in range(3):
                if powers[axis] > 0:
                    lowered = powers.copy()
                    lowered[axis] -= 1
                    slopes[axis, row, column] = powers[axis] * np.prod(points[row] ** lowered)
    inverse = invert(vander)
    derivs = np.stack([slopes[axis] @ inverse for axis in range(3)])
    moments = np.zeros((20, 20))
    for row in range(20):
        for column in range(20):
            left = nodes[row]
            right = nodes[column]
            sums = [left[0] + right[0], left[1] + right[1], left[2] + right[2]]
            moments[row, column] = (
                math.factorial(sums[0])
                * math.factorial(sums[1])
                * math.factorial(sums[2])
                / math.factorial(sum(sums) + 3)
            )
    mass = inverse.T @ moments @ inverse
    lattice = [(first, second) for second in range(4) for first in range(4) if first + second <= 3]
    face_nodes = np.array(
        [[nodes.index(locate(face, pair[0], pair[1])) for face in range(4)] for pair in lattice]
    )
    plane = np.array(
        [
            [(pair[0] / 3.0) ** expo[0] * (pair[1] / 3.0) ** expo[1] for expo in lattice]
            for pair in lattice
        ]
    )
    plane_inverse = invert(plane)
    plane_moments = np.zeros((10, 10))
    for row in range(10):
        for column in range(10):
            first = lattice[row][0] + lattice[column][0]
            second = lattice[row][1] + lattice[column][1]
            plane_moments[row, column] = (
                math.factorial(first) * math.factorial(second) / math.factorial(first + second + 2)
            )
    face_mass = plane_inverse.T @ plane_moments @ plane_inverse
    edges = np.zeros((20, 40))
    for face in range(4):
        for row in range(10):
            for column in range(10):
                edges[face_nodes[row, face], column * 4 + face] += face_mass[row, column]
    lift = invert(mass) @ edges
    turned = np.array([lattice.index((pair[1], 3 - pair[0] - pair[1])) for pair in lattice])
    rotations = np.stack([np.arange(10), turned, turned[turned]])
    return (derivs, lift, face_nodes, rotations)


def bf16_parts(values):
    values = np.asarray(values, np.float32)
    high = values.astype(jnp.bfloat16)
    rest = values - high.astype(np.float32)
    middle = rest.astype(jnp.bfloat16)
    low = (rest - middle.astype(np.float32)).astype(jnp.bfloat16)
    return high, middle, low


def packed_row(component, node):
    return 8 * component + node if node < 8 else 48 + 2 * component + node - 8


def left_operands():
    derivs, lift, face_nodes, rotations = element_tables()
    stack = np.zeros((3, 80, 32), np.float32)
    for index, part in enumerate(bf16_parts(derivs)):
        for axis in range(3):
            stack[index, 24 * axis : 24 * axis + 20, :20] = part[axis].astype(np.float32)
    high, middle, low = stack
    volume = np.concatenate([high, high, high, middle, low, middle], axis=1)
    blocks = np.zeros((3, 32, 64), np.float32)
    for index, part in enumerate(bf16_parts(lift)):
        for face in range(4):
            for node in range(10):
                blocks[index, :20, 16 * face + node] = part[:, node * 4 + face].astype(np.float32)
    raise_up = np.concatenate([blocks[0], blocks[1], blocks[0], blocks[0]], axis=1)
    spread = np.zeros((192, 64), np.float32)
    for turn in range(3):
        for component in range(6):
            for node in range(10):
                spread[
                    64 * turn + packed_row(component, node),
                    packed_row(component, rotations[turn][node]),
                ] = 1.0
    turned = np.concatenate([spread, spread, spread], axis=1)
    packed = np.zeros((304, 256), np.float32)
    for place, matrix in zip(OPERANDS, (volume, raise_up, turned)):
        packed[place : place + matrix.shape[0], : matrix.shape[1]] = matrix
    return jnp.asarray(packed)


def split(values):
    high = values.astype(jnp.bfloat16)
    rest = values - high.astype(jnp.float32)
    middle = rest.astype(jnp.bfloat16)
    low = (rest - middle.astype(jnp.float32)).astype(jnp.bfloat16)
    return high, middle, low


def iota(shape, axis):
    return lax.broadcasted_iota(jnp.int32, shape, axis)


def dot(left, right):
    return jnp.dot(left, right, preferred_element_type=jnp.float32)


def kernel(
    sizes,
    basis_hbm,
    geometry_hbm,
    normals_hbm,
    scale_hbm,
    material_hbm,
    send_list_hbm,
    source_hbm,
    turns_hbm,
    flags_hbm,
    constants_hbm,
    fresh,
    hessenberg,
    stored,
    geometry,
    normals,
    scale,
    material,
    send_list,
    source,
    turns,
    flags,
    constants_wide,
    constants,
    vector,
    field,
    around,
    table,
    others,
    rotated,
    image,
    flux,
    index_out,
    index_in,
    gram,
    held_bound,
    side_row,
    work,
    spread,
    taken,
    outgoing,
    arrived,
    sums_a,
    sums_b,
    load_sem,
    halo_send,
    halo_recv,
    sum_send,
    sum_recv,
):
    n_gx, n_gy, total, face_nodes = sizes
    kept = basis_hbm.shape[2]
    gx = lax.axis_index("gx")
    gy = lax.axis_index("gy")
    last = kept // 8 * 8
    block = (slice(None), slice(None), pl.ds(last, kept - last))
    rest = (slice(None), slice(None), pl.ds(0, last))
    loads = []
    for source_ref, target_ref in (
        (send_list_hbm, send_list),
        (basis_hbm.at[block], stored.at[block]),
        (constants_hbm, constants_wide),
        (basis_hbm.at[rest], stored.at[rest]),
        (source_hbm, source),
        (turns_hbm, turns),
        (flags_hbm, flags),
        (geometry_hbm, geometry),
        (normals_hbm, normals),
        (scale_hbm, scale),
        (material_hbm, material),
    ):
        loads.append(pltpu.make_async_copy(source_ref, target_ref, load_sem.at[len(loads)]))
    for load in loads[:2]:
        load.start()

    def turned_on(place, step, size):
        place = place + step
        return jnp.where(place >= size, place - size, place)

    partners = []
    for direction in DIRECTIONS:
        partners.append(
            (
                turned_on(gx, (direction // 3 - 1) % n_gx, n_gx),
                turned_on(gy, (direction % 3 - 1) % n_gy, n_gy),
            )
        )

    across = lax.rem(gx, X_CHIPS)
    up = lax.div(gx, X_CHIPS)
    core = lax.rem(gy, CORES)
    along = lax.div(gy, CORES)
    odd = lax.rem(across, 2)
    rows_up = n_gx // X_CHIPS
    layers = n_gy // CORES
    beside_x = gx + 1 - 2 * odd
    facing_x = gx + X_CHIPS - 1 - 2 * across
    hops_first = []
    for step in range(layers):
        for other in range(2):
            for flip in range(CORES):
                hops_first.append((min(step, layers - step) + other + flip / 2, step, other, flip))
    hops_second = []
    for step in range(rows_up):
        for other in range(2):
            hops_second.append((min(step, rows_up - step) + other, step, other))
    first_peers = [
        (
            hops,
            (
                beside_x if other else gx,
                turned_on(gy, CORES * step, n_gy) - core + turned_on(core, flip, CORES),
            ),
        )
        for hops, step, other, flip in sorted(hops_first, reverse=True)
        if hops > 0
    ]
    second_peers = [
        (hops, (turned_on(facing_x if other else gx, X_CHIPS * step, n_gx), gy))
        for hops, step, other in sorted(hops_second, reverse=True)
        if hops > 0
    ]
    first_group = (
        2 * CORES * layers,
        (2 * along + odd) * CORES + core,
        [peer for _, peer in first_peers],
    )
    second_group = (
        2 * rows_up,
        lax.div(across, 2) * rows_up + up,
        [peer for _, peer in second_peers],
    )

    def group_of(which, stage):
        is_gram = isinstance(which, int) and which == 2
        return second_group if (stage == 1) != is_gram else first_group

    barrier = pltpu.get_barrier_semaphore()
    greeted = sorted(first_peers + second_peers, key=lambda entry: -entry[0])
    greeted = [peer for _, peer in greeted] + partners
    for peer in greeted:
        pl.semaphore_signal(barrier, inc=1, device_id=peer, device_id_type=MESH)

    loads[0].wait()
    for tile in range(4):
        first, second = DIRECTIONS[2 * tile], DIRECTIONS[2 * tile + 1]
        index_out[pl.ds(tile, 1), :] = jnp.concatenate(
            [
                send_list[first // 3, pl.ds(first % 3, 1), :],
                send_list[second // 3, pl.ds(second % 3, 1), :],
            ],
            axis=1,
        )

    def pick(found, sources, index, first):
        lane = jnp.broadcast_to(jnp.bitwise_and(index, 127), (64, 128))
        tile = jnp.broadcast_to(jnp.right_shift(index, 7), (64, 128))
        for place, values in enumerate(sources):
            picked = jnp.take_along_axis(values, lane, axis=1, mode="promise_in_bounds")
            found = picked if found is None else jnp.where(tile == first + place, picked, found)
        return found

    half = iota((32, 128), 1) < 64

    def prepare(turn, greeting):
        for component in range(6):
            for face in range(4):
                for node in range(10):
                    row = pl.ds(packed_row(component, node), 1)
                    table[row, pl.ds(128 * face, 128)] = vector[
                        component, pl.ds(int(face_nodes[node, face]), 1), :
                    ]
        greeting()
        sources = [table[:, pl.ds(128 * tile, 128)] for tile in range(4)]
        for tile in (0, 3, 1, 2):
            sent = pick(None, sources, index_out[pl.ds(tile, 1), :], 0)
            top = sent[0:32]
            bottom = sent[32:64]
            outgoing[turn, 2 * tile] = jnp.where(half, top, pltpu.roll(bottom, 64, 1))
            outgoing[turn, 2 * tile + 1] = jnp.where(half, pltpu.roll(top, 64, 1), bottom)
            for index in (2 * tile, 2 * tile + 1):
                pltpu.make_async_remote_copy(
                    src_ref=outgoing.at[turn, index],
                    dst_ref=arrived.at[turn, 7 - index],
                    send_sem=halo_send.at[turn],
                    recv_sem=halo_recv.at[turn],
                    device_id=partners[index],
                    device_id_type=MESH,
                ).start()

    def apply(turn, ready, beside):
        ready()
        for component in range(6):
            field[pl.ds(0, 20), pl.ds(128 * component, 128)] = vector[component]
        high, middle, low = split(field[...])
        around[...] = dot(
            constants[pl.ds(0, 80), pl.ds(0, 192)],
            jnp.concatenate([high, middle, low, high, high, middle], axis=0)
        )

        def gradient(axis, component):
            column = pl.ds(128 * component, 128)
            return (
                around[pl.ds(0, 20), column] * geometry[pl.ds(axis, 1), :]
                + around[pl.ds(24, 20), column] * geometry[pl.ds(3 + axis, 1), :]
                + around[pl.ds(48, 20), column] * geometry[pl.ds(6 + axis, 1), :]
            )

        for component in range(3):
            after, before = (component + 1) % 3, (component + 2) % 3
            curl_e = gradient(after, before) - gradient(before, after)
            curl_h = gradient(after, 3 + before) - gradient(before, 3 + after)
            image[component] = (
                material[pl.ds(0, 1), :] * curl_h - material[pl.ds(2, 1), :] * vector[component]
            )
            image[3 + component] = -material[pl.ds(1, 1), :] * curl_e
        beside()
        sources = [table[:, pl.ds(128 * tile, 128)] for tile in range(4)]
        for face in range(4):
            lane = pl.ds(128 * face, 128)
            others[:, lane] = pick(None, sources, index_in[pl.ds(face, 1), :], 0)
        pltpu.make_async_copy(arrived.at[turn], arrived.at[turn], halo_recv.at[turn]).wait()
        sources = []
        for tile in range(4):
            even = arrived[turn, 2 * tile]
            odd = arrived[turn, 2 * tile + 1]
            sources.append(
                jnp.concatenate(
                    [
                        jnp.where(half, even, pltpu.roll(odd, 64, 1)),
                        jnp.where(half, pltpu.roll(even, 64, 1), odd),
                    ],
                    axis=0,
                )
            )
        found = jnp.concatenate(
            [
                pick(
                    others[:, pl.ds(128 * face, 128)], sources, index_in[pl.ds(face, 1), :], 4
                )
                for face in range(4)
            ],
            axis=1,
        )
        rotated[...] = dot(
            constants[pl.ds(112, 192), pl.ds(0, 192)], jnp.concatenate(split(found), axis=0)
        )
        for face in range(4):
            lane = pl.ds(128 * face, 128)
            spin = turns[pl.ds(face, 1), :]
            wall = flags[pl.ds(face, 1), :] == 1
            weight = 0.5 * scale[pl.ds(face, 1), :]
            n_x = normals[0, pl.ds(face, 1), :]
            n_y = normals[1, pl.ds(face, 1), :]
            n_z = normals[2, pl.ds(face, 1), :]
            for first_node, count in ((0, 8), (8, 2)):
                jumps = []
                for component in range(6):
                    row = packed_row(component, first_node)
                    here = table[pl.ds(row, count), lane]
                    other = jnp.where(
                        spin == 0,
                        rotated[pl.ds(row, count), lane],
                        jnp.where(
                            spin == 1,
                            rotated[pl.ds(64 + row, count), lane],
                            rotated[pl.ds(128 + row, count), lane],
                        ),
                    )
                    other = jnp.where(wall, -here if component < 3 else here, other)
                    jumps.append(other - here)
                e_x, e_y, e_z, h_x, h_y, h_z = jumps
                along_e = n_x * e_x + n_y * e_y + n_z * e_z
                along_h = n_x * h_x + n_y * h_y + n_z * h_z
                terms = [
                    n_y * h_z - n_z * h_y + e_x - along_e * n_x,
                    n_z * h_x - n_x * h_z + e_y - along_e * n_y,
                    n_x * h_y - n_y * h_x + e_z - along_e * n_z,
                    n_z * e_y - n_y * e_z + h_x - along_h * n_x,
                    n_x * e_z - n_z * e_x + h_y - along_h * n_y,
                    n_y * e_x - n_x * e_y + h_z - along_h * n_z,
                ]
                for component in range(6):
                    place = pl.ds(16 * face + first_node, count)
                    flux[place, pl.ds(128 * component, 128)] = terms[component] * weight
        high, middle, low = split(flux[...])
        lifted = dot(constants[pl.ds(80, 32), :], jnp.concatenate([high, high, middle, low], axis=0))
        for component in range(6):
            raised = lifted[0:20, 128 * component : 128 * component + 128]
            image[component] += material[pl.ds(component // 3, 1), :] * raised

    sub8 = iota((8, 128), 0)
    sub24 = iota((24, 128), 0)
    lane24 = iota((24, 128), 1)
    lane1 = iota((1, 128), 1)
    eye = sub24 == lane24

    def inner(vector_ref, *pairs):
        def some(component, held):
            held = list(held)
            for node in range(20):
                held[node % 3] += (
                    stored[component, node] * vector_ref[component, pl.ds(node, 1), :]
                )
            return tuple(held)

        zero = jnp.zeros((kept, 128), jnp.float32)
        for place, (left, right) in enumerate(pairs):
            partial = jnp.sum(left[...] * right[...], axis=0)
            work[pl.ds(kept + place, 1), :] = jnp.sum(partial, axis=0, keepdims=True)
        one, two, three = lax.fori_loop(0, 6, some, (zero, zero, zero))
        work[pl.ds(0, kept), :] = one + two + three
        return to_row(jnp.sum(work[...], axis=1, keepdims=True))

    def to_row(column):
        return jnp.sum(jnp.where(eye, column, 0.0), axis=0, keepdims=True)

    def to_column(row):
        return jnp.sum(jnp.where(eye, row, 0.0), axis=1, keepdims=True)

    def fill_gram():
        def upper(node, held):
            held = list(held)
            for component in range(6):
                tile = stored[component, node]
                for index in range(8):
                    held[index] += tile * stored[component, node, pl.ds(index, 1), :]
            return tuple(held)

        def lower(node, held):
            held = list(held)
            for component in range(6):
                tile = stored[component, node, pl.ds(8, kept - 8), :]
                for index in range(8, 16):
                    held[index - 8] += tile * stored[component, node, pl.ds(index, 1), :]
                tile = tile[8:]
                for index in range(16, kept):
                    held[index - 8] += tile * stored[component, node, pl.ds(index, 1), :]
            return tuple(held)

        def zeros(count, number):
            return (jnp.zeros((count, 128), jnp.float32),) * number

        found = list(lax.fori_loop(0, 20, upper, zeros(kept, 8)))
        found += lax.fori_loop(
            0, 20, lower, zeros(kept - 8, 8) + zeros(kept - 16, kept - 16)
        )
        gram[...] = jnp.zeros((24, 128), jnp.float32)
        for first in (0, 8, 16):
            count = kept - first
            sub = iota((count, 128), 0)
            lane = iota((count, 128), 1)
            held = jnp.zeros((count, 128), jnp.float32)
            for index in range(first, min(first + 8, kept)):
                column = jnp.sum(found[index], axis=1, keepdims=True)
                held = jnp.where(lane == index, column, held)
                row = jnp.sum(jnp.where(sub + first == lane, column, 0.0), axis=0, keepdims=True)
                held = jnp.where((sub == index - first) & (lane >= first), row, held)
            if first == 0:
                gram[pl.ds(0, kept), :] = held
            else:
                old = gram[pl.ds(first, count), :]
                gram[pl.ds(first, count), :] = jnp.where(lane >= first, held, old)

    def begin(value, buffer, which, stage):
        size, mine, peers = group_of(which, stage)
        buffer[stage, mine] = value
        for peer in peers:
            pltpu.make_async_remote_copy(
                src_ref=buffer.at[stage, mine],
                dst_ref=buffer.at[stage, mine],
                send_sem=sum_send.at[which, stage],
                recv_sem=sum_recv.at[which, stage],
                device_id=peer,
                device_id_type=MESH,
            ).start()

    def finish(buffer, which, stage):
        size, mine, peers = group_of(which, stage)
        if size > 1:
            others = buffer.at[stage, pl.ds(0, size - 1)]
            pltpu.make_async_copy(others, others, sum_recv.at[which, stage]).wait()
        values = [buffer[stage, member] for member in range(size)]
        while len(values) > 1:
            values = [sum(values[at : at + 2]) for at in range(0, len(values), 2)]
        return values[0]

    def project(column):
        weights = jnp.broadcast_to(column[0:kept], (kept, 128))

        def one(component, carry):
            for node in range(20):
                product = stored[component, node] * weights
                short = jnp.concatenate(
                    [product[16:kept], jnp.zeros((24 - kept, 128), jnp.float32)], axis=0
                )
                spread[component, pl.ds(8 * node, 8), :] = product[0:8] + product[8:16] + short
            return carry

        lax.fori_loop(0, 6, one, 0)
        for component in range(6):
            parts_of = [spread[component, pl.ds(at, 20, stride=8), :] for at in range(8)]
            while len(parts_of) > 1:
                parts_of = [sum(parts_of[at : at + 2]) for at in range(0, len(parts_of), 2)]
            taken[component] = parts_of[0]

    field[pl.ds(16, 16), :] = jnp.zeros((16, 768), jnp.float32)
    table[pl.ds(56, 8), :] = jnp.zeros((8, 512), jnp.float32)
    flux[...] = jnp.zeros((64, 768), jnp.float32)
    held_bound[...] = jnp.ones((1, 128), jnp.float32)
    side_row[...] = jnp.zeros((1, 128), jnp.float32)
    work[...] = jnp.zeros((24, 128), jnp.float32)
    hessenberg[...] = jnp.zeros((2, kept + 2), jnp.float32)
    loads[1].wait()
    for load in loads[2:]:
        load.start()
    for component in range(6):
        vector[component] = stored[component, :, kept - 1, :]

    def step(turn, carry):
        first_step = turn == 0
        sums = sums_b.at[turn]

        def ready():
            @pl.when(first_step)
            def _():
                for load in loads[2:]:
                    load.wait()
                constants[...] = constants_wide[...].astype(jnp.bfloat16)

        def beside():
            @pl.when(first_step)
            def _():
                for face in range(4):
                    named = source[pl.ds(face, 1), :]
                    index_in[pl.ds(face, 1), :] = jnp.where(
                        named >= 512 + 4 * 64, named - 64, named
                    )
                fill_gram()
                packed = (
                    gram[pl.ds(0, 8), :]
                    + pltpu.roll(gram[pl.ds(8, 8), :], 32, 1)
                    + pltpu.roll(gram[pl.ds(16, 8), :], 64, 1)
                )
                begin(packed, sums_a, 2, 0)

            @pl.when(jnp.logical_not(first_step))
            def _():
                side_row[...] = pltpu.roll(inner(vector, (vector, vector)), 32, 1)

        def greeting():
            @pl.when(first_step)
            def _():
                pl.semaphore_wait(barrier, len(greeted))

        prepare(turn, greeting)
        apply(turn, ready, beside)

        row = inner(image, (vector, image), (image, image))
        begin(row + side_row[...], sums, turn, 0)

        @pl.when(first_step)
        def _():
            begin(finish(sums_a, 2, 0), sums_a, 2, 1)

        begin(finish(sums, turn, 0), sums, turn, 1)

        @pl.when(first_step)
        def _():
            packed = finish(sums_a, 2, 1) * (1.0 / total)
            products = jnp.concatenate(
                [packed, pltpu.roll(packed, 96, 1), pltpu.roll(packed, 64, 1)], axis=0
            )
            gram[...] = jnp.where(lane24 < 24, products, 0.0)

        products = gram[...]
        own = jnp.sum(jnp.where(eye, products, 0.0), axis=1, keepdims=True)
        message = finish(sums, turn, 1) * (1.0 / total)

        bound = held_bound[...][:, 0:1]
        row = jnp.where(lane1 < kept + turn, message, 0.0)
        side = jnp.where(lane1 < kept + 1, pltpu.roll(message, 96, 1), 0.0)
        square = jnp.sum(jnp.where(lane1 == kept + 1, message, 0.0), keepdims=True)
        length = jnp.sum(jnp.where(lane1 == kept, side, 0.0), keepdims=True)
        height = jnp.sqrt(length * (bound * bound) + 1e-06)
        grow = jnp.where(first_step, 1.0, bound / height)
        side = side * jnp.where(lane1 == kept, grow * grow, grow)
        row = row * jnp.where(lane1 == kept, grow * grow, grow)
        extended = kept + turn - 1
        products = jnp.where((lane24 == kept) & (extended == kept), to_column(side), products)
        products = jnp.where((sub24 == kept) & (extended == kept), side, products)
        column = jnp.sum((jnp.where(eye, 2.0, 0.0) - products) * row, axis=1, keepdims=True)
        column_row = to_row(column)

        @pl.when(jnp.logical_not(first_step))
        def _():
            before = hessenberg[pl.ds(0, 1), :]
            hessenberg[pl.ds(0, 1), :] = jnp.where(
                lane1[:, 0:24] == kept, height, before
            )

        square = square * (grow * grow)
        length = square + jnp.sum(
            column * (products * column_row - jnp.where(eye, 2.0, 0.0) * row), keepdims=True
        )
        height = jnp.sqrt(jnp.maximum(length, 0.0) + 1e-06)
        bound = jnp.sum(jnp.abs(column) * jnp.sqrt(own), keepdims=True) + jnp.sqrt(square) + 1e-3
        held_bound[...] = jnp.broadcast_to(bound, (1, 128))
        shrink = 1.0 / jnp.where(first_step, bound, height)
        project(column)
        on_own = column[kept : kept + 1] * grow
        for component in range(6):
            current = vector[component]
            new = (image[component] * grow - current * on_own - taken[component]) * shrink
            fresh[0, component] = current * grow
            fresh[1, component] = new
            vector[component] = new
        hessenberg[pl.ds(turn, 1), :] = jnp.where(
            lane1 == kept + 1, jnp.where(first_step, 0.0, height), column_row
        )[:, 0:24]
        return carry

    lax.fori_loop(0, 2, step, 0)
    for turn in range(2):
        pltpu.make_async_copy(outgoing.at[turn], outgoing.at[turn], halo_send.at[turn]).wait()
    for which in range(3):
        for stage in range(2):
            size = group_of(which, stage)[0]
            if size > 1:
                buffer = sums_a if which == 2 else sums_b.at[which]
                others = buffer.at[stage, pl.ds(0, size - 1)]
                pltpu.make_async_copy(others, others, sum_send.at[which, stage]).wait()


def body(
    n_gx,
    n_gy,
    basis,
    geometry,
    face_normals,
    face_scale,
    material,
    send_list,
    neighbour_source,
    node_rotation,
    boundary_flag,
):
    kept, components, nodes, local_count = basis.shape
    total = float(components * nodes * local_count * n_gx * n_gy)
    f32, bf16 = jnp.float32, jnp.bfloat16
    members = max(2 * n_gy, 2 * n_gx // X_CHIPS)
    anywhere = pl.BlockSpec(memory_space=pl.ANY)
    vmem = pl.BlockSpec(memory_space=pltpu.VMEM)
    return pl.pallas_call(
        functools.partial(kernel, (n_gx, n_gy, total, element_tables()[2])),
        out_shape=(
            pltpu.VMEM((2, components, nodes, local_count), f32),
            pltpu.VMEM((2, kept + 2), f32),
        ),
        in_specs=[anywhere] * 10,
        out_specs=(vmem, vmem),
        scratch_shapes=[
            pltpu.VMEM((components, nodes, kept, local_count), f32),
            pltpu.VMEM(geometry.shape, f32),
            pltpu.VMEM(face_normals.shape, f32),
            pltpu.VMEM(face_scale.shape, f32),
            pltpu.VMEM(material.shape, f32),
            pltpu.VMEM(send_list.shape, jnp.int32),
            pltpu.VMEM(neighbour_source.shape, jnp.int32),
            pltpu.VMEM(node_rotation.shape, jnp.int32),
            pltpu.VMEM(boundary_flag.shape, jnp.int32),
            pltpu.VMEM((304, 256), f32),
            pltpu.VMEM((304, 256), bf16),
            pltpu.VMEM((components, nodes, local_count), f32),
            pltpu.VMEM((32, 768), f32),
            pltpu.VMEM((80, 768), f32),
            pltpu.VMEM((64, 512), f32),
            pltpu.VMEM((64, 512), f32),
            pltpu.VMEM((192, 512), f32),
            pltpu.VMEM((components, nodes, local_count), f32),
            pltpu.VMEM((64, 768), f32),
            pltpu.VMEM((4, 128), jnp.int32),
            pltpu.VMEM((4, 128), jnp.int32),
            pltpu.VMEM((24, 128), f32),
            pltpu.VMEM((1, 128), f32),
            pltpu.VMEM((1, 128), f32),
            pltpu.VMEM((24, 128), f32),
            pltpu.VMEM((components, 8 * nodes, local_count), f32),
            pltpu.VMEM((components, nodes, local_count), f32),
            pltpu.VMEM((2, 8, 32, 128), f32),
            pltpu.VMEM((2, 8, 32, 128), f32),
            pltpu.VMEM((2, members, 8, 128), f32),
            pltpu.VMEM((2, 2, members, 1, 128), f32),
            pltpu.SemaphoreType.DMA((12,)),
            pltpu.SemaphoreType.DMA((2,)),
            pltpu.SemaphoreType.DMA((2,)),
            pltpu.SemaphoreType.DMA((3, 3)),
            pltpu.SemaphoreType.DMA((3, 3)),
        ],
        compiler_params=pltpu.CompilerParams(
            collective_id=0, has_side_effects=True, vmem_limit_bytes=32 * 1024 * 1024
        ),
    )(
        *[
            pltpu.with_memory_space_constraint(operand, pltpu.HBM)
            for operand in (
                jnp.transpose(basis, (1, 2, 0, 3)),
                geometry,
                face_normals,
                face_scale,
                material,
                send_list,
                neighbour_source,
                node_rotation,
                boundary_flag,
                left_operands(),
            )
        ]
    )


def solution(mesh):
    placed = (
        P(None, None, None, ("gx", "gy")),
        P(None, ("gx", "gy")),
        P(None, None, ("gx", "gy")),
        P(None, ("gx", "gy")),
        P(None, ("gx", "gy")),
        P("gx", "gy", None),
        P(None, ("gx", "gy")),
        P(None, ("gx", "gy")),
        P(None, ("gx", "gy")),
    )
    return jax.shard_map(
        functools.partial(body, mesh.shape["gx"], mesh.shape["gy"]),
        mesh=mesh,
        in_specs=placed,
        out_specs=(P(None, None, None, ("gx", "gy")), P()),
        check_vma=False,
    )
```

```python
import functools
import math

import jax
import jax.numpy as jnp
import numpy as np
from jax import lax
from jax.experimental import pallas as pl
from jax.experimental.pallas import tpu as pltpu
from jax.sharding import PartitionSpec as P

MESH = pl.DeviceIdType.MESH
X_CHIPS = 4
CORES = 2
OPERANDS = (0, 80, 112)
DIRECTIONS = (0, 1, 2, 3, 5, 6, 7, 8)


def invert(matrix):
    dimension = len(matrix)
    augmented = []
    for row_index in range(dimension):
        augmented.append(
            [float(matrix[row_index][column]) for column in range(dimension)]
            + [1.0 if column == row_index else 0.0 for column in range(dimension)]
        )
    for column in range(dimension):
        pivot_row = column
        for row_index in range(column + 1, dimension):
            if abs(augmented[row_index][column]) > abs(augmented[pivot_row][column]):
                pivot_row = row_index
        augmented[column], augmented[pivot_row] = (augmented[pivot_row], augmented[column])
        leading = augmented[column][column]
        augmented[column] = [value / leading for value in augmented[column]]
        for row_index in range(dimension):
            if row_index != column:
                factor = augmented[row_index][column]
                augmented[row_index] = [
                    left - factor * right
                    for left, right in zip(augmented[row_index], augmented[column])
                ]
    return np.array([entries[dimension:] for entries in augmented])


def locate(face, first, second):
    if face == 0:
        return (first, second, 0)
    if face == 1:
        return (first, 0, second)
    if face == 2:
        return (3 - first - second, first, second)
    return (0, first, second)


def element_tables():
    nodes = [(i, j, k) for k in range(4) for j in range(4) for i in range(4) if i + j + k <= 3]
    points = np.array(nodes) / 3.0
    vander = np.zeros((20, 20))
    slopes = np.zeros((3, 20, 20))
    for row in range(20):
        for column in range(20):
            powers = np.array(nodes[column])
            vander[row, column] = np.prod(points[row] ** powers)
            for axis in range(3):
                if powers[axis] > 0:
                    lowered = powers.copy()
                    lowered[axis] -= 1
                    slopes[axis, row, column] = powers[axis] * np.prod(points[row] ** lowered)
    inverse = invert(vander)
    derivs = np.stack([slopes[axis] @ inverse for axis in range(3)])
    moments = np.zeros((20, 20))
    for row in range(20):
        for column in range(20):
            left = nodes[row]
            right = nodes[column]
            sums = [left[0] + right[0], left[1] + right[1], left[2] + right[2]]
            moments[row, column] = (
                math.factorial(sums[0])
                * math.factorial(sums[1])
                * math.factorial(sums[2])
                / math.factorial(sum(sums) + 3)
            )
    mass = inverse.T @ moments @ inverse
    lattice = [(first, second) for second in range(4) for first in range(4) if first + second <= 3]
    face_nodes = np.array(
        [[nodes.index(locate(face, pair[0], pair[1])) for face in range(4)] for pair in lattice]
    )
    plane = np.array(
        [
            [(pair[0] / 3.0) ** expo[0] * (pair[1] / 3.0) ** expo[1] for expo in lattice]
            for pair in lattice
        ]
    )
    plane_inverse = invert(plane)
    plane_moments = np.zeros((10, 10))
    for row in range(10):
        for column in range(10):
            first = lattice[row][0] + lattice[column][0]
            second = lattice[row][1] + lattice[column][1]
            plane_moments[row, column] = (
                math.factorial(first) * math.factorial(second) / math.factorial(first + second + 2)
            )
    face_mass = plane_inverse.T @ plane_moments @ plane_inverse
    edges = np.zeros((20, 40))
    for face in range(4):
        for row in range(10):
            for column in range(10):
                edges[face_nodes[row, face], column * 4 + face] += face_mass[row, column]
    lift = invert(mass) @ edges
    turned = np.array([lattice.index((pair[1], 3 - pair[0] - pair[1])) for pair in lattice])
    rotations = np.stack([np.arange(10), turned, turned[turned]])
    return (derivs, lift, face_nodes, rotations)


def bf16_parts(values):
    values = np.asarray(values, np.float32)
    high = values.astype(jnp.bfloat16)
    rest = values - high.astype(np.float32)
    middle = rest.astype(jnp.bfloat16)
    low = (rest - middle.astype(np.float32)).astype(jnp.bfloat16)
    return high, middle, low


def packed_row(component, node):
    return 8 * component + node if node < 8 else 48 + 2 * component + node - 8


def left_operands():
    derivs, lift, face_nodes, rotations = element_tables()
    stack = np.zeros((3, 80, 32), np.float32)
    for index, part in enumerate(bf16_parts(derivs)):
        for axis in range(3):
            stack[index, 24 * axis : 24 * axis + 20, :20] = part[axis].astype(np.float32)
    high, middle, low = stack
    volume = np.concatenate([high, high, high, middle, low, middle], axis=1)
    blocks = np.zeros((3, 32, 64), np.float32)
    for index, part in enumerate(bf16_parts(lift)):
        for face in range(4):
            for node in range(10):
                blocks[index, :20, 16 * face + node] = part[:, node * 4 + face].astype(np.float32)
    raise_up = np.concatenate([blocks[0], blocks[1], blocks[0], blocks[0]], axis=1)
    spread = np.zeros((192, 64), np.float32)
    for turn in range(3):
        for component in range(6):
            for node in range(10):
                spread[
                    64 * turn + packed_row(component, node),
                    packed_row(component, rotations[turn][node]),
                ] = 1.0
    turned = np.concatenate([spread, spread, spread], axis=1)
    packed = np.zeros((304, 256), np.float32)
    for place, matrix in zip(OPERANDS, (volume, raise_up, turned)):
        packed[place : place + matrix.shape[0], : matrix.shape[1]] = matrix
    return jnp.asarray(packed)


def split(values):
    high = values.astype(jnp.bfloat16)
    rest = values - high.astype(jnp.float32)
    middle = rest.astype(jnp.bfloat16)
    low = (rest - middle.astype(jnp.float32)).astype(jnp.bfloat16)
    return high, middle, low


def iota(shape, axis):
    return lax.broadcasted_iota(jnp.int32, shape, axis)


def dot(left, right):
    return jnp.dot(left, right, preferred_element_type=jnp.float32)


def kernel(
    sizes,
    basis_hbm,
    geometry_hbm,
    normals_hbm,
    scale_hbm,
    material_hbm,
    send_list_hbm,
    source_hbm,
    turns_hbm,
    flags_hbm,
    constants_hbm,
    fresh,
    hessenberg,
    stored,
    geometry,
    normals,
    scale,
    material,
    send_list,
    source,
    turns,
    flags,
    constants_wide,
    constants,
    vector,
    field,
    around,
    table,
    others,
    rotated,
    image,
    flux,
    index_out,
    index_in,
    gram,
    held_bound,
    side_row,
    work,
    spread,
    taken,
    outgoing,
    arrived,
    sums_a,
    sums_b,
    load_sem,
    halo_send,
    halo_recv,
    sum_send,
    sum_recv,
):
    n_gx, n_gy, total, face_nodes = sizes
    kept = basis_hbm.shape[2]
    gx = lax.axis_index("gx")
    gy = lax.axis_index("gy")
    last = kept // 8 * 8
    block = (slice(None), slice(None), pl.ds(last, kept - last))
    rest = (slice(None), slice(None), pl.ds(0, last))
    loads = []
    for source_ref, target_ref in (
        (send_list_hbm, send_list),
        (basis_hbm.at[block], stored.at[block]),
        (constants_hbm, constants_wide),
        (basis_hbm.at[rest], stored.at[rest]),
        (source_hbm, source),
        (turns_hbm, turns),
        (flags_hbm, flags),
        (geometry_hbm, geometry),
        (normals_hbm, normals),
        (scale_hbm, scale),
        (material_hbm, material),
    ):
        loads.append(pltpu.make_async_copy(source_ref, target_ref, load_sem.at[len(loads)]))
    for load in loads[:2]:
        load.start()

    def turned_on(place, step, size):
        place = place + step
        return jnp.where(place >= size, place - size, place)

    partners = []
    for direction in DIRECTIONS:
        partners.append(
            (
                turned_on(gx, (direction // 3 - 1) % n_gx, n_gx),
                turned_on(gy, (direction % 3 - 1) % n_gy, n_gy),
            )
        )

    across = lax.rem(gx, X_CHIPS)
    up = lax.div(gx, X_CHIPS)
    core = lax.rem(gy, CORES)
    along = lax.div(gy, CORES)
    odd = lax.rem(across, 2)
    rows_up = n_gx // X_CHIPS
    layers = n_gy // CORES
    beside_x = gx + 1 - 2 * odd
    facing_x = gx + X_CHIPS - 1 - 2 * across
    hops_first = []
    for step in range(layers):
        for other in range(2):
            for flip in range(CORES):
                hops_first.append((min(step, layers - step) + other + flip / 2, step, other, flip))
    hops_second = []
    for step in range(rows_up):
        for other in range(2):
            hops_second.append((min(step, rows_up - step) + other, step, other))
    first_peers = [
        (
            hops,
            (
                beside_x if other else gx,
                turned_on(gy, CORES * step, n_gy) - core + turned_on(core, flip, CORES),
            ),
        )
        for hops, step, other, flip in sorted(hops_first, reverse=True)
        if hops > 0
    ]
    second_peers = [
        (hops, (turned_on(facing_x if other else gx, X_CHIPS * step, n_gx), gy))
        for hops, step, other in sorted(hops_second, reverse=True)
        if hops > 0
    ]
    first_group = (
        2 * CORES * layers,
        (2 * along + odd) * CORES + core,
        [peer for _, peer in first_peers],
    )
    second_group = (
        2 * rows_up,
        lax.div(across, 2) * rows_up + up,
        [peer for _, peer in second_peers],
    )

    def group_of(which, stage):
        is_gram = isinstance(which, int) and which == 2
        return second_group if (stage == 1) != is_gram else first_group

    barrier = pltpu.get_barrier_semaphore()
    greeted = sorted(first_peers + second_peers, key=lambda entry: -entry[0])
    greeted = [peer for _, peer in greeted] + partners
    for peer in greeted:
        pl.semaphore_signal(barrier, inc=1, device_id=peer, device_id_type=MESH)

    loads[0].wait()
    for tile in range(4):
        first, second = DIRECTIONS[2 * tile], DIRECTIONS[2 * tile + 1]
        index_out[pl.ds(tile, 1), :] = jnp.concatenate(
            [
                send_list[first // 3, pl.ds(first % 3, 1), :],
                send_list[second // 3, pl.ds(second % 3, 1), :],
            ],
            axis=1,
        )

    def pick(found, sources, index, first):
        lane = jnp.broadcast_to(jnp.bitwise_and(index, 127), (64, 128))
        tile = jnp.broadcast_to(jnp.right_shift(index, 7), (64, 128))
        for place, values in enumerate(sources):
            picked = jnp.take_along_axis(values, lane, axis=1, mode="promise_in_bounds")
            found = picked if found is None else jnp.where(tile == first + place, picked, found)
        return found

    half = iota((32, 128), 1) < 64

    def prepare(turn, greeting):
        for component in range(6):
            for face in range(4):
                for node in range(10):
                    row = pl.ds(packed_row(component, node), 1)
                    table[row, pl.ds(128 * face, 128)] = vector[
                        component, pl.ds(int(face_nodes[node, face]), 1), :
                    ]
        sources = [table[:, pl.ds(128 * tile, 128)] for tile in range(4)]
        for tile in (0, 3, 1, 2):
            sent = pick(None, sources, index_out[pl.ds(tile, 1), :], 0)
            top = sent[0:32]
            bottom = sent[32:64]
            outgoing[turn, 2 * tile] = jnp.where(half, top, pltpu.roll(bottom, 64, 1))
            outgoing[turn, 2 * tile + 1] = jnp.where(half, pltpu.roll(top, 64, 1), bottom)
        greeting()
        for index in (0, 1, 6, 7, 2, 5, 3, 4):
            pltpu.make_async_remote_copy(
                src_ref=outgoing.at[turn, index],
                dst_ref=arrived.at[turn, 7 - index],
                send_sem=halo_send.at[turn],
                recv_sem=halo_recv.at[turn],
                device_id=partners[index],
                device_id_type=MESH,
            ).start()

    def apply(turn, ready, beside):
        ready()
        for component in range(6):
            field[pl.ds(0, 20), pl.ds(128 * component, 128)] = vector[component]
        high, middle, low = split(field[...])
        around[...] = dot(
            constants[pl.ds(0, 80), pl.ds(0, 192)],
            jnp.concatenate([high, middle, low, high, high, middle], axis=0)
        )

        def gradient(axis, component):
            column = pl.ds(128 * component, 128)
            return (
                around[pl.ds(0, 20), column] * geometry[pl.ds(axis, 1), :]
                + around[pl.ds(24, 20), column] * geometry[pl.ds(3 + axis, 1), :]
                + around[pl.ds(48, 20), column] * geometry[pl.ds(6 + axis, 1), :]
            )

        for component in range(3):
            after, before = (component + 1) % 3, (component + 2) % 3
            curl_e = gradient(after, before) - gradient(before, after)
            curl_h = gradient(after, 3 + before) - gradient(before, 3 + after)
            image[component] = (
                material[pl.ds(0, 1), :] * curl_h - material[pl.ds(2, 1), :] * vector[component]
            )
            image[3 + component] = -material[pl.ds(1, 1), :] * curl_e
        beside()
        sources = [table[:, pl.ds(128 * tile, 128)] for tile in range(4)]
        for face in range(4):
            lane = pl.ds(128 * face, 128)
            others[:, lane] = pick(None, sources, index_in[pl.ds(face, 1), :], 0)
        pltpu.make_async_copy(arrived.at[turn], arrived.at[turn], halo_recv.at[turn]).wait()
        sources = []
        for tile in range(4):
            even = arrived[turn, 2 * tile]
            odd = arrived[turn, 2 * tile + 1]
            sources.append(
                jnp.concatenate(
                    [
                        jnp.where(half, even, pltpu.roll(odd, 64, 1)),
                        jnp.where(half, pltpu.roll(even, 64, 1), odd),
                    ],
                    axis=0,
                )
            )
        found = jnp.concatenate(
            [
                pick(
                    others[:, pl.ds(128 * face, 128)], sources, index_in[pl.ds(face, 1), :], 4
                )
                for face in range(4)
            ],
            axis=1,
        )
        rotated[...] = dot(
            constants[pl.ds(112, 192), pl.ds(0, 192)], jnp.concatenate(split(found), axis=0)
        )
        for face in range(4):
            lane = pl.ds(128 * face, 128)
            spin = turns[pl.ds(face, 1), :]
            wall = flags[pl.ds(face, 1), :] == 1
            weight = 0.5 * scale[pl.ds(face, 1), :]
            n_x = normals[0, pl.ds(face, 1), :]
            n_y = normals[1, pl.ds(face, 1), :]
            n_z = normals[2, pl.ds(face, 1), :]
            for first_node, count in ((0, 8), (8, 2)):
                jumps = []
                for component in range(6):
                    row = packed_row(component, first_node)
                    here = table[pl.ds(row, count), lane]
                    other = jnp.where(
                        spin == 0,
                        rotated[pl.ds(row, count), lane],
                        jnp.where(
                            spin == 1,
                            rotated[pl.ds(64 + row, count), lane],
                            rotated[pl.ds(128 + row, count), lane],
                        ),
                    )
                    other = jnp.where(wall, -here if component < 3 else here, other)
                    jumps.append(other - here)
                e_x, e_y, e_z, h_x, h_y, h_z = jumps
                along_e = n_x * e_x + n_y * e_y + n_z * e_z
                along_h = n_x * h_x + n_y * h_y + n_z * h_z
                terms = [
                    n_y * h_z - n_z * h_y + e_x - along_e * n_x,
                    n_z * h_x - n_x * h_z + e_y - along_e * n_y,
                    n_x * h_y - n_y * h_x + e_z - along_e * n_z,
                    n_z * e_y - n_y * e_z + h_x - along_h * n_x,
                    n_x * e_z - n_z * e_x + h_y - along_h * n_y,
                    n_y * e_x - n_x * e_y + h_z - along_h * n_z,
                ]
                for component in range(6):
                    place = pl.ds(16 * face + first_node, count)
                    flux[place, pl.ds(128 * component, 128)] = terms[component] * weight
        high, middle, low = split(flux[...])
        lifted = dot(constants[pl.ds(80, 32), :], jnp.concatenate([high, high, middle, low], axis=0))
        for component in range(6):
            raised = lifted[0:20, 128 * component : 128 * component + 128]
            image[component] += material[pl.ds(component // 3, 1), :] * raised

    sub8 = iota((8, 128), 0)
    sub24 = iota((24, 128), 0)
    lane24 = iota((24, 128), 1)
    lane1 = iota((1, 128), 1)
    eye = sub24 == lane24

    def inner(vector_ref, *pairs):
        def some(component, held):
            held = list(held)
            for node in range(20):
                held[node % 3] += (
                    stored[component, node] * vector_ref[component, pl.ds(node, 1), :]
                )
            return tuple(held)

        zero = jnp.zeros((kept, 128), jnp.float32)
        for place, (left, right) in enumerate(pairs):
            partial = jnp.sum(left[...] * right[...], axis=0)
            work[pl.ds(kept + place, 1), :] = jnp.sum(partial, axis=0, keepdims=True)
        one, two, three = lax.fori_loop(0, 6, some, (zero, zero, zero))
        work[pl.ds(0, kept), :] = one + two + three
        return to_row(jnp.sum(work[...], axis=1, keepdims=True))

    def to_row(column):
        return jnp.sum(jnp.where(eye, column, 0.0), axis=0, keepdims=True)

    def to_column(row):
        return jnp.sum(jnp.where(eye, row, 0.0), axis=1, keepdims=True)

    def fill_gram():
        def upper(node, held):
            held = list(held)
            for component in range(6):
                tile = stored[component, node]
                for index in range(8):
                    held[index] += tile * stored[component, node, pl.ds(index, 1), :]
            return tuple(held)

        def lower(node, held):
            held = list(held)
            for component in range(6):
                tile = stored[component, node, pl.ds(8, kept - 8), :]
                for index in range(8, 16):
                    held[index - 8] += tile * stored[component, node, pl.ds(index, 1), :]
                tile = tile[8:]
                for index in range(16, kept):
                    held[index - 8] += tile * stored[component, node, pl.ds(index, 1), :]
            return tuple(held)

        def zeros(count, number):
            return (jnp.zeros((count, 128), jnp.float32),) * number

        found = list(lax.fori_loop(0, 20, upper, zeros(kept, 8)))
        found += lax.fori_loop(
            0, 20, lower, zeros(kept - 8, 8) + zeros(kept - 16, kept - 16)
        )
        gram[...] = jnp.zeros((24, 128), jnp.float32)
        for first in (0, 8, 16):
            count = kept - first
            sub = iota((count, 128), 0)
            lane = iota((count, 128), 1)
            held = jnp.zeros((count, 128), jnp.float32)
            for index in range(first, min(first + 8, kept)):
                column = jnp.sum(found[index], axis=1, keepdims=True)
                held = jnp.where(lane == index, column, held)
                row = jnp.sum(jnp.where(sub + first == lane, column, 0.0), axis=0, keepdims=True)
                held = jnp.where((sub == index - first) & (lane >= first), row, held)
            if first == 0:
                gram[pl.ds(0, kept), :] = held
            else:
                old = gram[pl.ds(first, count), :]
                gram[pl.ds(first, count), :] = jnp.where(lane >= first, held, old)

    def begin(value, buffer, which, stage):
        size, mine, peers = group_of(which, stage)
        buffer[stage, mine] = value
        for peer in peers:
            pltpu.make_async_remote_copy(
                src_ref=buffer.at[stage, mine],
                dst_ref=buffer.at[stage, mine],
                send_sem=sum_send.at[which, stage],
                recv_sem=sum_recv.at[which, stage],
                device_id=peer,
                device_id_type=MESH,
            ).start()

    def finish(buffer, which, stage):
        size, mine, peers = group_of(which, stage)
        if size > 1:
            others = buffer.at[stage, pl.ds(0, size - 1)]
            pltpu.make_async_copy(others, others, sum_recv.at[which, stage]).wait()
        values = [buffer[stage, member] for member in range(size)]
        while len(values) > 1:
            values = [sum(values[at : at + 2]) for at in range(0, len(values), 2)]
        return values[0]

    def project(column):
        weights = jnp.broadcast_to(column[0:kept], (kept, 128))

        def one(component, carry):
            for node in range(20):
                product = stored[component, node] * weights
                short = jnp.concatenate(
                    [product[16:kept], jnp.zeros((24 - kept, 128), jnp.float32)], axis=0
                )
                spread[component, pl.ds(8 * node, 8), :] = product[0:8] + product[8:16] + short
            return carry

        lax.fori_loop(0, 6, one, 0)
        for component in range(6):
            parts_of = [spread[component, pl.ds(at, 20, stride=8), :] for at in range(8)]
            while len(parts_of) > 1:
                parts_of = [sum(parts_of[at : at + 2]) for at in range(0, len(parts_of), 2)]
            taken[component] = parts_of[0]

    field[pl.ds(16, 16), :] = jnp.zeros((16, 768), jnp.float32)
    table[pl.ds(56, 8), :] = jnp.zeros((8, 512), jnp.float32)
    flux[...] = jnp.zeros((64, 768), jnp.float32)
    held_bound[...] = jnp.ones((1, 128), jnp.float32)
    side_row[...] = jnp.zeros((1, 128), jnp.float32)
    work[...] = jnp.zeros((24, 128), jnp.float32)
    hessenberg[...] = jnp.zeros((2, kept + 2), jnp.float32)
    loads[1].wait()
    for load in loads[2:]:
        load.start()
    for component in range(6):
        vector[component] = stored[component, :, kept - 1, :]

    def step(turn, carry):
        first_step = turn == 0
        sums = sums_b.at[turn]

        def ready():
            @pl.when(first_step)
            def _():
                for load in loads[2:]:
                    load.wait()
                constants[...] = constants_wide[...].astype(jnp.bfloat16)

        def beside():
            @pl.when(first_step)
            def _():
                for face in range(4):
                    named = source[pl.ds(face, 1), :]
                    index_in[pl.ds(face, 1), :] = jnp.where(
                        named >= 512 + 4 * 64, named - 64, named
                    )
                fill_gram()
                packed = (
                    gram[pl.ds(0, 8), :]
                    + pltpu.roll(gram[pl.ds(8, 8), :], 32, 1)
                    + pltpu.roll(gram[pl.ds(16, 8), :], 64, 1)
                )
                begin(packed, sums_a, 2, 0)

            @pl.when(jnp.logical_not(first_step))
            def _():
                side_row[...] = pltpu.roll(inner(vector, (vector, vector)), 32, 1)

        def greeting():
            @pl.when(first_step)
            def _():
                pl.semaphore_wait(barrier, len(greeted))

        prepare(turn, greeting)
        apply(turn, ready, beside)

        row = inner(image, (vector, image), (image, image))
        begin(row + side_row[...], sums, turn, 0)

        @pl.when(first_step)
        def _():
            begin(finish(sums_a, 2, 0), sums_a, 2, 1)

        begin(finish(sums, turn, 0), sums, turn, 1)

        @pl.when(first_step)
        def _():
            packed = finish(sums_a, 2, 1) * (1.0 / total)
            products = jnp.concatenate(
                [packed, pltpu.roll(packed, 96, 1), pltpu.roll(packed, 64, 1)], axis=0
            )
            gram[...] = jnp.where(lane24 < 24, products, 0.0)

        products = gram[...]
        own = jnp.sum(jnp.where(eye, products, 0.0), axis=1, keepdims=True)
        message = finish(sums, turn, 1) * (1.0 / total)

        bound = held_bound[...][:, 0:1]
        row = jnp.where(lane1 < kept + turn, message, 0.0)
        side = jnp.where(lane1 < kept + 1, pltpu.roll(message, 96, 1), 0.0)
        square = jnp.sum(jnp.where(lane1 == kept + 1, message, 0.0), keepdims=True)
        length = jnp.sum(jnp.where(lane1 == kept, side, 0.0), keepdims=True)
        height = jnp.sqrt(length * (bound * bound) + 1e-06)
        grow = jnp.where(first_step, 1.0, bound / height)
        side = side * jnp.where(lane1 == kept, grow * grow, grow)
        row = row * jnp.where(lane1 == kept, grow * grow, grow)
        extended = kept + turn - 1
        products = jnp.where((lane24 == kept) & (extended == kept), to_column(side), products)
        products = jnp.where((sub24 == kept) & (extended == kept), side, products)
        column = jnp.sum((jnp.where(eye, 2.0, 0.0) - products) * row, axis=1, keepdims=True)
        column_row = to_row(column)

        @pl.when(jnp.logical_not(first_step))
        def _():
            before = hessenberg[pl.ds(0, 1), :]
            hessenberg[pl.ds(0, 1), :] = jnp.where(
                lane1[:, 0:24] == kept, height, before
            )

        square = square * (grow * grow)
        length = square + jnp.sum(
            column * (products * column_row - jnp.where(eye, 2.0, 0.0) * row), keepdims=True
        )
        height = jnp.sqrt(jnp.maximum(length, 0.0) + 1e-06)
        bound = jnp.sum(jnp.abs(column) * jnp.sqrt(own), keepdims=True) + jnp.sqrt(square) + 1e-3
        held_bound[...] = jnp.broadcast_to(bound, (1, 128))
        shrink = 1.0 / jnp.where(first_step, bound, height)
        project(column)
        on_own = column[kept : kept + 1] * grow
        for component in range(6):
            current = vector[component]
            new = (image[component] * grow - current * on_own - taken[component]) * shrink
            fresh[0, component] = current * grow
            fresh[1, component] = new
            vector[component] = new
        hessenberg[pl.ds(turn, 1), :] = jnp.where(
            lane1 == kept + 1, jnp.where(first_step, 0.0, height), column_row
        )[:, 0:24]
        return carry

    lax.fori_loop(0, 2, step, 0)
    for turn in range(2):
        pltpu.make_async_copy(outgoing.at[turn], outgoing.at[turn], halo_send.at[turn]).wait()
    for which in range(3):
        for stage in range(2):
            size = group_of(which, stage)[0]
            if size > 1:
                buffer = sums_a if which == 2 else sums_b.at[which]
                others = buffer.at[stage, pl.ds(0, size - 1)]
                pltpu.make_async_copy(others, others, sum_send.at[which, stage]).wait()


def body(
    n_gx,
    n_gy,
    basis,
    geometry,
    face_normals,
    face_scale,
    material,
    send_list,
    neighbour_source,
    node_rotation,
    boundary_flag,
):
    kept, components, nodes, local_count = basis.shape
    total = float(components * nodes * local_count * n_gx * n_gy)
    f32, bf16 = jnp.float32, jnp.bfloat16
    members = max(2 * n_gy, 2 * n_gx // X_CHIPS)
    anywhere = pl.BlockSpec(memory_space=pl.ANY)
    vmem = pl.BlockSpec(memory_space=pltpu.VMEM)
    return pl.pallas_call(
        functools.partial(kernel, (n_gx, n_gy, total, element_tables()[2])),
        out_shape=(
            pltpu.VMEM((2, components, nodes, local_count), f32),
            pltpu.VMEM((2, kept + 2), f32),
        ),
        in_specs=[anywhere] * 10,
        out_specs=(vmem, vmem),
        scratch_shapes=[
            pltpu.VMEM((components, nodes, kept, local_count), f32),
            pltpu.VMEM(geometry.shape, f32),
            pltpu.VMEM(face_normals.shape, f32),
            pltpu.VMEM(face_scale.shape, f32),
            pltpu.VMEM(material.shape, f32),
            pltpu.VMEM(send_list.shape, jnp.int32),
            pltpu.VMEM(neighbour_source.shape, jnp.int32),
            pltpu.VMEM(node_rotation.shape, jnp.int32),
            pltpu.VMEM(boundary_flag.shape, jnp.int32),
            pltpu.VMEM((304, 256), f32),
            pltpu.VMEM((304, 256), bf16),
            pltpu.VMEM((components, nodes, local_count), f32),
            pltpu.VMEM((32, 768), f32),
            pltpu.VMEM((80, 768), f32),
            pltpu.VMEM((64, 512), f32),
            pltpu.VMEM((64, 512), f32),
            pltpu.VMEM((192, 512), f32),
            pltpu.VMEM((components, nodes, local_count), f32),
            pltpu.VMEM((64, 768), f32),
            pltpu.VMEM((4, 128), jnp.int32),
            pltpu.VMEM((4, 128), jnp.int32),
            pltpu.VMEM((24, 128), f32),
            pltpu.VMEM((1, 128), f32),
            pltpu.VMEM((1, 128), f32),
            pltpu.VMEM((24, 128), f32),
            pltpu.VMEM((components, 8 * nodes, local_count), f32),
            pltpu.VMEM((components, nodes, local_count), f32),
            pltpu.VMEM((2, 8, 32, 128), f32),
            pltpu.VMEM((2, 8, 32, 128), f32),
            pltpu.VMEM((2, members, 8, 128), f32),
            pltpu.VMEM((2, 2, members, 1, 128), f32),
            pltpu.SemaphoreType.DMA((12,)),
            pltpu.SemaphoreType.DMA((2,)),
            pltpu.SemaphoreType.DMA((2,)),
            pltpu.SemaphoreType.DMA((3, 3)),
            pltpu.SemaphoreType.DMA((3, 3)),
        ],
        compiler_params=pltpu.CompilerParams(
            collective_id=0, has_side_effects=True, vmem_limit_bytes=32 * 1024 * 1024
        ),
    )(
        *[
            pltpu.with_memory_space_constraint(operand, pltpu.HBM)
            for operand in (
                jnp.transpose(basis, (1, 2, 0, 3)),
                geometry,
                face_normals,
                face_scale,
                material,
                send_list,
                neighbour_source,
                node_rotation,
                boundary_flag,
                left_operands(),
            )
        ]
    )


def solution(mesh):
    placed = (
        P(None, None, None, ("gx", "gy")),
        P(None, ("gx", "gy")),
        P(None, None, ("gx", "gy")),
        P(None, ("gx", "gy")),
        P(None, ("gx", "gy")),
        P("gx", "gy", None),
        P(None, ("gx", "gy")),
        P(None, ("gx", "gy")),
        P(None, ("gx", "gy")),
    )
    return jax.shard_map(
        functools.partial(body, mesh.shape["gx"], mesh.shape["gy"]),
        mesh=mesh,
        in_specs=placed,
        out_specs=(P(None, None, None, ("gx", "gy")), P()),
        check_vma=False,
    )
```
